32 devices in a mesh: dp: 8 (over y, x, core), shard: 4 (over z).
Axes of the slice: x: 2, y: 2, z: 4, core: 2. Of those that a mesh axis runs over, the one named last changes fastest.
Arguments:
- tokens: bfloat16 [8192, 1024], P(('dp', 'shard')), may hold values from -6 to 6
- cotangent: bfloat16 [8192, 1024], P(('dp', 'shard')), may hold values from -6 to 6
- lengths: int32 [8], P('dp'), may hold values from 1 to 1024, 5120 in all
- norm1_gain: bfloat16 [1024], P(('dp', 'shard')), may hold values from 0.5 to 1.5
- w_query: bfloat16 [1024, 1024], P(('dp', 'shard')), may hold values from -0.1875 to 0.1875
- w_key: bfloat16 [1024, 1024], P(('dp', 'shard')), may hold values from -0.1875 to 0.1875
- w_value: bfloat16 [1024, 1024], P(('dp', 'shard')), may hold values from -0.1875 to 0.1875
- w_gate_low: bfloat16 [1024, 16], P(('dp', 'shard')), may hold values from -0.1875 to 0.1875
- w_gate_up: bfloat16 [256, 16], P(('dp', 'shard')), may hold values from -1.5 to 1.5
- gate_bias: bfloat16 [256], P(('dp', 'shard')), may hold values from -2 to 6
- head_gain: bfloat16 [256], P(('dp', 'shard')), may hold values from 0.5 to 1.5
- w_swish: bfloat16 [1024, 1024], P(('dp', 'shard')), may hold values from -0.1875 to 0.1875
- w_out: bfloat16 [1024, 1024], P(('dp', 'shard')), may hold values from -0.375 to 0.375
- norm2_gain: bfloat16 [1024], P(('dp', 'shard')), may hold values from 0.5 to 1.5
- w_ffn_gate: bfloat16 [1024, 2816], P(('dp', 'shard')), may hold values from -0.1875 to 0.1875
- w_ffn_up: bfloat16 [1024, 2816], P(('dp', 'shard')), may hold values from -0.1875 to 0.1875
- w_ffn_down: bfloat16 [2816, 1024], P(('dp', 'shard')), may hold values from -0.15625 to 0.15625
Outputs:
- output: bfloat16 [8192, 1024], P(('dp', 'shard'))
- d_tokens: float32 [8192, 1024], P(('dp', 'shard'))
- d_norm1_gain: float32 [1024], P(('dp', 'shard'))
- d_query: float32 [1024, 1024], P(('dp', 'shard'))
- d_key: float32 [1024, 1024], P(('dp', 'shard'))
- d_value: float32 [1024, 1024], P(('dp', 'shard'))
- d_gate_low: float32 [1024, 16], P(('dp', 'shard'))
- d_gate_up: float32 [256, 16], P(('dp', 'shard'))
- d_gate_bias: float32 [256], P(('dp', 'shard'))
- d_head_gain: float32 [256], P(('dp', 'shard'))
- d_swish: float32 [1024, 1024], P(('dp', 'shard'))
- d_out: float32 [1024, 1024], P(('dp', 'shard'))
- d_norm2_gain: float32 [1024], P(('dp', 'shard'))
- d_ffn_gate: float32 [1024, 2816], P(('dp', 'shard'))
- d_ffn_up: float32 [1024, 2816], P(('dp', 'shard'))
- d_ffn_down: float32 [2816, 1024], P(('dp', 'shard'))
The draws below stay inside these ranges and needn't reach their ends.
Inputs may be any that keep to these rules, and one draw needn't show every extreme that they name: The lengths add up to 5120.
All inputs are finite; a program needn't handle non-finite values. No bound on the sum of `lengths` on one device may be relied on, other than what follows from the above.
Results may differ from the reference program's by a relative error of at most 0.022.
Values may be sent and summed in bfloat16 or wider, within the bound.
A program may use at most 112 MiB of HBM per device.

```python
import math
import jax
import jax.numpy as jnp
import numpy as np
from jax import lax

D = 1024
HEADS = 4
HEAD = 256
SLOTS = 64
FF = 2816
RANK = 16
GROUP = 64
LENGTH = 1024
SEQS = 8
TOKENS = 8192
GATES = 256


def level_of(stream_key, shape, cuts, low, largest):
    level, own = 1.0, jax.random.fold_in(stream_key, 6)
    for dim, blocks in cuts:
        steps = jnp.exp(jax.random.uniform(jax.random.fold_in(own, dim), (blocks,), jnp.float32, low / len(cuts), largest / len(cuts)))
        level = level * jnp.repeat(steps, shape[dim] // blocks).reshape([-1 if axis == dim else 1 for axis in range(len(shape))])
    return level


def length_profile(count, total, limit, skew):
    loads = [(1 << 20) // math.isqrt(rank ** skew) + 1 for rank in range(2, count + 1)]
    surplus, counts = total - limit - (count - 1), [1] * (count - 1)
    while surplus > 0:
        movable = [i for i in range(count - 1) if counts[i] < limit]
        pool, budget = sum([loads[i] for i in movable]), surplus
        for i in movable:
            addition = min(limit - counts[i], max(1, budget * loads[i] // pool), surplus)
            counts[i] = counts[i] + addition
            surplus = surplus - addition
    return np.array([limit] + counts)


def uneven(stream_key, count, total, limit, lean):
    if count == 2:
        one = jax.random.randint(stream_key, (), max(1, total - limit), min(limit, total - 1) + 1)
        return jnp.stack([one, total - one])
    tallies = jnp.asarray(length_profile(count, total, limit, lean), jnp.int32)
    pairs = (count - 1) // 2
    donor, receiver = tallies[1:1 + 2 * pairs:2], tallies[2:2 + 2 * pairs:2]
    room = jnp.minimum(donor - 1, limit - receiver)
    moved = jax.random.randint(jax.random.fold_in(stream_key, 1), (pairs,), 0, 1 << 20) % (room + 1)
    tallies = tallies.at[1:1 + 2 * pairs:2].set(donor - moved).at[2:2 + 2 * pairs:2].set(receiver + moved)
    return tallies[jax.random.permutation(jax.random.fold_in(stream_key, 2), count)]


def noise(key, dims, scale, limit, cuts=(), held_as=jnp.bfloat16):
    values = scale * jax.random.normal(key, dims, jnp.float32)
    if cuts:
        values = values * level_of(key, dims, cuts, -0.22, 0.18)
    return jnp.clip(values, -limit, limit).astype(held_as)


def setup_inputs(seed: int = 0) -> dict:
    seeds = jax.random.split(jax.random.key(seed), 18)
    return {
        "tokens": noise(seeds[0], (TOKENS, D), 1.0, 6.0, ((0, 32),)),
        "cotangent": noise(seeds[1], (TOKENS, D), 1.0, 6.0, ((0, 32),)),
        "lengths": uneven(seeds[2], SEQS, TOKENS * 5 // 8, LENGTH, 2).astype(jnp.int32),
        "norm1_gain": jnp.clip(1.0 + 0.1 * jax.random.normal(seeds[3], (D,), jnp.float32), 0.5, 1.5).astype(jnp.bfloat16),
        "w_query": noise(seeds[4], (D, D), D ** -0.5, 0.1875, ((0, 32),)),
        "w_key": noise(seeds[5], (D, D), D ** -0.5, 0.1875, ((0, 32),)),
        "w_value": noise(seeds[6], (D, D), D ** -0.5, 0.1875, ((0, 32),)),
        "w_gate_low": noise(seeds[7], (D, RANK), D ** -0.5, 0.1875, ((0, 32),)),
        "w_gate_up": noise(seeds[8], (GATES, RANK), RANK ** -0.5, 1.5, ((0, 32),)),
        "gate_bias": jnp.clip(-2.0 + 8.0 * jax.random.uniform(seeds[9], (GATES,), jnp.float32) ** level_of(seeds[9], (GATES,), ((0, 32),), -0.2, 0.2), -2.0, 6.0).astype(jnp.bfloat16),
        "head_gain": jnp.clip(1.0 + 0.1 * jax.random.normal(seeds[10], (HEAD,), jnp.float32), 0.5, 1.5).astype(jnp.bfloat16),
        "w_swish": noise(seeds[11], (D, D), D ** -0.5, 0.1875, ((0, 32),)),
        "w_out": noise(seeds[12], (D, D), (D // 4) ** -0.5, 0.375, ((0, 32),)),
        "norm2_gain": jnp.clip(1.0 + 0.1 * jax.random.normal(seeds[13], (D,), jnp.float32), 0.5, 1.5).astype(jnp.bfloat16),
        "w_ffn_gate": noise(seeds[14], (D, FF), D ** -0.5, 0.1875, ((0, 32),)),
        "w_ffn_up": noise(seeds[15], (D, FF), D ** -0.5, 0.1875, ((0, 32),)),
        "w_ffn_down": noise(seeds[16], (FF, D), (FF // 2) ** -0.5, 0.15625, ((0, 32),)),
    }


norm_eps = 1e-06
gate_norm = 8.0
peak_score = lax.Precision.HIGHEST

@jax.custom_vjp
def low(v):
    return lax.optimization_barrier(v.astype(jnp.bfloat16)).astype(jnp.float32)

@jax.custom_vjp
def low_back(v):
    return v

def low_keep(v):
    return (low(v), None)

def low_pass(kept, grad):
    return (grad,)

def back_keep(v):
    return (v, None)

def back_low(kept, grad):
    return (low(grad),)
low.defvjp(low_keep, low_pass)
low_back.defvjp(back_keep, back_low)

def matmul(left, right):
    return jnp.dot(left, right, precision=peak_score)

def group_step(carry, block):
    slot_key_state, slot_value_state = carry
    query_rows, key_rows, value_rows, log_gate = block
    count = log_gate.shape[0]
    scale = 1.5 * query_rows.shape[-1] ** (-0.25)
    cumul = jnp.cumsum(log_gate, axis=0)
    causal = (jnp.arange(count)[:, None] >= jnp.arange(count)[None, :])[:, :, None, None]
    differ = cumul[:, None] - cumul[None, :]
    decay = jnp.where(causal, jnp.exp(jnp.where(causal, differ, 0.0)), 0.0)
    weight = decay * (1.0 - jnp.exp(log_gate))[None]
    leading_part = jnp.exp(cumul)
    inner = jnp.einsum('thd,jhd->htj', query_rows, key_rows, precision=peak_score)
    slot_scores = jnp.einsum('htj,tjhm->thm', inner, weight, precision=peak_score)
    slot_scores = slot_scores + leading_part * jnp.einsum('lrz,rbz->lrb', query_rows, slot_key_state, precision=peak_score)
    slot_probabilities = jax.nn.softmax(scale * slot_scores, axis=-1)
    mixing = jnp.einsum('thm,tjhm->htj', slot_probabilities, weight, precision=peak_score)
    output_rows = jnp.einsum('htj,jhd->thd', mixing, value_rows, precision=peak_score)
    output_rows = output_rows + jnp.einsum('gxq,xqa->gxa', slot_probabilities * leading_part, slot_value_state, precision=peak_score)
    final_entry = weight[-1]
    trailing_part = leading_part[-1][:, :, None]
    updated_key = trailing_part * slot_key_state + jnp.einsum('xrc,xrn->rcn', final_entry, key_rows, precision=peak_score)
    updated_value = trailing_part * slot_value_state + jnp.einsum('xrc,xrn->rcn', final_entry, value_rows, precision=peak_score)
    return ((updated_key, updated_value), output_rows)

def mixer(query_rows, key_rows, value_rows, log_gate):
    length = query_rows.shape[0]
    blocks = length // GROUP

    def split(array):
        return array.reshape((blocks, GROUP) + array.shape[1:])
    zeros = jnp.zeros((HEADS, SLOTS, HEAD), jnp.float32)
    carry, output_rows = lax.scan(jax.checkpoint(group_step), (zeros, zeros), (split(query_rows), split(key_rows), split(value_rows), split(log_gate)))
    return output_rows.reshape(length, HEADS, HEAD)

def forward(tokens, params, valid):
    norm1_gain, w_query, w_key, w_value, w_gate_low, w_gate_up, gate_bias, head_gain, w_swish, w_out, norm2_gain, w_ffn_gate, w_ffn_up, w_ffn_down = params
    count = tokens.shape[0]
    scale1 = lax.rsqrt(lax.optimization_barrier(jnp.mean(tokens * tokens, axis=-1, keepdims=True)) + norm_eps)
    normed = low(tokens * scale1 * norm1_gain)
    query_rows = low(low_back(matmul(normed, w_query)))
    key_rows = low(low_back(matmul(normed, w_key)))
    value_rows = low(low_back(matmul(normed, w_value)))
    low_rank = low(low_back(matmul(normed, w_gate_low)))
    logits = matmul(low_rank, w_gate_up.T) + gate_bias
    log_gate = jax.nn.log_sigmoid(logits) / gate_norm
    mixed = mixer(query_rows.reshape(count, HEADS, HEAD), key_rows.reshape(count, HEADS, HEAD), value_rows.reshape(count, HEADS, HEAD), log_gate.reshape(count, HEADS, SLOTS))
    head_scale = lax.rsqrt(lax.optimization_barrier(jnp.mean(mixed * mixed, axis=-1, keepdims=True)) + norm_eps)
    head_normed = mixed * head_scale * head_gain
    swish_pre = low_back(matmul(normed, w_swish))
    gated = low(low_back(head_normed.reshape(count, D) * jax.nn.silu(swish_pre)))
    hidden = tokens + low_back(matmul(gated, w_out))
    scale2 = lax.rsqrt(lax.optimization_barrier(jnp.mean(hidden * hidden, axis=-1, keepdims=True)) + norm_eps)
    normed2 = low(hidden * scale2 * norm2_gain)
    gate_pre = low_back(matmul(normed2, w_ffn_gate))
    up_pre = low_back(matmul(normed2, w_ffn_up))
    inner = low(low_back(jax.nn.silu(gate_pre) * up_pre))
    return valid * (hidden + low_back(matmul(inner, w_ffn_down)))

def reference(tokens, cotangent, lengths, norm1_gain, w_query, w_key, w_value, w_gate_low, w_gate_up, gate_bias, head_gain, w_swish, w_out, norm2_gain, w_ffn_gate, w_ffn_up, w_ffn_down):
    params = tuple((w.astype(jnp.float32) for w in (norm1_gain, w_query, w_key, w_value, w_gate_low, w_gate_up, gate_bias, head_gain, w_swish, w_out, norm2_gain, w_ffn_gate, w_ffn_up, w_ffn_down)))
    seq_tokens = tokens.astype(jnp.float32).reshape(SEQS, LENGTH, D)
    seq_grads = cotangent.astype(jnp.float32).reshape(SEQS, LENGTH, D)

    def step(total, item):
        row_tokens, row_grads, count = item
        valid = (jnp.arange(LENGTH, dtype=jnp.int32) < count).astype(row_tokens.dtype)[:, None]
        result, pullback = jax.vjp(lambda a, p: forward(a, p, valid), row_tokens, params)
        grad_tokens, grad_params = pullback(row_grads)
        return (jax.tree.map(jnp.add, total, grad_params), (result.astype(jnp.bfloat16), grad_tokens))
    zeros = jax.tree.map(jnp.zeros_like, params)
    grads, (results, grad_rows) = lax.scan(step, zeros, (seq_tokens, seq_grads, lengths))
    return (results.reshape(TOKENS, D), grad_rows.reshape(TOKENS, D), grads[0], grads[1], grads[2], grads[3], grads[4], grads[5], grads[6], grads[7], grads[8], grads[9], grads[10], grads[11], grads[12], grads[13])
```

```python
import functools

import jax
import jax.numpy as jnp
import numpy as np
from jax import lax
from jax.experimental import pallas as pl
from jax.experimental.pallas import tpu as pltpu
from jax.sharding import PartitionSpec as P

D = 1024
HEADS = 4
HEAD = 256
SLOTS = 64
norm_eps = 1e-06
gate_norm = 8.0
MESH = pl.DeviceIdType.MESH


class Place:
    def __init__(self, n_square, n_line):
        self.n_square, self.n_line = n_square, n_line
        dp = lax.axis_index("dp")
        self.z = lax.axis_index("shard")
        self.c = lax.rem(dp, 2)
        self.a = lax.div(dp, 2)

    def device(self, a, c, z):
        return {"dp": a * 2 + c, "shard": z}

    def slab(self, a, c, z):
        return (a * 2 + c) * self.n_line + z


def flip(value, bits):
    for b in range(8):
        if bits >> b & 1:
            digit = lax.rem(lax.div(value, 1 << b), 2)
            value = value + (1 - 2 * digit) * (1 << b)
    return value


def square_orders(n_square):
    bits = [1 << b for b in range((n_square - 1).bit_length())]
    return (bits, bits[::-1])


def stages(bits):
    held, out = [0], []
    for bit in bits:
        out.append((bit, list(held)))
        held = held + [m ^ bit for m in held]
    return out


def barrier(place):
    sem = pltpu.get_barrier_semaphore()
    peers = [place.device(place.a, 1 - place.c, place.z)]
    bit = 1
    while bit < place.n_square:
        peers.append(place.device(flip(place.a, bit), place.c, place.z))
        bit *= 2
    for k in range(1, place.n_line):
        peers.append(place.device(place.a, place.c, flip(place.z, k)))
    for peer in peers:
        pl.semaphore_signal(sem, inc=1, device_id=peer, device_id_type=MESH)
    pl.semaphore_wait(sem, len(peers))


def pieces_of(shapes, n_square):
    first, second = square_orders(n_square)
    out = []
    for i, (rows, cols) in enumerate(shapes):
        if cols >= 256:
            out.append((i, 0, cols // 2, first))
            out.append((i, cols // 2, cols // 2, second))
        else:
            out.append((i, 0, cols, first))
    return out


def gather_body(pieces, n_arrays, n_square, n_line, *refs):
    ins, outs = refs[:n_arrays], refs[n_arrays : 2 * n_arrays]
    local_sem, net_send, net_recv, core_send, core_recv = refs[2 * n_arrays :]
    p = Place(n_square, n_line)
    own = [
        pltpu.make_async_copy(ins[i], outs[i].at[p.slab(p.a, p.c, p.z)], local_sem.at[i])
        for i in range(n_arrays)
    ]
    for copy in own:
        copy.start()
    barrier(p)

    def at(piece, m, k, c=None):
        i, start, width, _ = pieces[piece]
        s = p.slab(flip(p.a, m), p.c if c is None else c, flip(p.z, k))
        return outs[i].at[s, :, pl.ds(start, width)]

    def source(piece, m, k):
        if m == 0 and k == 0:
            i, start, width, _ = pieces[piece]
            return ins[i].at[:, pl.ds(start, width)]
        return at(piece, m, k)

    def net(piece, m, k, to_m, to_k, peer, src=True):
        return pltpu.make_async_remote_copy(
            src_ref=source(piece, m, k),
            dst_ref=at(piece, m, k),
            send_sem=net_send.at[piece, to_m, to_k],
            recv_sem=net_recv.at[piece, to_m, to_k],
            device_id=peer,
            device_id_type=MESH,
        )

    def core(piece, m, k):
        return pltpu.make_async_remote_copy(
            src_ref=source(piece, m, k),
            dst_ref=at(piece, m, k),
            send_sem=core_send.at[piece, m, k],
            recv_sem=core_recv.at[piece, m, k],
            device_id=p.device(p.a, 1 - p.c, p.z),
            device_id_type=MESH,
        )

    def arrived(piece, m, k):
        pltpu.make_async_remote_copy(
            src_ref=at(piece, m, k),
            dst_ref=at(piece, m, k),
            send_sem=net_send.at[piece, m, k],
            recv_sem=net_recv.at[piece, m, k],
            device_id=p.device(p.a, 1 - p.c, p.z),
            device_id_type=MESH,
        ).wait_recv()

    started = []

    def go(copy):
        copy.start()
        started.append(copy)

    n_pieces = len(pieces)
    for k in range(1, n_line):
        for q in range(n_pieces):
            go(net(q, 0, 0, 0, k, p.device(p.a, p.c, flip(p.z, k))))
    n_bits = (n_square - 1).bit_length()
    for t in range(n_line + n_bits):
        for level in range(n_bits + 1):
            k = t - level
            if not 0 <= k < n_line:
                continue
            for q in range(n_pieces):
                bits = pieces[q][3]
                new = [0] if level == 0 else [m ^ bits[level - 1] for m in stages(bits)[level - 1][1]]
                for m in new:
                    if (m, k) != (0, 0):
                        arrived(q, m, k)
                    for bit in bits[level:]:
                        go(net(q, m, k, m ^ bit, k, p.device(flip(p.a, bit), p.c, p.z)))
                    go(core(q, m, k))
    for copy in own:
        copy.wait()
    for k in range(n_line):
        for q in range(n_pieces):
            for m in range(n_square):
                pltpu.make_async_remote_copy(
                    src_ref=at(q, m, k, 1 - p.c),
                    dst_ref=at(q, m, k, 1 - p.c),
                    send_sem=core_send.at[q, m, k],
                    recv_sem=core_recv.at[q, m, k],
                    device_id=p.device(p.a, 1 - p.c, p.z),
                    device_id_type=MESH,
                ).wait_recv()
    for copy in started:
        copy.wait_send()


def gather(arrays, n_square, n_line, collective_id):
    shapes = [a.shape for a in arrays]
    pieces = pieces_of(shapes, n_square)
    n = n_square * 2 * n_line
    sem = pltpu.SemaphoreType.DMA((len(pieces), n_square, n_line))
    any_space = pl.BlockSpec(memory_space=pl.ANY)
    return pl.pallas_call(
        functools.partial(gather_body, pieces, len(arrays), n_square, n_line),
        out_shape=[jax.ShapeDtypeStruct((n,) + s, a.dtype) for a, s in zip(arrays, shapes)],
        in_specs=[any_space] * len(arrays),
        out_specs=[any_space] * len(arrays),
        scratch_shapes=[pltpu.SemaphoreType.DMA((len(arrays),)), sem, sem, sem, sem],
        compiler_params=pltpu.CompilerParams(collective_id=collective_id, has_side_effects=True),
        name="gather_weights",
    )(*arrays)


def reduce_body(pieces, n_arrays, n_square, n_line, *refs):
    n_pieces = len(pieces)
    ins, outs = refs[:n_arrays], refs[n_arrays : 2 * n_arrays]
    rest = refs[2 * n_arrays :]
    mine, peer_part, landed = rest[:n_pieces], rest[n_pieces : 2 * n_pieces], rest[2 * n_pieces : 3 * n_pieces]
    local_sem, net_send, net_recv, core_send, core_recv = rest[3 * n_pieces :]
    p = Place(n_square, n_line)

    def load(q):
        i, start, width, _ = pieces[q]
        return pltpu.make_async_copy(
            ins[i].at[:, p.c, :, :, pl.ds(start, width)], mine[q], local_sem.at[q]
        )

    def core(q, k):
        i, start, width, _ = pieces[q]
        z = flip(p.z, k)
        return pltpu.make_async_remote_copy(
            src_ref=ins[i].at[:, 1 - p.c, z, :, pl.ds(start, width)],
            dst_ref=peer_part[q].at[:, z],
            send_sem=core_send.at[q, k],
            recv_sem=core_recv.at[q, k],
            device_id=p.device(p.a, 1 - p.c, p.z),
            device_id_type=MESH,
        )

    def net(q, m, k, bit):
        peer = p.device(flip(p.a, bit), p.c, p.z) if bit else p.device(p.a, p.c, flip(p.z, k))
        return pltpu.make_async_remote_copy(
            src_ref=mine[q].at[flip(p.a, m), flip(p.z, k)],
            dst_ref=landed[q].at[m, k],
            send_sem=net_send.at[q, m, k],
            recv_sem=net_recv.at[q, m, k],
            device_id=peer,
            device_id_type=MESH,
        )

    for q in range(n_pieces):
        load(q).start()
    barrier(p)
    ks = list(range(n_line))[::-1]
    for k in ks:
        for q in range(n_pieces):
            core(q, k).start()
    for q in range(n_pieces):
        load(q).wait()
    n_bits = (n_square - 1).bit_length()
    sent = []

    def add(ref, other):
        ref[...] = (ref[...].astype(jnp.float32) + other[...].astype(jnp.float32)).astype(ref.dtype)

    for t in range(n_line + n_bits):
        for level in range(n_bits, -1, -1):
            step = t - (n_bits - level)
            if not 0 <= step < n_line:
                continue
            k = ks[step]
            for q in range(n_pieces):
                bits = pieces[q][3]
                steps = stages(bits)
                if level == n_bits:
                    core(q, k).wait_recv()
                    order = sorted(range(n_square), key=lambda m: -(m & bits[-1]) if n_bits else 0)
                    for m in order:
                        a, z = flip(p.a, m), flip(p.z, k)
                        add(mine[q].at[a, z], peer_part[q].at[a, z])
                        if n_bits and m & bits[-1]:
                            copy = net(q, m, k, bits[-1])
                            copy.start()
                            sent.append(copy)
                else:
                    bit, kept = steps[level]
                    for m in kept:
                        net(q, m ^ bit, k, bit).wait_recv()
                        a, z = flip(p.a, m), flip(p.z, k)
                        add(mine[q].at[a, z], landed[q].at[m ^ bit, k])
                    if level:
                        lower = steps[level - 1][0]
                        for m in kept:
                            if m & lower:
                                copy = net(q, m, k, lower)
                                copy.start()
                                sent.append(copy)
                if level == 0 and k:
                    copy = net(q, 0, k, 0)
                    copy.start()
                    sent.append(copy)
    for q in range(n_pieces):
        i, start, width, _ = pieces[q]
        total = mine[q][p.a, p.z].astype(jnp.float32)
        for k in ks:
            if k:
                net(q, 0, k, 0).wait_recv()
                total = total + landed[q][0, k].astype(jnp.float32)
        outs[i][:, pl.ds(start, width)] = total
    for copy in sent:
        copy.wait_send()
    for k in ks:
        for q in range(n_pieces):
            core(q, k).wait_send()


def reduce_scatter(arrays, n_square, n_line, collective_id):
    shapes = [a.shape[1:] for a in arrays]
    pieces = pieces_of(shapes, n_square)
    views = [a.reshape((n_square, 2, n_line) + s) for a, s in zip(arrays, shapes)]
    sem = pltpu.SemaphoreType.DMA((len(pieces), n_square, n_line))
    core_sem = pltpu.SemaphoreType.DMA((len(pieces), n_line))
    any_space = pl.BlockSpec(memory_space=pl.ANY)
    boxes = [
        pltpu.VMEM((n_square, n_line, shapes[i][0], width), arrays[i].dtype)
        for i, start, width, _ in pieces
    ]
    return pl.pallas_call(
        functools.partial(reduce_body, pieces, len(arrays), n_square, n_line),
        out_shape=[jax.ShapeDtypeStruct(s, jnp.float32) for s in shapes],
        in_specs=[any_space] * len(arrays),
        out_specs=[pl.BlockSpec(memory_space=pltpu.VMEM)] * len(arrays),
        scratch_shapes=boxes * 3
        + [pltpu.SemaphoreType.DMA((len(pieces),)), sem, sem, core_sem, core_sem],
        compiler_params=pltpu.CompilerParams(
            collective_id=collective_id, has_side_effects=True, vmem_limit_bytes=60 << 20
        ),
        name="reduce_grads",
    )(*views)


f32, bf16 = jnp.float32, jnp.bfloat16
ROWS = 256
LEVELS = 8


def level_constants(rows):
    t, i = np.arange(rows)[:, None], np.arange(rows)[None, :]
    sums, masks = [], []
    for level in range((rows - 1).bit_length()):
        same = (t >> (level + 1)) == (i >> (level + 1))
        upper_t, upper_i = (t >> level) & 1, (i >> level) & 1
        sums.append(
            (same & (upper_t == 1) & (upper_i == 1) & (i <= t))
            | (same & (upper_t == 0) & (upper_i == 0) & (i > t))
        )
        masks.append((t > i) & (((t ^ i) >> level) == 1))
    sums += [i <= t, i > t]
    masks.append(t == i)
    return np.stack(sums).astype(bf16), np.stack(masks).astype(bf16)


def nn(a, b):
    return lax.dot_general(a, b, (((1,), (0,)), ((), ())), preferred_element_type=f32)


def nt(a, b):
    return lax.dot_general(a, b, (((1,), (1,)), ((), ())), preferred_element_type=f32)


def tn(a, b):
    return lax.dot_general(a, b, (((0,), (0,)), ((), ())), preferred_element_type=f32)


def split_low(x):
    high = x.astype(bf16)
    return high, (x - high.astype(f32)).astype(bf16)


def head_of_lane(shape):
    return lax.broadcasted_iota(jnp.int32, shape, 1) // SLOTS


def tall(x):
    head = head_of_lane(x.shape)
    zero = jnp.zeros_like(x)
    return jnp.concatenate([jnp.where(head == h, x, zero) for h in range(HEADS)], axis=0)


def wide(state):
    head = lax.broadcasted_iota(jnp.int32, state.shape, 0) // SLOTS
    zero = jnp.zeros_like(state)
    return jnp.concatenate([jnp.where(head == h, state, zero) for h in range(HEADS)], axis=1)


def of(x, h):
    return x[:, HEAD * h : HEAD * (h + 1)]


def slots(h):
    return slice(SLOTS * h, SLOTS * (h + 1))


def products(a, b):
    return jnp.concatenate([nt(of(a, h), of(b, h)) for h in range(HEADS)], axis=1).astype(bf16)


def masked(a, mask):
    return a * jnp.concatenate([mask] * HEADS, axis=1)


def share_of(log_gate):
    small = -log_gate * (1.0 + log_gate * (0.5 + log_gate * (1.0 / 6.0)))
    return jnp.where(log_gate > -0.01, small, 1.0 - jnp.exp(log_gate))


def head_sums(x):
    ones = (head_of_lane((256, 256)) == lax.broadcasted_iota(jnp.int32, (256, 256), 0) // SLOTS)
    ones = jnp.where(ones, 1.0, 0.0).astype(bf16)
    high, low = split_low(x)
    return nn(high, ones) + nn(low, ones)


SCALE = 1.5 * HEAD ** (-0.25)


def softmax_slots(scores):
    head = head_of_lane(scores.shape)
    peak = jnp.zeros_like(scores)
    for h in range(HEADS):
        top = jnp.max(jnp.where(head == h, scores, -jnp.inf), axis=1, keepdims=True)
        peak = jnp.where(head == h, top, peak)
    power = jnp.exp(scores - peak)
    return power / head_sums(power)


def decays(log_gate, sums_ref, decay_ref):
    high, low = split_low(log_gate)

    def one(level, unused):
        m = sums_ref[level]
        decay_ref[level] = jnp.exp(nn(m, high) + nn(m, low))
        return unused

    lax.fori_loop(0, LEVELS + 2, one, 0)
    ones = jnp.ones((ROWS, 256), bf16)
    return jnp.exp(tn(high, ones) + tn(low, ones))


def summaries(share_end, rows):
    return jnp.concatenate([tn(share_end, of(rows, h))[slots(h)] for h in range(HEADS)], axis=0)


def lower_scores(a_ref, share, decay_ref, masks_ref, total_ref, parts_ref=None):
    first = nn(masked(a_ref[...], masks_ref[LEVELS]), tall(share.astype(bf16)))
    total_ref[...] = first

    def one(level, unused):
        decay = decay_ref[level]
        part = decay * nn(
            masked(a_ref[...], masks_ref[level]), tall((decay * share).astype(bf16))
        )
        if parts_ref is not None:
            parts_ref[level] = part
        total_ref[...] += part
        return unused

    lax.fori_loop(0, LEVELS, one, 0)


def mixing(coefficient, share, decay_ref, masks_ref, out_ref):
    def pairs(x, f, mask):
        return masked(nt(x.astype(bf16), tall(f.astype(bf16))).astype(bf16), mask)

    out_ref[...] = pairs(coefficient, share, masks_ref[LEVELS])

    def one(level, unused):
        decay = decay_ref[level]
        out_ref[...] += pairs(coefficient * decay, decay * share, masks_ref[level])
        return unused

    lax.fori_loop(0, LEVELS, one, 0)


def line_barrier(z, n_line):
    dp = lax.axis_index("dp")
    sem = pltpu.get_barrier_semaphore()

    @pl.when(z > 0)
    def _():
        pl.semaphore_signal(sem, inc=1, device_id={"dp": dp, "shard": z - 1}, device_id_type=MESH)

    @pl.when(z < n_line - 1)
    def _():
        pl.semaphore_signal(sem, inc=1, device_id={"dp": dp, "shard": z + 1}, device_id_type=MESH)

    pl.semaphore_wait(sem, jnp.where(z > 0, 1, 0) + jnp.where(z < n_line - 1, 1, 0))


def line_copy(src, dst, send_sem, recv_sem, to):
    return pltpu.make_async_remote_copy(
        src_ref=src,
        dst_ref=dst,
        send_sem=send_sem,
        recv_sem=recv_sem,
        device_id={"dp": lax.axis_index("dp"), "shard": to},
        device_id_type=MESH,
    )


def mixer_forward(
    n_line, q_ref, k_ref, v_ref, gate_ref, sums_ref, masks_ref,
    mixed_ref, state_ref, scores_ref,
    decay_ref, a_ref, b_ref, in_ref, out_ref, send_sem, recv_sem,
):
    z = lax.axis_index("shard")
    line_barrier(z, n_line)
    log_gate = gate_ref[...]
    share = share_of(log_gate)
    through = decays(log_gate, sums_ref, decay_ref)
    share_end = (decay_ref[LEVELS + 1] * share).astype(bf16)
    k_sum = summaries(share_end, k_ref[...])
    v_sum = summaries(share_end, v_ref[...])

    @pl.when(z == 0)
    def _():
        in_ref[...] = jnp.zeros_like(in_ref)

    @pl.when(z > 0)
    def _():
        line_copy(out_ref, in_ref, send_sem, recv_sem, z - 1).wait_recv()

    @pl.when(z < n_line - 1)
    def _():
        out_ref[0] = (through * in_ref[0].astype(f32) + k_sum).astype(bf16)
        out_ref[1] = (through * in_ref[1].astype(f32) + v_sum).astype(bf16)
        line_copy(out_ref, in_ref, send_sem, recv_sem, z + 1).start()

    a_ref[...] = products(q_ref[...], k_ref[...])
    lower_scores(a_ref, share, decay_ref, masks_ref, scores_ref)
    before = decay_ref[LEVELS]
    scores = scores_ref[...] + before * nt(q_ref[...], wide(in_ref[0]))
    scores_ref[...] = scores
    chance = softmax_slots(SCALE * scores)
    mixing(chance, share, decay_ref, masks_ref, b_ref)
    carried = nn((chance * before).astype(bf16), wide(in_ref[1]))
    b = b_ref[...]
    v = v_ref[...]
    for h in range(HEADS):
        mixed_ref[:, HEAD * h : HEAD * (h + 1)] = nn(of(b, h), of(v, h)) + of(carried, h)
    state_ref[...] = in_ref[...]

    @pl.when(z < n_line - 1)
    def _():
        line_copy(out_ref, in_ref, send_sem, recv_sem, z + 1).wait_send()


def mixer_backward(
    n_line, q_ref, k_ref, v_ref, gate_ref, sums_ref, masks_ref, back_masks_ref, state_ref, scores_ref, g_ref,
    gq_ref, gk_ref, gv_ref, dgate_ref,
    decay_ref, a_ref, av_ref, at_ref, avt_ref, b_ref, bk_ref, s_parts, d_parts, s_sum, d_sum, shares_ref, in_ref, out_ref, send_sem, recv_sem,
):
    z = lax.axis_index("shard")
    line_barrier(z, n_line)
    log_gate = gate_ref[...]
    share = share_of(log_gate)
    through = decays(log_gate, sums_ref, decay_ref)
    q, k, v = q_ref[...], k_ref[...], v_ref[...]
    g = g_ref[...].astype(bf16)
    before, after = decay_ref[LEVELS], decay_ref[LEVELS + 1]
    key_in, value_in = state_ref[0], state_ref[1]
    chance = softmax_slots(SCALE * scores_ref[...])
    av_ref[...] = products(g, v)
    lower_scores(av_ref, share, decay_ref, masks_ref, d_sum, d_parts)
    d_state = before * nt(g, wide(value_in))
    slope = d_sum[...] + d_state
    spread = SCALE * chance * (slope - head_sums(chance * slope))
    chance_before = (chance * before).astype(bf16)
    spread_before = (spread * before).astype(bf16)
    key_sum = summaries(spread_before, q)
    value_sum = summaries(chance_before, g)

    @pl.when(z == n_line - 1)
    def _():
        in_ref[...] = jnp.zeros_like(in_ref)

    @pl.when(z < n_line - 1)
    def _():
        line_copy(out_ref, in_ref, send_sem, recv_sem, z + 1).wait_recv()

    @pl.when(z > 0)
    def _():
        out_ref[0] = (through * in_ref[0].astype(f32) + key_sum).astype(bf16)
        out_ref[1] = (through * in_ref[1].astype(f32) + value_sum).astype(bf16)
        line_copy(out_ref, in_ref, send_sem, recv_sem, z - 1).start()

    a_ref[...] = products(q, k)
    at_ref[...] = products(k, q)
    avt_ref[...] = products(v, g)
    lower_scores(a_ref, share, decay_ref, masks_ref, s_sum, s_parts)
    s_state = before * nt(q, wide(key_in))
    mixing(chance, share, decay_ref, masks_ref, b_ref)
    mixing(spread, share, decay_ref, masks_ref, bk_ref)
    dgate_ref[...] = tn(sums_ref[LEVELS], (spread * s_state + chance * d_state).astype(bf16))
    diagonal = back_masks_ref[LEVELS]
    shares_ref[...] = nn(masked(at_ref[...], diagonal), tall(spread.astype(bf16))) + nn(
        masked(avt_ref[...], diagonal), tall(chance.astype(bf16))
    )

    def one(level, unused):
        decay = decay_ref[level]
        mask = back_masks_ref[level]
        taken = decay * (
            nn(masked(at_ref[...], mask), tall((spread * decay).astype(bf16)))
            + nn(masked(avt_ref[...], mask), tall((chance * decay).astype(bf16)))
        )
        shares_ref[...] += taken
        given = spread * s_parts[level] + chance * d_parts[level]
        place = lax.broadcasted_iota(jnp.int32, (ROWS, 256), 0)
        upper = lax.bitwise_and(lax.shift_right_logical(place, level), 1) == 1
        both = jnp.where(upper, given, taken * share).astype(bf16)
        dgate_ref[...] += tn(sums_ref[level], both)
        return unused

    lax.fori_loop(0, LEVELS, one, 0)
    out_key, out_value = in_ref[0], in_ref[1]
    wide_key, wide_value = wide(out_key), wide(out_value)
    taken = after * (nt(k, wide_key) + nt(v, wide_value))
    shares = shares_ref[...] + taken
    kept = key_in.astype(f32) * out_key.astype(f32) + value_in.astype(f32) * out_value.astype(f32)
    high, low = split_low(kept * through)
    ones = jnp.ones((8, 256), bf16)
    kept_row = (nt(ones, high) + nt(ones, low))[:1]
    dgate = dgate_ref[...] + tn(sums_ref[LEVELS + 1], (taken * share).astype(bf16)) + kept_row
    dgate_ref[...] = dgate - jnp.exp(log_gate) * shares
    end = (after * share).astype(bf16)
    q_state = nn(spread_before, wide(key_in))
    k_state = nn(end, wide_key)
    v_state = nn(end, wide_value)
    b, bk = b_ref[...], bk_ref[...]
    for h in range(HEADS):
        at = slice(HEAD * h, HEAD * (h + 1))
        gq_ref[:, at] = (nn(of(bk, h), of(k, h)) + of(q_state, h)).astype(bf16)
        gk_ref[:, at] = (tn(of(bk, h), of(q, h)) + of(k_state, h)).astype(bf16)
        gv_ref[:, at] = (tn(of(b, h), of(g, h)) + of(v_state, h)).astype(bf16)

    @pl.when(z > 0)
    def _():
        line_copy(out_ref, in_ref, send_sem, recv_sem, z - 1).wait_send()


def run_mixer_forward(n_line, q, k, v, log_gate, sums, masks, collective_id):
    whole = pl.BlockSpec(memory_space=pltpu.VMEM)
    state = pltpu.VMEM((2, 256, HEAD), bf16)
    return pl.pallas_call(
        functools.partial(mixer_forward, n_line),
        out_shape=[
            jax.ShapeDtypeStruct((ROWS, D), f32),
            jax.ShapeDtypeStruct((2, 256, HEAD), bf16),
            jax.ShapeDtypeStruct((ROWS, 256), f32),
        ],
        in_specs=[whole] * 6,
        out_specs=[whole] * 3,
        scratch_shapes=[
            pltpu.VMEM((LEVELS + 2, ROWS, 256), f32),
            pltpu.VMEM((ROWS, HEADS * ROWS), bf16),
            pltpu.VMEM((ROWS, HEADS * ROWS), bf16),
            state,
            state,
            pltpu.SemaphoreType.DMA,
            pltpu.SemaphoreType.DMA,
        ],
        compiler_params=pltpu.CompilerParams(
            collective_id=collective_id, has_side_effects=True, vmem_limit_bytes=40 << 20
        ),
        name="mixer_forward",
    )(q, k, v, log_gate, sums, masks)


def run_mixer_backward(n_line, q, k, v, log_gate, sums, masks, back_masks, state, scores, g, collective_id):
    whole = pl.BlockSpec(memory_space=pltpu.VMEM)
    pair = pltpu.VMEM((ROWS, HEADS * ROWS), bf16)
    box = pltpu.VMEM((2, 256, HEAD), bf16)
    parts = pltpu.VMEM((LEVELS, ROWS, 256), f32)
    flat = pltpu.VMEM((ROWS, 256), f32)
    return pl.pallas_call(
        functools.partial(mixer_backward, n_line),
        out_shape=[jax.ShapeDtypeStruct((ROWS, D), bf16)] * 3 + [jax.ShapeDtypeStruct((ROWS, 256), f32)],
        in_specs=[whole] * 10,
        out_specs=[whole] * 4,
        scratch_shapes=[pltpu.VMEM((LEVELS + 2, ROWS, 256), f32)]
        + [pair] * 6
        + [parts, parts, flat, flat, flat, box, box, pltpu.SemaphoreType.DMA, pltpu.SemaphoreType.DMA],
        compiler_params=pltpu.CompilerParams(
            collective_id=collective_id, has_side_effects=True, vmem_limit_bytes=50 << 20
        ),
        name="mixer_backward",
    )(q, k, v, log_gate, sums, masks, back_masks, state, scores, g)


def silu_slope(value):
    sig = jax.nn.sigmoid(value)
    return sig * (1.0 + value * (1.0 - sig))


def flat_pack(parts, rows, dtype):
    flat = jnp.concatenate([p.reshape(-1) for p in parts]).astype(dtype)
    return jnp.pad(flat, (0, rows * 128 - flat.shape[0])).reshape(rows, 128)


def flat_unpack(packed, shapes):
    n = packed.shape[0]
    flat = packed.reshape(n, -1)
    out, start = [], 0
    for shape in shapes:
        size = int(np.prod(shape))
        out.append(flat[:, start : start + size].reshape((n * shape[0],) + tuple(shape[1:])))
        start += size
    return out


def per_device(
    n_square, n_line,
    tokens, cotangent, lengths, norm1_gain, w_query, w_key, w_value, w_gate_low, w_gate_up,
    gate_bias, head_gain, w_swish, w_out, norm2_gain, w_ffn_gate, w_ffn_up, w_ffn_down,
):
    count = tokens.shape[0]
    n = n_square * 2 * n_line
    small_parts = (w_gate_low, w_gate_up, gate_bias, head_gain, norm1_gain, norm2_gain)
    small_shapes = [p.shape for p in small_parts]
    small = flat_pack(small_parts, 16, bf16)
    mixer_in = jnp.concatenate([w_query, w_key, w_value, w_swish], axis=1)
    ffn_in = jnp.concatenate([w_ffn_gate, w_ffn_up], axis=1)
    got = gather([mixer_in, w_out, small, ffn_in, w_ffn_down], n_square, n_line, 1)
    w_in = got[0].reshape(D, 4 * D)
    w_o = got[1].reshape(D, D)
    w_gu = got[3].reshape(D, -1)
    w_d = got[4].reshape(-1, D)
    ff = w_d.shape[0]
    low_w, up_w, bias, hgain, gain1, gain2 = flat_unpack(got[2], small_shapes)
    bias, hgain, gain1, gain2 = (x.astype(f32) for x in (bias, hgain, gain1, gain2))
    sums, masks = level_constants(count)
    back_masks = np.ascontiguousarray(np.swapaxes(masks, 1, 2))

    position = lax.axis_index("shard") * count + jnp.arange(count, dtype=jnp.int32)
    valid = (position < lengths[0]).astype(f32)[:, None]
    resid = tokens.astype(f32)
    scale1 = lax.rsqrt(jnp.mean(resid * resid, axis=-1, keepdims=True) + norm_eps)
    normed = (resid * scale1 * gain1).astype(bf16)
    qkvs = nn(normed, w_in)
    q, k, v = (qkvs[:, i * D : (i + 1) * D].astype(bf16) for i in range(3))
    swish_pre = qkvs[:, 3 * D :]
    low_rank = nn(normed, low_w).astype(bf16)
    logits = nt(low_rank, up_w) + bias
    log_gate = jax.nn.log_sigmoid(logits) / gate_norm
    mixed, state, scores = run_mixer_forward(n_line, q, k, v, log_gate, sums, masks, 2)
    mixed = mixed.reshape(count, HEADS, HEAD)
    head_scale = lax.rsqrt(jnp.mean(mixed * mixed, axis=-1, keepdims=True) + norm_eps)
    head_normed = (mixed * head_scale * hgain).reshape(count, D)
    swish_act = jax.nn.silu(swish_pre)
    gated = (head_normed * swish_act).astype(bf16)
    hidden = resid + nn(gated, w_o)
    scale2 = lax.rsqrt(jnp.mean(hidden * hidden, axis=-1, keepdims=True) + norm_eps)
    normed2 = (hidden * scale2 * gain2).astype(bf16)
    gu = nn(normed2, w_gu)
    gate_pre, up_pre = gu[:, :ff], gu[:, ff:]
    inner = (jax.nn.silu(gate_pre) * up_pre).astype(bf16)
    output = (valid * (hidden + nn(inner, w_d))).astype(bf16)

    grad_out = cotangent.astype(f32) * valid
    grad_low = grad_out.astype(bf16)
    d_down = tn(inner, grad_low).astype(bf16)
    grad_inner = nt(grad_low, w_d).astype(bf16).astype(f32)
    grad_gate = (grad_inner * up_pre * silu_slope(gate_pre)).astype(bf16)
    grad_up = (grad_inner * jax.nn.silu(gate_pre)).astype(bf16)
    grad_gu = jnp.concatenate([grad_gate, grad_up], axis=1)
    d_gu = tn(normed2, grad_gu).astype(bf16)
    grad_normed2 = nt(grad_gu, w_gu)
    d_gain2 = jnp.sum(grad_normed2 * hidden * scale2, axis=0)
    spread2 = grad_normed2 * gain2
    grad_hidden = (
        grad_out
        + scale2 * spread2
        - hidden * scale2**3 * jnp.mean(spread2 * hidden, axis=-1, keepdims=True)
    )
    s_gu, s_down = reduce_scatter(
        [d_gu.reshape(n, D // n, -1), d_down.reshape(n, ff // n, D)], n_square, n_line, 3
    )
    grad_branch = grad_hidden.astype(bf16)
    d_out = tn(gated, grad_branch).astype(bf16)
    grad_gated = nt(grad_branch, w_o).astype(bf16).astype(f32)
    grad_swish = (grad_gated * head_normed * silu_slope(swish_pre)).astype(bf16)
    grad_head = (grad_gated * swish_act).reshape(count, HEADS, HEAD)
    d_head_gain = jnp.sum(grad_head * mixed * head_scale, axis=(0, 1))
    spread_o = grad_head * hgain
    grad_mixed = head_scale * spread_o - mixed * head_scale**3 * jnp.mean(
        spread_o * mixed, axis=-1, keepdims=True
    )
    grad_q, grad_k, grad_v, grad_log = run_mixer_backward(
        n_line, q, k, v, log_gate, sums, masks, back_masks, state, scores, grad_mixed.reshape(count, D), 4
    )
    grad_logits = grad_log / gate_norm * jax.nn.sigmoid(-logits)
    d_bias = jnp.sum(grad_logits, axis=0)
    logits_high, logits_low = split_low(grad_logits)
    d_up = tn(logits_high, low_rank) + tn(logits_low, low_rank)
    grad_lowrank = (nn(logits_high, up_w) + nn(logits_low, up_w)).astype(bf16)
    grad_qkvs = jnp.concatenate([grad_q, grad_k, grad_v, grad_swish], axis=1)
    d_in = tn(normed, grad_qkvs).astype(bf16)
    d_low = tn(normed, grad_lowrank)
    grad_normed = nt(grad_qkvs, w_in) + nt(grad_lowrank, low_w)
    d_gain1 = jnp.sum(grad_normed * resid * scale1, axis=0)
    spread1 = grad_normed * gain1
    d_tokens = (
        grad_hidden
        + scale1 * spread1
        - resid * scale1**3 * jnp.mean(spread1 * resid, axis=-1, keepdims=True)
    )
    d_small = jnp.concatenate(
        [x.reshape(n, -1) for x in (d_low, d_up, d_bias, d_head_gain, d_gain1, d_gain2)], axis=1
    )
    d_small = jnp.pad(d_small, ((0, 0), (0, 1024 - d_small.shape[1]))).reshape(n, 8, 128)
    s_in, s_out, s_small = reduce_scatter(
        [d_in.reshape(n, D // n, -1), d_out.reshape(n, D // n, D), d_small], n_square, n_line, 5
    )
    o_low, o_up, o_bias, o_hgain, o_gain1, o_gain2 = flat_unpack(s_small[None], small_shapes)
    return (
        output, d_tokens, o_gain1,
        s_in[:, :D], s_in[:, D : 2 * D], s_in[:, 2 * D : 3 * D],
        o_low, o_up, o_bias, o_hgain,
        s_in[:, 3 * D :], s_out, o_gain2,
        s_gu[:, :ff], s_gu[:, ff:], s_down,
    )


def solution(mesh):
    rows, row = P(("dp", "shard"), None), P(("dp", "shard"))
    placed = (rows, rows, P("dp"), row, rows, rows, rows, rows, rows, row, row, rows, rows, row, rows, rows, rows)
    out = (rows, rows, row, rows, rows, rows, rows, rows, row, row, rows, rows, row, rows, rows, rows)
    return jax.shard_map(
        functools.partial(per_device, mesh.shape["dp"] // 2, mesh.shape["shard"]),
        mesh=mesh,
        in_specs=placed,
        out_specs=out,
        check_vma=False,
    )
```

```python
import functools

import jax
import jax.numpy as jnp
import numpy as np
from jax import lax
from jax.experimental import pallas as pl
from jax.experimental.pallas import tpu as pltpu
from jax.sharding import PartitionSpec as P

D = 1024
HEADS = 4
HEAD = 256
SLOTS = 64
norm_eps = 1e-06
gate_norm = 8.0
MESH = pl.DeviceIdType.MESH


class Place:
    def __init__(self, n_square, n_line):
        self.n_square, self.n_line = n_square, n_line
        dp = lax.axis_index("dp")
        self.z = lax.axis_index("shard")
        self.c = lax.rem(dp, 2)
        self.a = lax.div(dp, 2)

    def device(self, a, c, z):
        return {"dp": a * 2 + c, "shard": z}

    def slab(self, a, c, z):
        return (a * 2 + c) * self.n_line + z


def flip(value, bits):
    for b in range(8):
        if bits >> b & 1:
            digit = lax.rem(lax.div(value, 1 << b), 2)
            value = value + (1 - 2 * digit) * (1 << b)
    return value


def square_orders(n_square):
    bits = [1 << b for b in range((n_square - 1).bit_length())]
    return (bits, bits[::-1])


def stages(bits):
    held, out = [0], []
    for bit in bits:
        out.append((bit, list(held)))
        held = held + [m ^ bit for m in held]
    return out


def barrier(place):
    sem = pltpu.get_barrier_semaphore()
    peers = [place.device(place.a, 1 - place.c, place.z)]
    bit = 1
    while bit < place.n_square:
        peers.append(place.device(flip(place.a, bit), place.c, place.z))
        bit *= 2
    for k in range(1, place.n_line):
        peers.append(place.device(place.a, place.c, flip(place.z, k)))
    for peer in peers:
        pl.semaphore_signal(sem, inc=1, device_id=peer, device_id_type=MESH)
    pl.semaphore_wait(sem, len(peers))


def pieces_of(shapes, n_square):
    first, second = square_orders(n_square)
    out = []
    for i, (rows, cols) in enumerate(shapes):
        if cols >= 256:
            out.append((i, 0, cols // 2, first))
            out.append((i, cols // 2, cols // 2, second))
        else:
            out.append((i, 0, cols, first))
    return out


class Gather:
    def __init__(self, pieces, ins, outs, sems, n_square, n_line):
        self.pieces, self.ins, self.outs = pieces, ins, outs
        self.local_sem, self.net_send, self.net_recv, self.core_send, self.core_recv = sems
        self.n_square, self.n_line = n_square, n_line
        self.p = Place(n_square, n_line)
        self.own = [
            pltpu.make_async_copy(
                ins[i], outs[i].at[self.p.slab(self.p.a, self.p.c, self.p.z)], self.local_sem.at[i]
            )
            for i in range(len(ins))
        ]
        self.started, self.todo = [], []
        n_bits = (n_square - 1).bit_length()
        for t in range(n_line + n_bits):
            for level in range(n_bits + 1):
                k = t - level
                if not 0 <= k < n_line:
                    continue
                for q in range(len(pieces)):
                    bits = pieces[q][3]
                    new = [0] if level == 0 else [m ^ bits[level - 1] for m in stages(bits)[level - 1][1]]
                    self.todo += [(level, q, m, k) for m in new]

    def at(self, q, m, k, c=None):
        i, start, width, _ = self.pieces[q]
        p = self.p
        s = p.slab(flip(p.a, m), p.c if c is None else c, flip(p.z, k))
        return self.outs[i].at[s, :, pl.ds(start, width)]

    def source(self, q, m, k):
        if m == 0 and k == 0:
            i, start, width, _ = self.pieces[q]
            return self.ins[i].at[:, pl.ds(start, width)]
        return self.at(q, m, k)

    def go(self, q, m, k, sems, index, peer):
        copy = pltpu.make_async_remote_copy(
            src_ref=self.source(q, m, k),
            dst_ref=self.at(q, m, k),
            send_sem=sems[0].at[index],
            recv_sem=sems[1].at[index],
            device_id=peer,
            device_id_type=MESH,
        )
        copy.start()
        self.started.append(copy)

    def arrived(self, q, m, k, sems, c):
        p = self.p
        pltpu.make_async_remote_copy(
            src_ref=self.at(q, m, k, c),
            dst_ref=self.at(q, m, k, c),
            send_sem=sems[0].at[q, m, k],
            recv_sem=sems[1].at[q, m, k],
            device_id=p.device(p.a, 1 - p.c, p.z),
            device_id_type=MESH,
        ).wait_recv()

    def load_own(self):
        for copy in self.own:
            copy.start()

    def start(self):
        p = self.p
        net = (self.net_send, self.net_recv)
        for k in range(1, self.n_line):
            for q in range(len(self.pieces)):
                self.go(q, 0, 0, net, (q, 0, k), p.device(p.a, p.c, flip(p.z, k)))

    def run(self, n):
        p = self.p
        net, core = (self.net_send, self.net_recv), (self.core_send, self.core_recv)
        for level, q, m, k in self.todo[:n]:
            if (m, k) != (0, 0):
                self.arrived(q, m, k, net, p.c)
            for bit in self.pieces[q][3][level:]:
                self.go(q, m, k, net, (q, m ^ bit, k), p.device(flip(p.a, bit), p.c, p.z))
            self.go(q, m, k, core, (q, m, k), p.device(p.a, 1 - p.c, p.z))
        self.todo = self.todo[n:]

    def finish(self):
        self.run(len(self.todo))
        for copy in self.own:
            copy.wait()
        for k in range(self.n_line):
            for q in range(len(self.pieces)):
                for m in range(self.n_square):
                    self.arrived(q, m, k, (self.core_send, self.core_recv), 1 - self.p.c)
        for copy in self.started:
            copy.wait_send()


def gather_body(pieces, n_arrays, n_square, n_line, *refs):
    job = Gather(pieces, refs[:n_arrays], refs[n_arrays : 2 * n_arrays], refs[2 * n_arrays :], n_square, n_line)
    job.load_own()
    barrier(job.p)
    job.start()
    job.finish()


def gather_sems(n_pieces, n_arrays, n_square, n_line):
    sem = pltpu.SemaphoreType.DMA((n_pieces, n_square, n_line))
    return [pltpu.SemaphoreType.DMA((n_arrays,)), sem, sem, sem, sem]


def gather(arrays, n_square, n_line, collective_id):
    shapes = [a.shape for a in arrays]
    pieces = pieces_of(shapes, n_square)
    n = n_square * 2 * n_line
    any_space = pl.BlockSpec(memory_space=pl.ANY)
    return pl.pallas_call(
        functools.partial(gather_body, pieces, len(arrays), n_square, n_line),
        out_shape=[jax.ShapeDtypeStruct((n,) + s, a.dtype) for a, s in zip(arrays, shapes)],
        in_specs=[any_space] * len(arrays),
        out_specs=[any_space] * len(arrays),
        scratch_shapes=gather_sems(len(pieces), len(arrays), n_square, n_line),
        compiler_params=pltpu.CompilerParams(collective_id=collective_id, has_side_effects=True),
        name="gather_weights",
    )(*arrays)


def add_into(ref, other):
    ref[...] = (ref[...].astype(jnp.float32) + other[...].astype(jnp.float32)).astype(ref.dtype)


class Reduce:
    def __init__(self, pieces, mine, theirs, peer_part, landed, sems, n_square, n_line):
        self.pieces, self.mine, self.theirs = pieces, mine, theirs
        self.peer_part, self.landed = peer_part, landed
        self.net_send, self.net_recv, self.core_send, self.core_recv = sems
        self.n_square, self.n_line = n_square, n_line
        self.p = Place(n_square, n_line)
        self.ks = list(range(n_line))[::-1]
        self.sent, self.todo = [], []
        n_bits = (n_square - 1).bit_length()
        for t in range(n_line + n_bits):
            for level in range(n_bits, -1, -1):
                step = t - (n_bits - level)
                if 0 <= step < n_line:
                    for q in range(len(pieces)):
                        self.todo.append((level, q, self.ks[step]))

    def core(self, q, k):
        p = self.p
        return pltpu.make_async_remote_copy(
            src_ref=self.theirs(q, k),
            dst_ref=self.peer_part[q].at[:, flip(p.z, k)],
            send_sem=self.core_send.at[q, k],
            recv_sem=self.core_recv.at[q, k],
            device_id=p.device(p.a, 1 - p.c, p.z),
            device_id_type=MESH,
        )

    def net(self, q, m, k, bit):
        p = self.p
        peer = p.device(flip(p.a, bit), p.c, p.z) if bit else p.device(p.a, p.c, flip(p.z, k))
        return pltpu.make_async_remote_copy(
            src_ref=self.mine(q, flip(p.a, m), flip(p.z, k)),
            dst_ref=self.landed[q].at[m, k],
            send_sem=self.net_send.at[q, m, k],
            recv_sem=self.net_recv.at[q, m, k],
            device_id=peer,
            device_id_type=MESH,
        )

    def go(self, q, m, k, bit):
        copy = self.net(q, m, k, bit)
        copy.start()
        self.sent.append(copy)

    def start(self, pieces=None):
        for k in self.ks:
            for q in range(len(self.pieces)) if pieces is None else pieces:
                self.core(q, k).start()

    def run(self, n):
        p = self.p
        n_bits = (self.n_square - 1).bit_length()
        for level, q, k in self.todo[:n]:
            bits = self.pieces[q][3]
            if level == n_bits:
                self.core(q, k).wait_recv()
                for m in sorted(range(self.n_square), key=lambda m: -(m & bits[-1])):
                    a, z = flip(p.a, m), flip(p.z, k)
                    add_into(self.mine(q, a, z), self.peer_part[q].at[a, z])
                    if m & bits[-1]:
                        self.go(q, m, k, bits[-1])
            else:
                bit, kept = stages(bits)[level]
                for m in kept:
                    self.net(q, m ^ bit, k, bit).wait_recv()
                    add_into(self.mine(q, flip(p.a, m), flip(p.z, k)), self.landed[q].at[m ^ bit, k])
                    if level and m & bits[level - 1]:
                        self.go(q, m, k, bits[level - 1])
            if level == 0 and k:
                self.go(q, 0, k, 0)
        self.todo = self.todo[n:]

    def finish(self, outs):
        self.run(len(self.todo))
        p = self.p
        for q in range(len(self.pieces)):
            i, start, width, _ = self.pieces[q]
            total = self.mine(q, p.a, p.z)[...].astype(jnp.float32)
            for k in self.ks:
                if k:
                    self.net(q, 0, k, 0).wait_recv()
                    total = total + self.landed[q][0, k].astype(jnp.float32)
            outs[i][:, pl.ds(start, width)] = total
        for copy in self.sent:
            copy.wait_send()
        for k in self.ks:
            for q in range(len(self.pieces)):
                self.core(q, k).wait_send()


def reduce_boxes(pieces, shapes, dtypes, n_square, n_line):
    return [
        pltpu.VMEM((n_square, n_line, shapes[i][0], width), dtypes[i]) for i, start, width, _ in pieces
    ]


def reduce_sems(n_pieces, n_square, n_line):
    sem = pltpu.SemaphoreType.DMA((n_pieces, n_square, n_line))
    core_sem = pltpu.SemaphoreType.DMA((n_pieces, n_line))
    return [sem, sem, core_sem, core_sem]


class ReduceFromHbm(Reduce):
    def __init__(self, pieces, ins, mine, peer_part, landed, local_sem, sems, n_square, n_line):
        p = Place(n_square, n_line)

        def columns(q):
            i, start, width, _ = pieces[q]
            return ins[i], pl.ds(start, width)

        def theirs(q, k):
            ref, cols = columns(q)
            return ref.at[:, 1 - p.c, flip(p.z, k), :, cols]

        super().__init__(pieces, lambda q, a, z: mine[q].at[a, z], theirs, peer_part, landed, sems, n_square, n_line)
        self.loads = []
        for q in range(len(pieces)):
            ref, cols = columns(q)
            self.loads.append(pltpu.make_async_copy(ref.at[:, p.c, :, :, cols], mine[q], local_sem.at[q]))

    def load(self):
        for copy in self.loads:
            copy.start()

    def loaded(self):
        for copy in self.loads:
            copy.wait()


def reduce_body(pieces, n_arrays, n_square, n_line, *refs):
    n = len(pieces)
    ins, outs, rest = refs[:n_arrays], refs[n_arrays : 2 * n_arrays], refs[2 * n_arrays :]
    job = ReduceFromHbm(
        pieces, ins, rest[:n], rest[n : 2 * n], rest[2 * n : 3 * n], rest[3 * n], rest[3 * n + 1 :], n_square, n_line
    )
    job.load()
    barrier(job.p)
    job.start()
    job.loaded()
    job.finish(outs)


def reduce_scatter(arrays, n_square, n_line, collective_id):
    shapes = [a.shape[1:] for a in arrays]
    pieces = pieces_of(shapes, n_square)
    views = [a.reshape((n_square, 2, n_line) + s) for a, s in zip(arrays, shapes)]
    any_space = pl.BlockSpec(memory_space=pl.ANY)
    boxes = reduce_boxes(pieces, shapes, [x.dtype for x in arrays], n_square, n_line)
    return pl.pallas_call(
        functools.partial(reduce_body, pieces, len(arrays), n_square, n_line),
        out_shape=[jax.ShapeDtypeStruct(s, jnp.float32) for s in shapes],
        in_specs=[any_space] * len(arrays),
        out_specs=[pl.BlockSpec(memory_space=pltpu.VMEM)] * len(arrays),
        scratch_shapes=boxes * 3
        + [pltpu.SemaphoreType.DMA((len(pieces),))]
        + reduce_sems(len(pieces), n_square, n_line),
        compiler_params=pltpu.CompilerParams(
            collective_id=collective_id, has_side_effects=True, vmem_limit_bytes=60 << 20
        ),
        name="reduce_grads",
    )(*views)


f32, bf16 = jnp.float32, jnp.bfloat16
ROWS = 256
LEVELS = 8


def level_constants(rows):
    t, i = np.arange(rows)[:, None], np.arange(rows)[None, :]
    sums, masks = [], []
    for level in range((rows - 1).bit_length()):
        same = (t >> (level + 1)) == (i >> (level + 1))
        upper_t, upper_i = (t >> level) & 1, (i >> level) & 1
        sums.append(
            (same & (upper_t == 1) & (upper_i == 1) & (i <= t))
            | (same & (upper_t == 0) & (upper_i == 0) & (i > t))
        )
        masks.append((t > i) & (((t ^ i) >> level) == 1))
    sums += [i <= t, i > t]
    masks.append(t == i)
    return np.stack(sums).astype(bf16), np.stack(masks).astype(bf16)


def nn(a, b):
    return lax.dot_general(a, b, (((1,), (0,)), ((), ())), preferred_element_type=f32)


def nt(a, b):
    return lax.dot_general(a, b, (((1,), (1,)), ((), ())), preferred_element_type=f32)


def tn(a, b):
    return lax.dot_general(a, b, (((0,), (0,)), ((), ())), preferred_element_type=f32)


def split_low(x):
    high = x.astype(bf16)
    return high, (x - high.astype(f32)).astype(bf16)


def head_of_lane(shape):
    return lax.broadcasted_iota(jnp.int32, shape, 1) // SLOTS


def tall(x):
    head = head_of_lane(x.shape)
    zero = jnp.zeros_like(x)
    return jnp.concatenate([jnp.where(head == h, x, zero) for h in range(HEADS)], axis=0)


def wide(state):
    head = lax.broadcasted_iota(jnp.int32, state.shape, 0) // SLOTS
    zero = jnp.zeros_like(state)
    return jnp.concatenate([jnp.where(head == h, state, zero) for h in range(HEADS)], axis=1)


def of(x, h):
    return x[:, HEAD * h : HEAD * (h + 1)]


def slots(h):
    return slice(SLOTS * h, SLOTS * (h + 1))


def products(a, b):
    return jnp.concatenate([nt(of(a, h), of(b, h)) for h in range(HEADS)], axis=1).astype(bf16)


def masked(a, mask):
    return a * jnp.concatenate([mask] * HEADS, axis=1)


def share_of(log_gate):
    small = -log_gate * (1.0 + log_gate * (0.5 + log_gate * (1.0 / 6.0)))
    return jnp.where(log_gate > -0.01, small, 1.0 - jnp.exp(log_gate))


def head_sums(x):
    ones = (head_of_lane((256, 256)) == lax.broadcasted_iota(jnp.int32, (256, 256), 0) // SLOTS)
    ones = jnp.where(ones, 1.0, 0.0).astype(bf16)
    high, low = split_low(x)
    return nn(high, ones) + nn(low, ones)


SCALE = 1.5 * HEAD ** (-0.25)


def softmax_slots(scores):
    head = head_of_lane(scores.shape)
    peak = jnp.zeros_like(scores)
    for h in range(HEADS):
        top = jnp.max(jnp.where(head == h, scores, -jnp.inf), axis=1, keepdims=True)
        peak = jnp.where(head == h, top, peak)
    power = jnp.exp(scores - peak)
    return power / head_sums(power)


def decays(log_gate, sums_ref, decay_ref):
    high, low = split_low(log_gate)

    def one(level, unused):
        m = sums_ref[level]
        decay_ref[level] = jnp.exp(nn(m, high) + nn(m, low))
        return unused

    lax.fori_loop(0, LEVELS + 2, one, 0)
    ones = jnp.ones((ROWS, 256), bf16)
    return jnp.exp(tn(high, ones) + tn(low, ones))


def summaries(share_end, rows):
    return jnp.concatenate([tn(share_end, of(rows, h))[slots(h)] for h in range(HEADS)], axis=0)


def lower_scores(a_ref, share, decay_ref, masks_ref, total_ref, parts_ref=None):
    first = nn(masked(a_ref[...], masks_ref[LEVELS]), tall(share.astype(bf16)))
    total_ref[...] = first

    def one(level, unused):
        decay = decay_ref[level]
        part = decay * nn(
            masked(a_ref[...], masks_ref[level]), tall((decay * share).astype(bf16))
        )
        if parts_ref is not None:
            parts_ref[level] = part
        total_ref[...] += part
        return unused

    lax.fori_loop(0, LEVELS, one, 0)


def mixing(coefficient, share, decay_ref, masks_ref, out_ref):
    def pairs(x, f, mask):
        return masked(nt(x.astype(bf16), tall(f.astype(bf16))).astype(bf16), mask)

    out_ref[...] = pairs(coefficient, share, masks_ref[LEVELS])

    def one(level, unused):
        decay = decay_ref[level]
        out_ref[...] += pairs(coefficient * decay, decay * share, masks_ref[level])
        return unused

    lax.fori_loop(0, LEVELS, one, 0)


class Chain:
    def __init__(self, n_line, backward, in_ref, out_ref, send_sem, recv_sem):
        self.z = lax.axis_index("shard")
        self.turn = n_line - 1 - self.z if backward else self.z
        self.next = self.z - 1 if backward else self.z + 1
        self.n_line, self.in_ref, self.out_ref = n_line, in_ref, out_ref
        self.send_sem, self.recv_sem = send_sem, recv_sem

    def copy(self, part):
        half = (part // 2, pl.ds(128 * (part % 2), 128))
        return pltpu.make_async_remote_copy(
            src_ref=self.out_ref.at[half],
            dst_ref=self.in_ref.at[half],
            send_sem=self.send_sem.at[part],
            recv_sem=self.recv_sem.at[part],
            device_id={"dp": lax.axis_index("dp"), "shard": self.next},
            device_id_type=MESH,
        )

    def step(self, i, through, sums_ref):
        if i >= self.n_line:
            return

        @pl.when(self.turn == i)
        def _():
            for part in range(4):
                which, rows = part // 2, slice(128 * (part % 2), 128 * (part % 2) + 128)
                if i == 0:
                    self.in_ref[which, rows] = jnp.zeros((128, HEAD), bf16)
                    new = sums_ref[which, rows]
                else:
                    self.copy(part).wait_recv()
                    new = through[rows] * self.in_ref[which, rows].astype(f32) + sums_ref[which, rows]
                if i < self.n_line - 1:
                    self.out_ref[which, rows] = new.astype(bf16)
                    self.copy(part).start()

    def finish(self):
        @pl.when(self.turn < self.n_line - 1)
        def _():
            for part in range(4):
                self.copy(part).wait_send()


def chain_scratch():
    box = pltpu.VMEM((2, 256, HEAD), bf16)
    sem = pltpu.SemaphoreType.DMA((4,))
    return [box, box, sem, sem, pltpu.VMEM((2, 256, HEAD), f32)]


def sigmoid(x):
    return 1.0 / (1.0 + jnp.exp(-x))


def forward_kernel(pieces, n_ffn, n_square, n_line, *refs):
    (normed_ref, gate_ref, tokens_ref, hgain_ref, gain2_ref, sums_ref, masks_ref, w_in_ref, w_o_ref) = refs[:9]
    shards, refs = refs[9 : 9 + n_ffn], refs[9 + n_ffn :]
    (q_ref, k_ref, v_ref, swish_ref, mixed_ref, state_ref, scores_ref, gated_ref, hidden_ref, normed2_ref) = refs[:10]
    gathered, refs = refs[10 : 10 + n_ffn], refs[10 + n_ffn :]
    w_in, w_o, decay_ref, a_ref, b_ref, in_ref, out_ref, chain_send, chain_recv, part_ref, w_sem = refs[:11]
    job = Gather(pieces, shards, gathered, refs[11:], n_square, n_line)
    chain = Chain(n_line, False, in_ref, out_ref, chain_send, chain_recv)
    loads = {}
    for i in (1, 2, 0, 3):
        loads[i] = pltpu.make_async_copy(w_in_ref.at[:, pl.ds(D * i, D)], w_in.at[i], w_sem.at[i])
        loads[i].start()
    loads[4] = pltpu.make_async_copy(w_o_ref, w_o, w_sem.at[4])
    loads[4].start()
    job.load_own()
    barrier(job.p)
    job.start()
    tick = job.run
    tick(4)
    normed = normed_ref[...]

    def project(i):
        loads[i].wait()
        return nn(normed, w_in[i])

    log_gate = gate_ref[...]
    share = share_of(log_gate)
    through = decays(log_gate, sums_ref, decay_ref)
    share_end = (decay_ref[LEVELS + 1] * share).astype(bf16)
    k_ref[...] = project(1).astype(bf16)
    v_ref[...] = project(2).astype(bf16)
    tick(4)
    part_ref[0] = summaries(share_end, k_ref[...])
    part_ref[1] = summaries(share_end, v_ref[...])
    chain.step(0, through, part_ref)
    tick(4)
    q_ref[...] = project(0).astype(bf16)
    a_ref[...] = products(q_ref[...], k_ref[...])
    tick(4)
    chain.step(1, through, part_ref)
    swish_ref[...] = project(3)
    lower_scores(a_ref, share, decay_ref, masks_ref, scores_ref)
    tick(8)
    for i in range(2, n_line):
        chain.step(i, through, part_ref)
        tick(4)
    before = decay_ref[LEVELS]
    scores = scores_ref[...] + before * nt(q_ref[...], wide(in_ref[0]))
    scores_ref[...] = scores
    chance = softmax_slots(SCALE * scores)
    tick(4)
    mixing(chance, share, decay_ref, masks_ref, b_ref)
    tick(6)
    carried = nn((chance * before).astype(bf16), wide(in_ref[1]))
    state_ref[...] = in_ref[...]
    b, v = b_ref[...], v_ref[...]
    for h in range(HEADS):
        at = slice(HEAD * h, HEAD * (h + 1))
        mixed = nn(of(b, h), of(v, h)) + of(carried, h)
        mixed_ref[:, at] = mixed
        head_scale = lax.rsqrt(jnp.mean(mixed * mixed, axis=-1, keepdims=True) + norm_eps)
        swish = swish_ref[:, at]
        gated_ref[:, at] = (mixed * head_scale * hgain_ref[...] * (swish * sigmoid(swish))).astype(bf16)
    tick(6)
    loads[4].wait()
    hidden = tokens_ref[...].astype(f32) + nn(gated_ref[...], w_o[...])
    hidden_ref[...] = hidden
    scale2 = lax.rsqrt(jnp.mean(hidden * hidden, axis=-1, keepdims=True) + norm_eps)
    normed2_ref[...] = (hidden * scale2 * gain2_ref[...]).astype(bf16)
    job.finish()
    chain.finish()


VMEM_BLOCK = pl.BlockSpec(memory_space=pltpu.VMEM)
ANY_BLOCK = pl.BlockSpec(memory_space=pl.ANY)


def run_forward(normed, log_gate, tokens, hgain, gain2, sums, masks, w_in, w_o, shards, n_square, n_line, collective_id):
    rows = normed.shape[0]
    n = n_square * 2 * n_line
    shapes = [s.shape for s in shards]
    pieces = pieces_of(shapes, n_square)
    full = lambda dtype: jax.ShapeDtypeStruct((rows, D), dtype)
    pair = pltpu.VMEM((ROWS, HEADS * ROWS), bf16)
    return pl.pallas_call(
        functools.partial(forward_kernel, pieces, len(shards), n_square, n_line),
        out_shape=[full(bf16)] * 3
        + [full(f32)] * 2
        + [jax.ShapeDtypeStruct((2, 256, HEAD), bf16), jax.ShapeDtypeStruct((rows, 256), f32)]
        + [full(bf16), full(f32), full(bf16)]
        + [jax.ShapeDtypeStruct((n,) + s, bf16) for s in shapes],
        in_specs=[VMEM_BLOCK] * 7 + [ANY_BLOCK] * (2 + len(shards)),
        out_specs=[VMEM_BLOCK] * 10 + [ANY_BLOCK] * len(shards),
        scratch_shapes=[
            pltpu.VMEM((4, D, D), bf16),
            pltpu.VMEM((D, D), bf16),
            pltpu.VMEM((LEVELS + 2, ROWS, 256), f32),
            pair,
            pair,
        ]
        + chain_scratch()
        + [pltpu.SemaphoreType.DMA((5,))]
        + gather_sems(len(pieces), len(shards), n_square, n_line),
        compiler_params=pltpu.CompilerParams(
            collective_id=collective_id, has_side_effects=True, vmem_limit_bytes=60 << 20
        ),
        name="mixer_forward",
    )(normed, log_gate, tokens, hgain, gain2, sums, masks, w_in, w_o, *shards)


def backward_kernel(pieces, n_ffn, n_square, n_line, *refs):
    (
        gh_ref, swish_ref, mixed_ref, hgain_ref, q_ref, k_ref, v_ref, gate_ref, sums_ref, masks_ref, back_masks_ref,
        state_ref, scores_ref, w_o_ref,
    ) = refs[:14]
    partial, refs = refs[14 : 14 + n_ffn], refs[14 + n_ffn :]
    gqkvs_ref, branch_ref, dgate_ref, dhgain_ref = refs[:4]
    reduced, refs = refs[4 : 4 + n_ffn], refs[4 + n_ffn :]
    (
        w_o, decay_ref, a_ref, av_ref, at_ref, avt_ref, b_ref, bk_ref, s_parts, d_parts, s_sum, d_sum, shares_ref,
        g_ref, in_ref, out_ref, chain_send, chain_recv, part_ref, w_sem,
    ) = refs[:20]
    refs = refs[20:]
    m = len(pieces)
    job = ReduceFromHbm(
        pieces, partial, refs[:m], refs[m : 2 * m], refs[2 * m : 3 * m], refs[3 * m], refs[3 * m + 1 :], n_square, n_line
    )
    chain = Chain(n_line, True, in_ref, out_ref, chain_send, chain_recv)
    w_load = pltpu.make_async_copy(w_o_ref, w_o, w_sem)
    w_load.start()
    job.load()
    barrier(job.p)
    job.start()
    tick = job.run

    log_gate = gate_ref[...]
    share = share_of(log_gate)
    through = decays(log_gate, sums_ref, decay_ref)
    branch = gh_ref[...].astype(bf16)
    branch_ref[...] = branch
    w_load.wait()
    grad_gated = nt(branch, w_o[...]).astype(bf16)
    gain = hgain_ref[...]
    dhgain = jnp.zeros((1, HEAD), f32)
    for h in range(HEADS):
        at = slice(HEAD * h, HEAD * (h + 1))
        mixed, swish = mixed_ref[:, at], swish_ref[:, at]
        gg = of(grad_gated, h).astype(f32)
        sig = sigmoid(swish)
        head_scale = lax.rsqrt(jnp.mean(mixed * mixed, axis=-1, keepdims=True) + norm_eps)
        scaled = mixed * head_scale
        g_head = gg * (swish * sig)
        dhgain += jnp.sum(g_head * scaled, axis=0, keepdims=True)
        gqkvs_ref[:, 3 * D + HEAD * h : 3 * D + HEAD * (h + 1)] = (
            gg * (scaled * gain) * (sig * (1.0 + swish * (1.0 - sig)))
        ).astype(bf16)
        u = g_head * gain
        g_ref[:, at] = (
            head_scale * (u - scaled * (head_scale * jnp.mean(u * mixed, axis=-1, keepdims=True)))
        ).astype(bf16)
    dhgain_ref[...] = jnp.broadcast_to(dhgain, (8, HEAD))
    job.loaded()
    tick(2)
    q, k, v, g = q_ref[...], k_ref[...], v_ref[...], g_ref[...]
    before, after = decay_ref[LEVELS], decay_ref[LEVELS + 1]
    key_in, value_in = state_ref[0], state_ref[1]
    chance = softmax_slots(SCALE * scores_ref[...])
    av_ref[...] = products(g, v)
    lower_scores(av_ref, share, decay_ref, masks_ref, d_sum, d_parts)
    tick(2)
    d_state = before * nt(g, wide(value_in))
    slope = d_sum[...] + d_state
    spread = SCALE * chance * (slope - head_sums(chance * slope))
    chance_before = (chance * before).astype(bf16)
    spread_before = (spread * before).astype(bf16)
    part_ref[0] = summaries(spread_before, q)
    part_ref[1] = summaries(chance_before, g)
    chain.step(0, through, part_ref)
    tick(2)
    a_ref[...] = products(q, k)
    at_ref[...] = products(k, q)
    avt_ref[...] = products(v, g)
    lower_scores(a_ref, share, decay_ref, masks_ref, s_sum, s_parts)
    chain.step(1, through, part_ref)
    tick(2)
    s_state = before * nt(q, wide(key_in))
    mixing(chance, share, decay_ref, masks_ref, b_ref)
    chain.step(2, through, part_ref)
    tick(2)
    mixing(spread, share, decay_ref, masks_ref, bk_ref)
    for i in range(3, n_line):
        chain.step(i, through, part_ref)
        tick(2)
    dgate_ref[...] = tn(sums_ref[LEVELS], (spread * s_state + chance * d_state).astype(bf16))
    diagonal = back_masks_ref[LEVELS]
    shares_ref[...] = nn(masked(at_ref[...], diagonal), tall(spread.astype(bf16))) + nn(
        masked(avt_ref[...], diagonal), tall(chance.astype(bf16))
    )

    def one(level, unused):
        decay = decay_ref[level]
        mask = back_masks_ref[level]
        taken = decay * (
            nn(masked(at_ref[...], mask), tall((spread * decay).astype(bf16)))
            + nn(masked(avt_ref[...], mask), tall((chance * decay).astype(bf16)))
        )
        shares_ref[...] += taken
        given = spread * s_parts[level] + chance * d_parts[level]
        place = lax.broadcasted_iota(jnp.int32, (ROWS, 256), 0)
        upper = lax.bitwise_and(lax.shift_right_logical(place, level), 1) == 1
        both = jnp.where(upper, given, taken * share).astype(bf16)
        dgate_ref[...] += tn(sums_ref[level], both)
        return unused

    lax.fori_loop(0, LEVELS, one, 0)
    tick(2)
    out_key, out_value = in_ref[0], in_ref[1]
    wide_key, wide_value = wide(out_key), wide(out_value)
    taken = after * (nt(k, wide_key) + nt(v, wide_value))
    shares = shares_ref[...] + taken
    kept = key_in.astype(f32) * out_key.astype(f32) + value_in.astype(f32) * out_value.astype(f32)
    high, low = split_low(kept * through)
    ones = jnp.ones((8, 256), bf16)
    kept_row = (nt(ones, high) + nt(ones, low))[:1]
    dgate = dgate_ref[...] + tn(sums_ref[LEVELS + 1], (taken * share).astype(bf16)) + kept_row
    dgate_ref[...] = dgate - jnp.exp(log_gate) * shares
    tick(2)
    end = (after * share).astype(bf16)
    q_state = nn(spread_before, wide(key_in))
    k_state = nn(end, wide_key)
    v_state = nn(end, wide_value)
    b, bk = b_ref[...], bk_ref[...]
    for h in range(HEADS):
        low_at = HEAD * h
        gqkvs_ref[:, low_at : low_at + HEAD] = (nn(of(bk, h), of(k, h)) + of(q_state, h)).astype(bf16)
        gqkvs_ref[:, D + low_at : D + low_at + HEAD] = (tn(of(bk, h), of(q, h)) + of(k_state, h)).astype(bf16)
        gqkvs_ref[:, 2 * D + low_at : 2 * D + low_at + HEAD] = (tn(of(b, h), of(g, h)) + of(v_state, h)).astype(bf16)
    job.finish(reduced)
    chain.finish()


def run_backward(
    grad_hidden, swish_pre, mixed, hgain, q, k, v, log_gate, sums, masks, back_masks, state, scores, w_o, partial,
    n_square, n_line, collective_id,
):
    rows = q.shape[0]
    shapes = [a.shape[1:] for a in partial]
    pieces = pieces_of(shapes, n_square)
    views = [a.reshape((n_square, 2, n_line) + s) for a, s in zip(partial, shapes)]
    boxes = reduce_boxes(pieces, shapes, [a.dtype for a in partial], n_square, n_line)
    pair = pltpu.VMEM((ROWS, HEADS * ROWS), bf16)
    parts = pltpu.VMEM((LEVELS, ROWS, 256), f32)
    flat = pltpu.VMEM((ROWS, 256), f32)
    return pl.pallas_call(
        functools.partial(backward_kernel, pieces, len(partial), n_square, n_line),
        out_shape=[
            jax.ShapeDtypeStruct((rows, 4 * D), bf16),
            jax.ShapeDtypeStruct((rows, D), bf16),
            jax.ShapeDtypeStruct((rows, 256), f32),
            jax.ShapeDtypeStruct((8, HEAD), f32),
        ]
        + [jax.ShapeDtypeStruct(s, f32) for s in shapes],
        in_specs=[VMEM_BLOCK] * 13 + [ANY_BLOCK] * (1 + len(partial)),
        out_specs=[VMEM_BLOCK] * (4 + len(partial)),
        scratch_shapes=[pltpu.VMEM((D, D), bf16), pltpu.VMEM((LEVELS + 2, ROWS, 256), f32)]
        + [pair] * 6
        + [parts, parts, flat, flat, flat, pltpu.VMEM((ROWS, D), bf16)]
        + chain_scratch()
        + [pltpu.SemaphoreType.DMA]
        + boxes * 3
        + [pltpu.SemaphoreType.DMA((len(pieces),))]
        + reduce_sems(len(pieces), n_square, n_line),
        compiler_params=pltpu.CompilerParams(
            collective_id=collective_id, has_side_effects=True, vmem_limit_bytes=62 << 20
        ),
        name="mixer_backward",
    )(grad_hidden, swish_pre, mixed, hgain, q, k, v, log_gate, sums, masks, back_masks, state, scores, w_o, *views)


def gradients_kernel(n_square, n_line, pieces, small_pieces, *refs):
    (normed_ref, gqkvs_ref, gated_ref, branch_ref, base_ref, gnlow_ref, gh_ref, tokens_ref, gain1_ref, w_in_ref) = refs[:10]
    in_out, out_out, small_out, dtok_ref = refs[10:14]
    refs = refs[14:]
    w_in, w_sem = refs[:2]
    refs = refs[2:]
    m = len(pieces)
    dw, peer_part, landed, refs = refs[:m], refs[m : 2 * m], refs[2 * m : 3 * m], refs[3 * m :]
    sems, refs = refs[:4], refs[4:]
    small_dw, small_peer, small_landed, small_sems = refs[0:1], refs[1:2], refs[2:3], refs[3:7]
    p = Place(n_square, n_line)

    def make(ps, boxes, peers, lands, ss):
        return Reduce(
            ps,
            lambda q, a, z: boxes[q].at[a, p.c, z],
            lambda q, k: boxes[q].at[:, 1 - p.c, flip(p.z, k)],
            peers, lands, ss, n_square, n_line,
        )

    job = make(pieces, dw, peer_part, landed, sems)
    small = make(small_pieces, small_dw, small_peer, small_landed, small_sems)
    load = pltpu.make_async_copy(w_in_ref, w_in, w_sem)
    load.start()
    barrier(p)
    normed = normed_ref[...]
    shape = (n_square, 2, n_line, D // (n_square * 2 * n_line))

    def weight(left, right):
        out = tn(left, right).astype(bf16)
        return out.reshape(shape + (out.shape[1],))

    for q in range(2):
        for part in range(2):
            at = (2 * q + part) * D
            dw[q][:, :, :, :, part * D : (part + 1) * D] = weight(normed, gqkvs_ref[:, at : at + D])
        job.start([q])
    for q in range(2):
        dw[2 + q][...] = weight(gated_ref[...], branch_ref[:, q * 512 : (q + 1) * 512])
        job.start([2 + q])
    job.run(2)
    load.wait()
    g = gnlow_ref[...]
    for i in range(4):
        g = g + nt(gqkvs_ref[:, i * D : (i + 1) * D], w_in[:, i * D : (i + 1) * D])
        job.run(1)
    x = tokens_ref[...].astype(f32)
    scale1 = lax.rsqrt(jnp.mean(x * x, axis=-1, keepdims=True) + norm_eps)
    u = g * gain1_ref[...]
    dtok_ref[...] = (
        gh_ref[...] + scale1 * u - x * (scale1 * scale1 * scale1 * jnp.mean(u * x, axis=-1, keepdims=True))
    )
    high, low = split_low(g * x * scale1)
    ones = jnp.ones((ROWS, 128), bf16)
    column = tn(high, ones) + tn(low, ones)
    lane = lax.broadcasted_iota(jnp.int32, (D, 128), 1)
    small_dw[0][...] = (base_ref[...] + jnp.where(lane == GAIN1_LANE, column, 0.0)).reshape(shape + (128,))
    small.start()
    while job.todo:
        job.run(4)
        small.run(1)
    small.finish([small_out])
    job.finish([in_out, out_out])


GAIN1_LANE = 34


def run_gradients(
    normed, gqkvs, gated, branch, base, gnlow, grad_hidden, tokens, gain1, w_in, n_square, n_line, collective_id
):
    n = n_square * 2 * n_line
    r = D // n
    rows = normed.shape[0]
    shapes = [(r, 4 * D), (r, D)]
    pieces = pieces_of(shapes, n_square)
    small_pieces = pieces_of([(r, 128)], n_square)
    widths = [w for i, s, w, b in pieces]
    dw = [pltpu.VMEM((n_square, 2, n_line, r, w), bf16) for w in widths]
    boxes = reduce_boxes(pieces, shapes, [bf16, bf16], n_square, n_line)
    small_box = pltpu.VMEM((n_square, n_line, r, 128), f32)
    return pl.pallas_call(
        functools.partial(gradients_kernel, n_square, n_line, pieces, small_pieces),
        out_shape=[
            jax.ShapeDtypeStruct((r, 4 * D), f32),
            jax.ShapeDtypeStruct((r, D), f32),
            jax.ShapeDtypeStruct((r, 128), f32),
            jax.ShapeDtypeStruct((rows, D), f32),
        ],
        in_specs=[VMEM_BLOCK] * 9 + [ANY_BLOCK],
        out_specs=[VMEM_BLOCK] * 4,
        scratch_shapes=[pltpu.VMEM((D, 4 * D), bf16), pltpu.SemaphoreType.DMA]
        + dw
        + boxes * 2
        + reduce_sems(len(pieces), n_square, n_line)
        + [pltpu.VMEM((n_square, 2, n_line, r, 128), f32), small_box, small_box]
        + reduce_sems(1, n_square, n_line),
        compiler_params=pltpu.CompilerParams(
            collective_id=collective_id, has_side_effects=True, vmem_limit_bytes=62 << 20
        ),
        name="weight_gradients",
    )(normed, gqkvs, gated, branch, base, gnlow, grad_hidden, tokens, gain1, w_in)


def silu_slope(value):
    sig = jax.nn.sigmoid(value)
    return sig * (1.0 + value * (1.0 - sig))


def pack_small(low, up, bias, hgain, gain1, gain2, dtype):
    n, rows = low.shape[0], low.shape[1]
    fill = lambda a: jnp.pad(a.astype(dtype), ((0, 0), (0, rows - a.shape[1]), (0, 0)))
    parts = [fill(low), fill(up)] + [fill(a[:, :, None]) for a in (bias, hgain, gain1, gain2)]
    out = jnp.concatenate(parts, axis=2)
    return jnp.pad(out, ((0, 0), (0, 0), (0, 128 - out.shape[2])))


def unpack_small(packed):
    n, rows = packed.shape[0], packed.shape[1]
    few = rows // 4
    low = packed[:, :, :16].reshape(n * rows, 16)
    up = packed[:, :few, 16:32].reshape(n * few, 16)
    bias, hgain = (packed[:, :few, lane].reshape(n * few) for lane in (32, 33))
    gain1, gain2 = (packed[:, :, lane].reshape(n * rows) for lane in (34, 35))
    return low, up, bias, hgain, gain1, gain2


def per_device(
    n_square, n_line,
    tokens, cotangent, lengths, norm1_gain, w_query, w_key, w_value, w_gate_low, w_gate_up,
    gate_bias, head_gain, w_swish, w_out, norm2_gain, w_ffn_gate, w_ffn_up, w_ffn_down,
):
    count = tokens.shape[0]
    n = n_square * 2 * n_line
    small = pack_small(
        *(a[None] for a in (w_gate_low, w_gate_up, gate_bias, head_gain, norm1_gain, norm2_gain)), bf16
    )[0]
    mixer_in = jnp.concatenate([w_query, w_key, w_value, w_swish], axis=1)
    ffn_in = jnp.concatenate([w_ffn_gate, w_ffn_up], axis=1)
    got = gather([mixer_in, w_out, small], n_square, n_line, 1)
    w_in = got[0].reshape(D, 4 * D)
    w_o = got[1].reshape(D, D)
    low_w, up_w, bias, hgain, gain1, gain2 = unpack_small(got[2])
    bias, hgain, gain1, gain2 = (x.astype(f32) for x in (bias, hgain, gain1, gain2))
    sums, masks = level_constants(count)
    back_masks = np.ascontiguousarray(np.swapaxes(masks, 1, 2))

    position = lax.axis_index("shard") * count + jnp.arange(count, dtype=jnp.int32)
    valid = (position < lengths[0]).astype(f32)[:, None]
    resid = tokens.astype(f32)
    scale1 = lax.rsqrt(jnp.mean(resid * resid, axis=-1, keepdims=True) + norm_eps)
    normed = (resid * scale1 * gain1).astype(bf16)
    low_rank = nn(normed, low_w).astype(bf16)
    logits = nt(low_rank, up_w) + bias
    log_gate = jax.nn.log_sigmoid(logits) / gate_norm
    q, k, v, swish_pre, mixed, state, scores, gated, hidden, normed2, g_gu, g_d = run_forward(
        normed, log_gate, tokens, hgain[None], gain2[None], sums, masks, w_in, w_o, [ffn_in, w_ffn_down], n_square, n_line, 2
    )
    w_gu = g_gu.reshape(D, -1)
    w_d = g_d.reshape(-1, D)
    ff = w_d.shape[0]
    gu = nn(normed2, w_gu)
    gate_pre, up_pre = gu[:, :ff], gu[:, ff:]
    inner = (jax.nn.silu(gate_pre) * up_pre).astype(bf16)
    output = (valid * (hidden + nn(inner, w_d))).astype(bf16)

    grad_out = cotangent.astype(f32) * valid
    grad_low = grad_out.astype(bf16)
    d_down = tn(inner, grad_low).astype(bf16)
    grad_inner = nt(grad_low, w_d).astype(bf16).astype(f32)
    grad_gate = (grad_inner * up_pre * silu_slope(gate_pre)).astype(bf16)
    grad_up = (grad_inner * jax.nn.silu(gate_pre)).astype(bf16)
    grad_gu = jnp.concatenate([grad_gate, grad_up], axis=1)
    d_gu = tn(normed2, grad_gu).astype(bf16)
    grad_normed2 = nt(grad_gu, w_gu)
    scale2 = lax.rsqrt(jnp.mean(hidden * hidden, axis=-1, keepdims=True) + norm_eps)
    d_gain2 = jnp.sum(grad_normed2 * hidden * scale2, axis=0)
    spread2 = grad_normed2 * gain2
    grad_hidden = (
        grad_out
        + scale2 * spread2
        - hidden * scale2**3 * jnp.mean(spread2 * hidden, axis=-1, keepdims=True)
    )
    gqkvs, branch, grad_log, d_hgain, s_gu, s_down = run_backward(
        grad_hidden, swish_pre, mixed, hgain[None], q, k, v, log_gate, sums, masks, back_masks, state, scores, w_o,
        [d_gu.reshape(n, D // n, -1), d_down.reshape(n, ff // n, D)], n_square, n_line, 3,
    )
    grad_logits = grad_log / gate_norm * jax.nn.sigmoid(-logits)
    d_bias = jnp.sum(grad_logits, axis=0)
    logits_high, logits_low = split_low(grad_logits)
    d_up = tn(logits_high, low_rank) + tn(logits_low, low_rank)
    grad_lowrank = (nn(logits_high, up_w) + nn(logits_low, up_w)).astype(bf16)
    d_low = tn(normed, grad_lowrank)
    base = pack_small(
        d_low.reshape(n, -1, 16), d_up.reshape(n, -1, 16), d_bias.reshape(n, -1), d_hgain[0].reshape(n, -1),
        jnp.zeros((n, D // n), f32), d_gain2.reshape(n, -1), f32,
    ).reshape(D, 128)
    s_in, s_out, s_small, d_tokens = run_gradients(
        normed, gqkvs, gated, branch, base, nt(grad_lowrank, low_w), grad_hidden, tokens, gain1[None], w_in,
        n_square, n_line, 4,
    )
    o_low, o_up, o_bias, o_hgain, o_gain1, o_gain2 = unpack_small(s_small[None])
    return (
        output, d_tokens, o_gain1,
        s_in[:, :D], s_in[:, D : 2 * D], s_in[:, 2 * D : 3 * D],
        o_low, o_up, o_bias, o_hgain,
        s_in[:, 3 * D :], s_out, o_gain2,
        s_gu[:, :ff], s_gu[:, ff:], s_down,
    )


def solution(mesh):
    rows, row = P(("dp", "shard"), None), P(("dp", "shard"))
    placed = (rows, rows, P("dp"), row, rows, rows, rows, rows, rows, row, row, rows, rows, row, rows, rows, rows)
    out = (rows, rows, row, rows, rows, rows, rows, rows, row, row, rows, rows, row, rows, rows, rows)
    return jax.shard_map(
        functools.partial(per_device, mesh.shape["dp"] // 2, mesh.shape["shard"]),
        mesh=mesh,
        in_specs=placed,
        out_specs=out,
        check_vma=False,
    )
```

```python
import functools

import jax
import jax.numpy as jnp
import numpy as np
from jax import lax
from jax.experimental import pallas as pl
from jax.experimental.pallas import tpu as pltpu
from jax.sharding import PartitionSpec as P

D = 1024
HEADS = 4
HEAD = 256
SLOTS = 64
norm_eps = 1e-06
gate_norm = 8.0
MESH = pl.DeviceIdType.MESH


class Place:
    def __init__(self, n_square, n_line):
        self.n_square, self.n_line = n_square, n_line
        dp = lax.axis_index("dp")
        self.z = lax.axis_index("shard")
        self.c = lax.rem(dp, 2)
        self.a = lax.div(dp, 2)

    def slot(self, k):
        out = 0
        for z in range(self.n_line):
            near = sorted(range(self.n_line), key=lambda other: (abs(other - z), other))
            out = out + jnp.where(self.z == z, near[k], 0)
        return out

    def device(self, a, c, z):
        return {"dp": a * 2 + c, "shard": z}

    def slab(self, a, c, z):
        return (a * 2 + c) * self.n_line + z


def flip(value, bits):
    for b in range(8):
        if bits >> b & 1:
            digit = lax.rem(lax.div(value, 1 << b), 2)
            value = value + (1 - 2 * digit) * (1 << b)
    return value


LINE = "line"
LATE_LINE = 3.5


class Tree:
    def __init__(self, order, n_line):
        self.slabs = [(0, 0)]
        self.up, self.down, self.time = {}, {(0, 0): []}, {(0, 0): 0}
        late = order[0] != LINE
        for stage, dim in enumerate(order):
            for m, k in list(self.slabs):
                steps = range(1, n_line) if dim == LINE else [dim]
                for step in steps:
                    child = (m, step) if dim == LINE else (m ^ step, k)
                    self.slabs.append(child)
                    self.up[child] = (dim, step, (m, k))
                    self.down[child] = []
                    self.down[(m, k)].append(child)
                    if dim == LINE:
                        self.time[child] = step + (n_line + 1 if late else 0)
                    else:
                        self.time[child] = self.time[(m, k)] + 1


def orders(n_square):
    bits = [1 << b for b in range((n_square - 1).bit_length())]
    return {"a": (LINE, *bits), "b": (LINE, *bits[::-1]), "c": (*bits[::-1], LINE)}


def split_pieces(plan, n_square):
    by_name = orders(n_square)
    return [(i, start, width, by_name[name]) for i, start, width, name in plan]


MIXER_PLAN = [
    (0, 0, 1024, "a"), (1, 0, 1024, "b"), (2, 0, 1024, "a"), (3, 0, 1024, "b"), (4, 512, 512, "a"), (4, 0, 512, "c"),
]
FFN_PLAN = [(0, 0, 2816, "a"), (1, 0, 2816, "b"), (2, 0, 384, "a"), (2, 384, 384, "b"), (2, 768, 256, "c")]


def barrier(place):
    sem = pltpu.get_barrier_semaphore()
    peers = [place.device(place.a, 1 - place.c, place.z)]
    bit = 1
    while bit < place.n_square:
        peers.append(place.device(flip(place.a, bit), place.c, place.z))
        bit *= 2
    for k in range(1, place.n_line):
        peers.append(place.device(place.a, place.c, flip(place.z, k)))
    for peer in peers:
        pl.semaphore_signal(sem, inc=1, device_id=peer, device_id_type=MESH)
    pl.semaphore_wait(sem, len(peers))


class Gather:
    def __init__(self, pieces, ins, outs, sems, n_square, n_line):
        self.pieces, self.ins, self.outs = pieces, ins, outs
        self.local_sem, self.net_send, self.net_recv, self.core_send, self.core_recv, self.line_send = sems
        self.n_square, self.n_line = n_square, n_line
        self.p = Place(n_square, n_line)
        self.own = [
            pltpu.make_async_copy(
                ins[i], outs[i].at[self.p.slab(self.p.a, self.p.c, self.p.z)], self.local_sem.at[i]
            )
            for i in range(len(ins))
        ]
        self.trees = [Tree(order, n_line) for i, start, width, order in pieces]
        events = [(tree.time[slab], q, slab, False) for q, tree in enumerate(self.trees) for slab in tree.slabs]
        for q, tree in enumerate(self.trees):
            if pieces[q][3][0] != LINE:
                events += [(LATE_LINE + 0.1 * j, q, slab, True) for j, slab in enumerate(tree.slabs) if slab[1] == 0]
        self.todo = sorted(events, key=lambda e: e[0])
        self.started = []
        self.places = [self.p.slot(k) for k in range(n_line)]

    def at(self, q, m, k, c=None):
        i, start, width, order = self.pieces[q]
        p = self.p
        z = self.places[k] if order[0] == LINE else flip(p.z, k)
        s = p.slab(flip(p.a, m), p.c if c is None else c, z)
        return self.outs[i].at[s, :, pl.ds(start, width)]

    def source(self, q, m, k):
        if m == 0 and k == 0:
            i, start, width, _ = self.pieces[q]
            return self.ins[i].at[:, pl.ds(start, width)]
        return self.at(q, m, k)

    def go(self, q, m, k, sems, index, peer):
        copy = pltpu.make_async_remote_copy(
            src_ref=self.source(q, m, k),
            dst_ref=self.at(q, m, k),
            send_sem=sems[0].at[index],
            recv_sem=sems[1].at[index],
            device_id=peer,
            device_id_type=MESH,
        )
        copy.start()
        self.started.append((None, copy))

    def along(self, q, k):
        p = self.p
        z = self.places[k]
        for way, (step, more) in enumerate(((1, (z <= p.z) & (p.z < self.n_line - 1)), (-1, (z >= p.z) & (p.z > 0)))):
            copy = pltpu.make_async_remote_copy(
                src_ref=self.source(q, 0, k),
                dst_ref=self.at(q, 0, k),
                send_sem=self.line_send.at[q, way, k],
                recv_sem=self.net_recv.at[q, 0, z],
                device_id=p.device(p.a, p.c, p.z + step),
                device_id_type=MESH,
            )
            pl.when(more)(copy.start)
            self.started.append((more, copy))

    def arrived(self, q, m, k, sems, c, place=None):
        p = self.p
        pltpu.make_async_remote_copy(
            src_ref=self.at(q, m, k, c),
            dst_ref=self.at(q, m, k, c),
            send_sem=sems[0].at[q, m, k],
            recv_sem=sems[1].at[q, m, k if place is None else place],
            device_id=p.device(p.a, 1 - p.c, p.z),
            device_id_type=MESH,
        ).wait_recv()

    def load_own(self):
        for copy in self.own:
            copy.start()

    def start(self):
        for q, tree in enumerate(self.trees):
            if self.pieces[q][3][0] == LINE:
                self.along(q, 0)

    def pass_on(self, q, slab, child):
        p = self.p
        dim, step, _ = self.trees[q].up[child]
        peer = p.device(p.a, p.c, flip(p.z, step)) if dim == LINE else p.device(flip(p.a, step), p.c, p.z)
        self.go(q, *slab, (self.net_send, self.net_recv), (q, *child), peer)

    def until(self, time):
        self.run(sum(e[0] <= time for e in self.todo))

    def run(self, n):
        p = self.p
        net, core = (self.net_send, self.net_recv), (self.core_send, self.core_recv)
        for time, q, slab, line in self.todo[:n]:
            tree = self.trees[q]
            first = self.pieces[q][3][0] == LINE
            if line:
                for child in tree.down[slab]:
                    if tree.up[child][0] == LINE:
                        self.pass_on(q, slab, child)
                continue
            if slab != (0, 0):
                lined = first and slab[0] == 0
                self.arrived(q, *slab, net, p.c, self.places[slab[1]] if lined else None)
                if lined:
                    self.along(q, slab[1])
            for child in tree.down[slab]:
                if tree.up[child][0] != LINE:
                    self.pass_on(q, slab, child)
            self.go(q, *slab, core, (q, *slab), p.device(p.a, 1 - p.c, p.z))
        self.todo = self.todo[n:]

    def finish(self):
        self.run(len(self.todo))
        for copy in self.own:
            copy.wait()
        for k in range(self.n_line):
            for q in range(len(self.pieces)):
                for m in range(self.n_square):
                    self.arrived(q, m, k, (self.core_send, self.core_recv), 1 - self.p.c)
        for more, copy in self.started:
            if more is None:
                copy.wait_send()
            else:
                pl.when(more)(copy.wait_send)


def gather_body(pieces, n_arrays, n_square, n_line, *refs):
    job = Gather(pieces, refs[:n_arrays], refs[n_arrays : 2 * n_arrays], refs[2 * n_arrays :], n_square, n_line)
    job.load_own()
    barrier(job.p)
    job.start()
    job.finish()


def gather_sems(n_pieces, n_arrays, n_square, n_line):
    sem = pltpu.SemaphoreType.DMA((n_pieces, n_square, n_line))
    line = pltpu.SemaphoreType.DMA((n_pieces, 2, n_line))
    return [pltpu.SemaphoreType.DMA((n_arrays,)), sem, sem, sem, sem, line]


def gather(arrays, plan, n_square, n_line, collective_id):
    shapes = [a.shape for a in arrays]
    pieces = split_pieces(plan, n_square)
    n = n_square * 2 * n_line
    any_space = pl.BlockSpec(memory_space=pl.ANY)
    return pl.pallas_call(
        functools.partial(gather_body, pieces, len(arrays), n_square, n_line),
        out_shape=[jax.ShapeDtypeStruct((n,) + s, a.dtype) for a, s in zip(arrays, shapes)],
        in_specs=[any_space] * len(arrays),
        out_specs=[pl.BlockSpec(memory_space=pl.ANY)] * len(arrays),
        scratch_shapes=gather_sems(len(pieces), len(arrays), n_square, n_line),
        compiler_params=pltpu.CompilerParams(collective_id=collective_id, has_side_effects=True),
        name="gather_weights",
    )(*arrays)


def add_into(ref, other):
    ref[...] = ref[...] + other[...]


class Reduce:
    def __init__(self, pieces, mine, theirs, peer_part, landed, sems, n_square, n_line):
        self.pieces, self.mine, self.theirs = pieces, mine, theirs
        self.peer_part, self.landed = peer_part, landed
        self.net_send, self.net_recv, self.core_send, self.core_recv = sems
        self.n_square, self.n_line = n_square, n_line
        self.p = Place(n_square, n_line)
        self.ks = list(range(n_line))[::-1]
        self.trees = [Tree(order, n_line) for i, start, width, order in pieces]
        events = [
            (-tree.time[slab], q, slab)
            for q, tree in enumerate(self.trees)
            for slab in tree.slabs[::-1]
        ]
        self.todo = sorted((e for e in events if e[2] != (0, 0)), key=lambda e: e[0])
        self.sent, self.have = [], set()

    def core(self, q, k):
        p = self.p
        return pltpu.make_async_remote_copy(
            src_ref=self.theirs(q, k),
            dst_ref=self.peer_part[q].at[:, flip(p.z, k)],
            send_sem=self.core_send.at[q, k],
            recv_sem=self.core_recv.at[q, k],
            device_id=p.device(p.a, 1 - p.c, p.z),
            device_id_type=MESH,
        )

    def net(self, q, slab):
        p = self.p
        m, k = slab
        dim, step, _ = self.trees[q].up[slab]
        peer = p.device(p.a, p.c, flip(p.z, step)) if dim == LINE else p.device(flip(p.a, step), p.c, p.z)
        return pltpu.make_async_remote_copy(
            src_ref=self.mine(q, flip(p.a, m), flip(p.z, k)),
            dst_ref=self.landed[q].at[m, k],
            send_sem=self.net_send.at[q, m, k],
            recv_sem=self.net_recv.at[q, m, k],
            device_id=peer,
            device_id_type=MESH,
        )

    def start(self, pieces=None):
        for q in range(len(self.pieces)) if pieces is None else pieces:
            for k in self.ks[:1] if self.pieces[q][3][0] == LINE else self.ks:
                self.core(q, k).start()

    def from_core(self, q, k):
        if (q, k) not in self.have:
            self.have.add((q, k))
            self.core(q, k).wait_recv()
            if k and self.pieces[q][3][0] == LINE:
                self.core(q, k - 1).start()

    def until(self, time):
        self.run(sum(e[0] <= time for e in self.todo))

    def run(self, n, pieces=None):
        p = self.p
        now = [e for e in self.todo if pieces is None or e[1] in pieces][:n]
        self.todo = [e for e in self.todo if e not in now]
        for time, q, slab in now:
            m, k = slab
            self.from_core(q, k)
            a, z = flip(p.a, m), flip(p.z, k)
            add_into(self.mine(q, a, z), self.peer_part[q].at[a, z])
            for child in self.trees[q].down[slab]:
                self.net(q, child).wait_recv()
                add_into(self.mine(q, a, z), self.landed[q].at[child])
            copy = self.net(q, slab)
            copy.start()
            self.sent.append(copy)

    def finish(self, outs):
        self.run(len(self.todo))
        p = self.p
        for q in range(len(self.pieces)):
            i, start, width, _ = self.pieces[q]
            self.from_core(q, 0)
            total = self.mine(q, p.a, p.z)[...].astype(jnp.float32)
            total = total + self.peer_part[q][p.a, p.z].astype(jnp.float32)
            for child in self.trees[q].down[(0, 0)]:
                self.net(q, child).wait_recv()
                total = total + self.landed[q][child].astype(jnp.float32)
            outs[i][:, pl.ds(start, width)] = total
        for copy in self.sent:
            copy.wait_send()
        for k in self.ks:
            for q in range(len(self.pieces)):
                self.core(q, k).wait_send()


def reduce_boxes(pieces, shapes, dtypes, n_square, n_line):
    return [
        pltpu.VMEM((n_square, n_line, shapes[i][0], width), dtypes[i]) for i, start, width, _ in pieces
    ]


def reduce_sems(n_pieces, n_square, n_line):
    sem = pltpu.SemaphoreType.DMA((n_pieces, n_square, n_line))
    core_sem = pltpu.SemaphoreType.DMA((n_pieces, n_line))
    return [sem, sem, core_sem, core_sem]


class ReduceFromHbm(Reduce):
    def __init__(self, pieces, ins, mine, peer_part, landed, local_sem, sems, n_square, n_line):
        p = Place(n_square, n_line)

        def columns(q):
            i, start, width, _ = pieces[q]
            return ins[i], pl.ds(start, width)

        def theirs(q, k):
            ref, cols = columns(q)
            return ref.at[:, 1 - p.c, flip(p.z, k), :, cols]

        super().__init__(pieces, lambda q, a, z: mine[q].at[a, z], theirs, peer_part, landed, sems, n_square, n_line)
        self.loads = []
        for q in range(len(pieces)):
            ref, cols = columns(q)
            self.loads.append(pltpu.make_async_copy(ref.at[:, p.c, :, :, cols], mine[q], local_sem.at[q]))

    def load(self):
        for copy in self.loads:
            copy.start()

    def loaded(self):
        for copy in self.loads:
            copy.wait()


def reduce_body(pieces, n_arrays, n_square, n_line, *refs):
    n = len(pieces)
    ins, outs, rest = refs[:n_arrays], refs[n_arrays : 2 * n_arrays], refs[2 * n_arrays :]
    job = ReduceFromHbm(
        pieces, ins, rest[:n], rest[n : 2 * n], rest[2 * n : 3 * n], rest[3 * n], rest[3 * n + 1 :], n_square, n_line
    )
    job.load()
    barrier(job.p)
    job.start()
    job.loaded()
    job.finish(outs)


def reduce_scatter(arrays, plan, n_square, n_line, collective_id):
    shapes = [a.shape[1:] for a in arrays]
    pieces = split_pieces(plan, n_square)
    views = [a.reshape((n_square, 2, n_line) + s) for a, s in zip(arrays, shapes)]
    any_space = pl.BlockSpec(memory_space=pl.ANY)
    boxes = reduce_boxes(pieces, shapes, [x.dtype for x in arrays], n_square, n_line)
    return pl.pallas_call(
        functools.partial(reduce_body, pieces, len(arrays), n_square, n_line),
        out_shape=[jax.ShapeDtypeStruct(s, jnp.float32) for s in shapes],
        in_specs=[any_space] * len(arrays),
        out_specs=[pl.BlockSpec(memory_space=pltpu.VMEM)] * len(arrays),
        scratch_shapes=boxes * 3
        + [pltpu.SemaphoreType.DMA((len(pieces),))]
        + reduce_sems(len(pieces), n_square, n_line),
        compiler_params=pltpu.CompilerParams(
            collective_id=collective_id, has_side_effects=True, vmem_limit_bytes=60 << 20
        ),
        name="reduce_grads",
    )(*views)


f32, bf16 = jnp.float32, jnp.bfloat16
ROWS = 256
LEVELS = 8


def level_constants(rows):
    t, i = np.arange(rows)[:, None], np.arange(rows)[None, :]
    sums, masks = [], []
    for level in range((rows - 1).bit_length()):
        same = (t >> (level + 1)) == (i >> (level + 1))
        upper_t, upper_i = (t >> level) & 1, (i >> level) & 1
        sums.append(
            (same & (upper_t == 1) & (upper_i == 1) & (i <= t))
            | (same & (upper_t == 0) & (upper_i == 0) & (i > t))
        )
        masks.append((t > i) & (((t ^ i) >> level) == 1))
    sums += [i <= t, i > t]
    masks.append(t == i)
    return np.stack(sums).astype(bf16), np.stack(masks).astype(bf16)


def nn(a, b):
    return lax.dot_general(a, b, (((1,), (0,)), ((), ())), preferred_element_type=f32)


def nt(a, b):
    return lax.dot_general(a, b, (((1,), (1,)), ((), ())), preferred_element_type=f32)


def tn(a, b):
    return lax.dot_general(a, b, (((0,), (0,)), ((), ())), preferred_element_type=f32)


def split_low(x):
    high = x.astype(bf16)
    return high, (x - high.astype(f32)).astype(bf16)


def head_of_lane(shape):
    return lax.broadcasted_iota(jnp.int32, shape, 1) // SLOTS


def tall(x):
    head = head_of_lane(x.shape)
    zero = jnp.zeros_like(x)
    return jnp.concatenate([jnp.where(head == h, x, zero) for h in range(HEADS)], axis=0)


def wide(state):
    head = lax.broadcasted_iota(jnp.int32, state.shape, 0) // SLOTS
    zero = jnp.zeros_like(state)
    return jnp.concatenate([jnp.where(head == h, state, zero) for h in range(HEADS)], axis=1)


def of(x, h):
    return x[:, HEAD * h : HEAD * (h + 1)]


def slots(h):
    return slice(SLOTS * h, SLOTS * (h + 1))


def products(a, b):
    return jnp.concatenate([nt(of(a, h), of(b, h)) for h in range(HEADS)], axis=1).astype(bf16)


def masked(a, mask):
    return a * jnp.concatenate([mask] * HEADS, axis=1)


def share_of(log_gate):
    small = -log_gate * (1.0 + log_gate * (0.5 + log_gate * (1.0 / 6.0)))
    return jnp.where(log_gate > -0.01, small, 1.0 - jnp.exp(log_gate))


def head_sums(x):
    ones = (head_of_lane((256, 256)) == lax.broadcasted_iota(jnp.int32, (256, 256), 0) // SLOTS)
    ones = jnp.where(ones, 1.0, 0.0).astype(bf16)
    high, low = split_low(x)
    return nn(high, ones) + nn(low, ones)


SCALE = 1.5 * HEAD ** (-0.25)


def softmax_slots(scores):
    head = head_of_lane(scores.shape)
    peak = jnp.zeros_like(scores)
    for h in range(HEADS):
        top = jnp.max(jnp.where(head == h, scores, -jnp.inf), axis=1, keepdims=True)
        peak = jnp.where(head == h, top, peak)
    power = jnp.exp(scores - peak)
    return power / head_sums(power)


def decays(log_gate, sums_ref, decay_ref, tick):
    high, low = split_low(log_gate)
    for level in range(LEVELS + 2):
        m = sums_ref[level]
        decay_ref[level] = jnp.exp(nn(m, high) + nn(m, low))
        if level % 2:
            tick(1)
    ones = jnp.ones((ROWS, 256), bf16)
    return jnp.exp(tn(high, ones) + tn(low, ones))


def summaries(share_end, rows):
    return jnp.concatenate([tn(share_end, of(rows, h))[slots(h)] for h in range(HEADS)], axis=0)


def lower_scores(a_ref, share, decay_ref, masks_ref, total_ref, tick, parts_ref=None):
    total_ref[...] = nn(masked(a_ref[...], masks_ref[LEVELS]), tall(share.astype(bf16)))
    for level in range(LEVELS):
        decay = decay_ref[level]
        part = decay * nn(
            masked(a_ref[...], masks_ref[level]), tall((decay * share).astype(bf16))
        )
        if parts_ref is not None:
            parts_ref[level] = part
        total_ref[...] += part
        tick(1)


def mixing(coefficient, share, decay_ref, masks_ref, out_ref, tick):
    def pairs(x, f, mask):
        return masked(nt(x.astype(bf16), tall(f.astype(bf16))).astype(bf16), mask)

    out_ref[...] = pairs(coefficient, share, masks_ref[LEVELS])
    for level in range(LEVELS):
        decay = decay_ref[level]
        out_ref[...] += pairs(coefficient * decay, decay * share, masks_ref[level])
        tick(1)


class Chain:
    def __init__(self, n_line, backward, in_ref, out_ref, send_sem, recv_sem):
        self.z = lax.axis_index("shard")
        self.turn = n_line - 1 - self.z if backward else self.z
        self.next = self.z - 1 if backward else self.z + 1
        self.n_line, self.in_ref, self.out_ref = n_line, in_ref, out_ref
        self.send_sem, self.recv_sem = send_sem, recv_sem

    def copy(self, part):
        half = (part // 2, pl.ds(128 * (part % 2), 128))
        return pltpu.make_async_remote_copy(
            src_ref=self.out_ref.at[half],
            dst_ref=self.in_ref.at[half],
            send_sem=self.send_sem.at[part],
            recv_sem=self.recv_sem.at[part],
            device_id={"dp": lax.axis_index("dp"), "shard": self.next},
            device_id_type=MESH,
        )

    def step(self, i, through, sums_ref):
        if i >= self.n_line:
            return

        @pl.when(self.turn == i)
        def _():
            for part in range(4):
                which, rows = part // 2, slice(128 * (part % 2), 128 * (part % 2) + 128)
                if i == 0:
                    self.in_ref[which, rows] = jnp.zeros((128, HEAD), bf16)
                    new = sums_ref[which, rows]
                else:
                    self.copy(part).wait_recv()
                    new = through[rows] * self.in_ref[which, rows].astype(f32) + sums_ref[which, rows]
                if i < self.n_line - 1:
                    self.out_ref[which, rows] = new.astype(bf16)
                    self.copy(part).start()

    def finish(self):
        @pl.when(self.turn < self.n_line - 1)
        def _():
            for part in range(4):
                self.copy(part).wait_send()


def chain_scratch():
    box = pltpu.VMEM((2, 256, HEAD), bf16)
    sem = pltpu.SemaphoreType.DMA((4,))
    return [box, box, sem, sem, pltpu.VMEM((2, 256, HEAD), f32)]


def sigmoid(x):
    return 1.0 / (1.0 + jnp.exp(-x))


def forward_kernel(pieces, n_ffn, n_square, n_line, *refs):
    (normed_ref, gate_ref, tokens_ref, hgain_ref, gain2_ref, sums_ref, masks_ref) = refs[:7]
    w_refs, refs = refs[7:12], refs[12:]
    shards, refs = refs[:n_ffn], refs[n_ffn:]
    (q_ref, k_ref, v_ref, swish_ref, mixed_ref, state_ref, scores_ref, gated_ref, hidden_ref, normed2_ref) = refs[:10]
    gathered, refs = refs[10 : 10 + n_ffn], refs[10 + n_ffn :]
    w_in, decay_ref, a_ref, b_ref, in_ref, out_ref, chain_send, chain_recv, part_ref, w_sem = refs[:10]
    job = Gather(pieces, shards, gathered, refs[10:], n_square, n_line)
    chain = Chain(n_line, False, in_ref, out_ref, chain_send, chain_recv)
    loads = {}
    for i in (1, 2, 0, 3, 4):
        loads[i] = pltpu.make_async_copy(w_refs[i], w_in.at[i], w_sem.at[i])
        loads[i].start()
    job.load_own()
    barrier(job.p)
    job.start()
    job.until(0)
    tick = job.run
    few = lambda n: job.run(2)
    normed = normed_ref[...]

    def project(i):
        loads[i].wait()
        return nn(normed, w_in[i])

    log_gate = gate_ref[...]
    share = share_of(log_gate)
    through = decays(log_gate, sums_ref, decay_ref, tick)
    share_end = (decay_ref[LEVELS + 1] * share).astype(bf16)
    k_ref[...] = project(1).astype(bf16)
    tick(2)
    v_ref[...] = project(2).astype(bf16)
    tick(2)
    part_ref[0] = summaries(share_end, k_ref[...])
    part_ref[1] = summaries(share_end, v_ref[...])
    chain.step(0, through, part_ref)
    tick(2)
    q_ref[...] = project(0).astype(bf16)
    tick(2)
    a_ref[...] = products(q_ref[...], k_ref[...])
    chain.step(1, through, part_ref)
    tick(2)
    swish_ref[...] = project(3)
    tick(2)
    lower_scores(a_ref, share, decay_ref, masks_ref, scores_ref, few)
    for i in range(2, n_line):
        chain.step(i, through, part_ref)
        tick(4)
    before = decay_ref[LEVELS]
    scores = scores_ref[...] + before * nt(q_ref[...], wide(in_ref[0]))
    scores_ref[...] = scores
    chance = softmax_slots(SCALE * scores)
    mixing(chance, share, decay_ref, masks_ref, b_ref, few)
    carried = nn((chance * before).astype(bf16), wide(in_ref[1]))
    state_ref[...] = in_ref[...]
    b, v = b_ref[...], v_ref[...]
    for h in range(HEADS):
        at = slice(HEAD * h, HEAD * (h + 1))
        mixed = nn(of(b, h), of(v, h)) + of(carried, h)
        mixed_ref[:, at] = mixed
        head_scale = lax.rsqrt(jnp.mean(mixed * mixed, axis=-1, keepdims=True) + norm_eps)
        swish = swish_ref[:, at]
        gated_ref[:, at] = (mixed * head_scale * hgain_ref[...] * (swish * sigmoid(swish))).astype(bf16)
        tick(2)
    loads[4].wait()
    hidden = tokens_ref[...].astype(f32) + nn(gated_ref[...], w_in[4])
    hidden_ref[...] = hidden
    scale2 = lax.rsqrt(jnp.mean(hidden * hidden, axis=-1, keepdims=True) + norm_eps)
    normed2_ref[...] = (hidden * scale2 * gain2_ref[...]).astype(bf16)
    job.finish()
    chain.finish()


VMEM_BLOCK = pl.BlockSpec(memory_space=pltpu.VMEM)
ANY_BLOCK = pl.BlockSpec(memory_space=pl.ANY)


def run_forward(normed, log_gate, tokens, hgain, gain2, sums, masks, weights, shards, n_square, n_line, collective_id):
    rows = normed.shape[0]
    n = n_square * 2 * n_line
    shapes = [s.shape for s in shards]
    pieces = split_pieces(FFN_PLAN, n_square)
    full = lambda dtype: jax.ShapeDtypeStruct((rows, D), dtype)
    pair = pltpu.VMEM((ROWS, HEADS * ROWS), bf16)
    return pl.pallas_call(
        functools.partial(forward_kernel, pieces, len(shards), n_square, n_line),
        out_shape=[full(bf16)] * 3
        + [full(f32)] * 2
        + [jax.ShapeDtypeStruct((2, 256, HEAD), bf16), jax.ShapeDtypeStruct((rows, 256), f32)]
        + [full(bf16), full(f32), full(bf16)]
        + [jax.ShapeDtypeStruct((n,) + s, bf16) for s in shapes],
        in_specs=[VMEM_BLOCK] * 7 + [ANY_BLOCK] * (5 + len(shards)),
        out_specs=[VMEM_BLOCK] * 10 + [ANY_BLOCK] * len(shards),
        scratch_shapes=[
            pltpu.VMEM((5, D, D), bf16),
            pltpu.VMEM((LEVELS + 2, ROWS, 256), f32),
            pair,
            pair,
        ]
        + chain_scratch()
        + [pltpu.SemaphoreType.DMA((5,))]
        + gather_sems(len(pieces), len(shards), n_square, n_line),
        compiler_params=pltpu.CompilerParams(
            collective_id=collective_id, has_side_effects=True, vmem_limit_bytes=60 << 20
        ),
        name="mixer_forward",
    )(normed, log_gate, tokens, hgain, gain2, sums, masks, *weights, *shards)


def backward_kernel(pieces, n_ffn, n_square, n_line, *refs):
    (
        gh_ref, swish_ref, mixed_ref, hgain_ref, q_ref, k_ref, v_ref, gate_ref, sums_ref, masks_ref, back_masks_ref,
        state_ref, scores_ref, w_o_ref,
    ) = refs[:14]
    partial, refs = refs[14 : 14 + n_ffn], refs[14 + n_ffn :]
    gqkvs_ref, branch_ref, dgate_ref, dhgain_ref = refs[:4]
    reduced, refs = refs[4 : 4 + n_ffn], refs[4 + n_ffn :]
    (
        w_o, decay_ref, a_ref, av_ref, at_ref, avt_ref, b_ref, bk_ref, s_parts, d_parts, s_sum, d_sum, shares_ref,
        g_ref, in_ref, out_ref, chain_send, chain_recv, part_ref, w_sem,
    ) = refs[:20]
    refs = refs[20:]
    m = len(pieces)
    job = ReduceFromHbm(
        pieces, partial, refs[:m], refs[m : 2 * m], refs[2 * m : 3 * m], refs[3 * m], refs[3 * m + 1 :], n_square, n_line
    )
    chain = Chain(n_line, True, in_ref, out_ref, chain_send, chain_recv)
    w_load = pltpu.make_async_copy(w_o_ref, w_o, w_sem)
    w_load.start()
    job.load()
    barrier(job.p)
    job.start()
    job.loaded()
    tick = job.run
    few = job.run

    log_gate = gate_ref[...]
    share = share_of(log_gate)
    through = decays(log_gate, sums_ref, decay_ref, lambda n: None)
    branch = gh_ref[...].astype(bf16)
    branch_ref[...] = branch
    w_load.wait()
    tick(4)
    grad_gated = nt(branch, w_o[...]).astype(bf16)
    gain = hgain_ref[...]
    dhgain = jnp.zeros((1, HEAD), f32)
    for h in range(HEADS):
        at = slice(HEAD * h, HEAD * (h + 1))
        mixed, swish = mixed_ref[:, at], swish_ref[:, at]
        gg = of(grad_gated, h).astype(f32)
        sig = sigmoid(swish)
        head_scale = lax.rsqrt(jnp.mean(mixed * mixed, axis=-1, keepdims=True) + norm_eps)
        scaled = mixed * head_scale
        g_head = gg * (swish * sig)
        dhgain += jnp.sum(g_head * scaled, axis=0, keepdims=True)
        gqkvs_ref[:, 3 * D + HEAD * h : 3 * D + HEAD * (h + 1)] = (
            gg * (scaled * gain) * (sig * (1.0 + swish * (1.0 - sig)))
        ).astype(bf16)
        u = g_head * gain
        g_ref[:, at] = (
            head_scale * (u - scaled * (head_scale * jnp.mean(u * mixed, axis=-1, keepdims=True)))
        ).astype(bf16)
        tick(3)
    dhgain_ref[...] = jnp.broadcast_to(dhgain, (8, HEAD))
    q, k, v, g = q_ref[...], k_ref[...], v_ref[...], g_ref[...]
    before, after = decay_ref[LEVELS], decay_ref[LEVELS + 1]
    key_in, value_in = state_ref[0], state_ref[1]
    chance = softmax_slots(SCALE * scores_ref[...])
    av_ref[...] = products(g, v)
    tick(2)
    lower_scores(av_ref, share, decay_ref, masks_ref, d_sum, few, d_parts)
    d_state = before * nt(g, wide(value_in))
    slope = d_sum[...] + d_state
    spread = SCALE * chance * (slope - head_sums(chance * slope))
    chance_before = (chance * before).astype(bf16)
    spread_before = (spread * before).astype(bf16)
    tick(1)
    part_ref[0] = summaries(spread_before, q)
    part_ref[1] = summaries(chance_before, g)
    chain.step(0, through, part_ref)
    a_ref[...] = products(q, k)
    tick(1)
    at_ref[...] = products(k, q)
    tick(1)
    avt_ref[...] = products(v, g)
    lower_scores(a_ref, share, decay_ref, masks_ref, s_sum, few, s_parts)
    chain.step(1, through, part_ref)
    s_state = before * nt(q, wide(key_in))
    mixing(chance, share, decay_ref, masks_ref, b_ref, few)
    chain.step(2, through, part_ref)
    mixing(spread, share, decay_ref, masks_ref, bk_ref, few)
    for i in range(3, n_line):
        chain.step(i, through, part_ref)
    dgate_ref[...] = tn(sums_ref[LEVELS], (spread * s_state + chance * d_state).astype(bf16))
    diagonal = back_masks_ref[LEVELS]
    shares_ref[...] = nn(masked(at_ref[...], diagonal), tall(spread.astype(bf16))) + nn(
        masked(avt_ref[...], diagonal), tall(chance.astype(bf16))
    )

    for level in range(LEVELS):
        decay = decay_ref[level]
        mask = back_masks_ref[level]
        taken = decay * (
            nn(masked(at_ref[...], mask), tall((spread * decay).astype(bf16)))
            + nn(masked(avt_ref[...], mask), tall((chance * decay).astype(bf16)))
        )
        shares_ref[...] += taken
        given = spread * s_parts[level] + chance * d_parts[level]
        place = lax.broadcasted_iota(jnp.int32, (ROWS, 256), 0)
        upper = lax.bitwise_and(lax.shift_right_logical(place, level), 1) == 1
        both = jnp.where(upper, given, taken * share).astype(bf16)
        dgate_ref[...] += tn(sums_ref[level], both)
        tick(2)
    out_key, out_value = in_ref[0], in_ref[1]
    wide_key, wide_value = wide(out_key), wide(out_value)
    taken = after * (nt(k, wide_key) + nt(v, wide_value))
    shares = shares_ref[...] + taken
    kept = key_in.astype(f32) * out_key.astype(f32) + value_in.astype(f32) * out_value.astype(f32)
    high, low = split_low(kept * through)
    ones = jnp.ones((8, 256), bf16)
    kept_row = (nt(ones, high) + nt(ones, low))[:1]
    dgate = dgate_ref[...] + tn(sums_ref[LEVELS + 1], (taken * share).astype(bf16)) + kept_row
    dgate_ref[...] = dgate - jnp.exp(log_gate) * shares
    end = (after * share).astype(bf16)
    q_state = nn(spread_before, wide(key_in))
    k_state = nn(end, wide_key)
    v_state = nn(end, wide_value)
    b, bk = b_ref[...], bk_ref[...]
    for h in range(HEADS):
        low_at = HEAD * h
        gqkvs_ref[:, low_at : low_at + HEAD] = (nn(of(bk, h), of(k, h)) + of(q_state, h)).astype(bf16)
        gqkvs_ref[:, D + low_at : D + low_at + HEAD] = (tn(of(bk, h), of(q, h)) + of(k_state, h)).astype(bf16)
        gqkvs_ref[:, 2 * D + low_at : 2 * D + low_at + HEAD] = (tn(of(b, h), of(g, h)) + of(v_state, h)).astype(bf16)
    job.finish(reduced)
    chain.finish()


def run_backward(
    grad_hidden, swish_pre, mixed, hgain, q, k, v, log_gate, sums, masks, back_masks, state, scores, w_o, partial,
    n_square, n_line, collective_id,
):
    rows = q.shape[0]
    shapes = [a.shape[1:] for a in partial]
    pieces = split_pieces(FFN_PLAN, n_square)
    views = [a.reshape((n_square, 2, n_line) + s) for a, s in zip(partial, shapes)]
    boxes = reduce_boxes(pieces, shapes, [a.dtype for a in partial], n_square, n_line)
    pair = pltpu.VMEM((ROWS, HEADS * ROWS), bf16)
    parts = pltpu.VMEM((LEVELS, ROWS, 256), f32)
    flat = pltpu.VMEM((ROWS, 256), f32)
    return pl.pallas_call(
        functools.partial(backward_kernel, pieces, len(partial), n_square, n_line),
        out_shape=[
            jax.ShapeDtypeStruct((rows, 4 * D), bf16),
            jax.ShapeDtypeStruct((rows, D), bf16),
            jax.ShapeDtypeStruct((rows, 256), f32),
            jax.ShapeDtypeStruct((8, HEAD), f32),
        ]
        + [jax.ShapeDtypeStruct(s, f32) for s in shapes],
        in_specs=[VMEM_BLOCK] * 13 + [ANY_BLOCK] * (1 + len(partial)),
        out_specs=[VMEM_BLOCK] * (4 + len(partial)),
        scratch_shapes=[pltpu.VMEM((D, D), bf16), pltpu.VMEM((LEVELS + 2, ROWS, 256), f32)]
        + [pair] * 6
        + [parts, parts, flat, flat, flat, pltpu.VMEM((ROWS, D), bf16)]
        + chain_scratch()
        + [pltpu.SemaphoreType.DMA]
        + boxes * 3
        + [pltpu.SemaphoreType.DMA((len(pieces),))]
        + reduce_sems(len(pieces), n_square, n_line),
        compiler_params=pltpu.CompilerParams(
            collective_id=collective_id, has_side_effects=True, vmem_limit_bytes=62 << 20
        ),
        name="mixer_backward",
    )(grad_hidden, swish_pre, mixed, hgain, q, k, v, log_gate, sums, masks, back_masks, state, scores, w_o, *views)


def gradients_kernel(n_square, n_line, pieces, small_pieces, *refs):
    (normed_ref, gqkvs_ref, gated_ref, branch_ref, base_ref, gnlow_ref, gh_ref, tokens_ref, gain1_ref) = refs[:9]
    w_refs, outs, small_out, dtok_ref, refs = refs[9:13], refs[13:18], refs[18], refs[19], refs[20:]
    w_in, w_sem = refs[:2]
    refs = refs[2:]
    m = len(pieces)
    dw, peer_part, landed, refs = refs[:m], refs[m : 2 * m], refs[2 * m : 3 * m], refs[3 * m :]
    sems, refs = refs[:4], refs[4:]
    small_dw, small_peer, small_landed, small_sems = refs[0:1], refs[1:2], refs[2:3], refs[3:7]
    p = Place(n_square, n_line)

    def make(ps, boxes, peers, lands, ss):
        return Reduce(
            ps,
            lambda q, a, z: boxes[q].at[a, p.c, z],
            lambda q, k: boxes[q].at[:, 1 - p.c, flip(p.z, k)],
            peers, lands, ss, n_square, n_line,
        )

    job = make(pieces, dw, peer_part, landed, sems)
    small = make(small_pieces, small_dw, small_peer, small_landed, small_sems)
    loads = [pltpu.make_async_copy(w_refs[i], w_in.at[i], w_sem.at[i]) for i in range(4)]
    for load in loads:
        load.start()
    barrier(p)
    normed = normed_ref[...]
    shape = (n_square, 2, n_line, D // (n_square * 2 * n_line))

    def part(i):
        return gqkvs_ref[:, i * D : (i + 1) * D]

    for q in sorted(range(m), key=lambda q: -q):
        i, start, width, order = pieces[q]
        left, right = (normed, part(i)) if i < 4 else (gated_ref[...], branch_ref[:, start : start + width])
        dw[q][...] = tn(left, right).astype(bf16).reshape(shape + (width,))
        job.start([q])
    job.until(-5)
    g = gnlow_ref[...]
    for i in range(4):
        loads[i].wait()
        g = g + nt(part(i), w_in[i])
        job.run(2)
    x = tokens_ref[...].astype(f32)
    scale1 = lax.rsqrt(jnp.mean(x * x, axis=-1, keepdims=True) + norm_eps)
    u = g * gain1_ref[...]
    dtok_ref[...] = (
        gh_ref[...] + scale1 * u - x * (scale1 * scale1 * scale1 * jnp.mean(u * x, axis=-1, keepdims=True))
    )
    job.run(4)
    high, low = split_low(g * x * scale1)
    ones = jnp.ones((ROWS, 128), bf16)
    column = tn(high, ones) + tn(low, ones)
    lane = lax.broadcasted_iota(jnp.int32, (D, 128), 1)
    small_dw[0][...] = (base_ref[...] + jnp.where(lane == GAIN1_LANE, column, 0.0)).reshape(shape + (128,))
    small.start()
    while job.todo:
        job.run(4)
        small.run(1)
    small.finish([small_out])
    job.finish(outs)


GAIN1_LANE = 34


def run_gradients(
    normed, gqkvs, gated, branch, base, gnlow, grad_hidden, tokens, gain1, weights, n_square, n_line, collective_id
):
    n = n_square * 2 * n_line
    r = D // n
    rows = normed.shape[0]
    shapes = [(r, D)] * 5
    pieces = split_pieces(MIXER_PLAN, n_square)
    small_pieces = split_pieces([(0, 0, 128, "a")], n_square)
    dw = [pltpu.VMEM((n_square, 2, n_line, r, width), bf16) for i, start, width, order in pieces]
    boxes = reduce_boxes(pieces, shapes, [bf16] * 5, n_square, n_line)
    small_box = pltpu.VMEM((n_square, n_line, r, 128), f32)
    return pl.pallas_call(
        functools.partial(gradients_kernel, n_square, n_line, pieces, small_pieces),
        out_shape=[jax.ShapeDtypeStruct((r, D), f32)] * 5
        + [jax.ShapeDtypeStruct((r, 128), f32), jax.ShapeDtypeStruct((rows, D), f32)],
        in_specs=[VMEM_BLOCK] * 9 + [ANY_BLOCK] * 4,
        out_specs=[VMEM_BLOCK] * 7,
        scratch_shapes=[pltpu.VMEM((4, D, D), bf16), pltpu.SemaphoreType.DMA((4,))]
        + dw
        + boxes * 2
        + reduce_sems(len(pieces), n_square, n_line)
        + [pltpu.VMEM((n_square, 2, n_line, r, 128), f32), small_box, small_box]
        + reduce_sems(1, n_square, n_line),
        compiler_params=pltpu.CompilerParams(
            collective_id=collective_id, has_side_effects=True, vmem_limit_bytes=62 << 20
        ),
        name="weight_gradients",
    )(normed, gqkvs, gated, branch, base, gnlow, grad_hidden, tokens, gain1, *weights)


FF_TILE = 256


def ffn_kernel(
    normed2_ref, hidden_ref, cot_ref, valid_ref, gain2_ref, wg_ref, wu_ref, wd_ref,
    output_ref, gh_ref, dgain2_ref, dg_ref, du_ref, dd_ref,
    low_ref, out_acc, back_acc,
):
    step = pl.program_id(0)

    @pl.when(step == 0)
    def _():
        low_ref[...] = (cot_ref[...].astype(f32) * valid_ref[...]).astype(bf16)
        out_acc[...] = jnp.zeros_like(out_acc)
        back_acc[...] = jnp.zeros_like(back_acc)

    x, low = normed2_ref[...], low_ref[...]
    wg, wu, wd = wg_ref[...], wu_ref[...], wd_ref[...]
    gate, up = nn(x, wg), nn(x, wu)
    inside = nt(low, wd).astype(bf16).astype(f32)
    sig = sigmoid(gate)
    act = gate * sig
    inner = (act * up).astype(bf16)
    g_gate = (inside * up * (sig * (1.0 + gate * (1.0 - sig)))).astype(bf16)
    g_up = (inside * act).astype(bf16)
    out_acc[...] += nn(inner, wd)
    dd_ref[...] = tn(inner, low).astype(bf16)
    dg_ref[...] = tn(x, g_gate).astype(bf16)
    du_ref[...] = tn(x, g_up).astype(bf16)
    back_acc[...] += nt(g_gate, wg) + nt(g_up, wu)

    @pl.when(step == pl.num_programs(0) - 1)
    def _():
        hidden, valid = hidden_ref[...], valid_ref[...]
        output_ref[...] = (valid * (hidden + out_acc[...])).astype(bf16)
        scale2 = lax.rsqrt(jnp.mean(hidden * hidden, axis=-1, keepdims=True) + norm_eps)
        back = back_acc[...]
        scaled = hidden * scale2
        dgain2_ref[...] = jnp.broadcast_to(jnp.sum(back * scaled, axis=0, keepdims=True), dgain2_ref.shape)
        u = back * gain2_ref[...]
        gh_ref[...] = cot_ref[...].astype(f32) * valid + scale2 * (
            u - scaled * (scale2 * jnp.mean(u * hidden, axis=-1, keepdims=True))
        )


def run_ffn(normed2, hidden, cotangent, valid, gain2, w_gate, w_up, w_down):
    rows = normed2.shape[0]
    ff = w_down.shape[0]
    tile = FF_TILE
    fixed = lambda *shape: pl.BlockSpec(shape, lambda j: (0, 0))
    cols = pl.BlockSpec((D, tile), lambda j: (0, j))
    down = pl.BlockSpec((tile, D), lambda j: (j, 0))
    return pl.pallas_call(
        ffn_kernel,
        grid=(ff // tile,),
        out_shape=[
            jax.ShapeDtypeStruct((rows, D), bf16),
            jax.ShapeDtypeStruct((rows, D), f32),
            jax.ShapeDtypeStruct((8, D), f32),
            jax.ShapeDtypeStruct((D, ff), bf16),
            jax.ShapeDtypeStruct((D, ff), bf16),
            jax.ShapeDtypeStruct((ff, D), bf16),
        ],
        in_specs=[fixed(rows, D)] * 3 + [fixed(rows, 1), fixed(1, D), cols, cols, down],
        out_specs=[fixed(rows, D), fixed(rows, D), fixed(8, D), cols, cols, down],
        scratch_shapes=[pltpu.VMEM((rows, D), bf16), pltpu.VMEM((rows, D), f32), pltpu.VMEM((rows, D), f32)],
        compiler_params=pltpu.CompilerParams(vmem_limit_bytes=40 << 20),
        name="ffn",
    )(normed2, hidden, cotangent, valid, gain2, w_gate, w_up, w_down)


def pack_small(low, up, bias, hgain, gain1, gain2, dtype):
    n, rows = low.shape[0], low.shape[1]
    fill = lambda a: jnp.pad(a.astype(dtype), ((0, 0), (0, rows - a.shape[1]), (0, 0)))
    parts = [fill(low), fill(up)] + [fill(a[:, :, None]) for a in (bias, hgain, gain1, gain2)]
    out = jnp.concatenate(parts, axis=2)
    return jnp.pad(out, ((0, 0), (0, 0), (0, 128 - out.shape[2])))


def unpack_small(packed):
    n, rows = packed.shape[0], packed.shape[1]
    few = rows // 4
    low = packed[:, :, :16].reshape(n * rows, 16)
    up = packed[:, :few, 16:32].reshape(n * few, 16)
    bias, hgain = (packed[:, :few, lane].reshape(n * few) for lane in (32, 33))
    gain1, gain2 = (packed[:, :, lane].reshape(n * rows) for lane in (34, 35))
    return low, up, bias, hgain, gain1, gain2


def per_device(
    n_square, n_line,
    tokens, cotangent, lengths, norm1_gain, w_query, w_key, w_value, w_gate_low, w_gate_up,
    gate_bias, head_gain, w_swish, w_out, norm2_gain, w_ffn_gate, w_ffn_up, w_ffn_down,
):
    count = tokens.shape[0]
    n = n_square * 2 * n_line
    small = pack_small(
        *(a[None] for a in (w_gate_low, w_gate_up, gate_bias, head_gain, norm1_gain, norm2_gain)), bf16
    )[0]
    got = gather(
        [w_query, w_key, w_value, w_swish, w_out, small], MIXER_PLAN + [(5, 0, 128, "a")], n_square, n_line, 1
    )
    weights = [g.reshape(D, D) for g in got[:5]]
    low_w, up_w, bias, hgain, gain1, gain2 = unpack_small(got[5])
    bias, hgain, gain1, gain2 = (x.astype(f32) for x in (bias, hgain, gain1, gain2))
    sums, masks = level_constants(count)
    back_masks = np.ascontiguousarray(np.swapaxes(masks, 1, 2))

    position = lax.axis_index("shard") * count + jnp.arange(count, dtype=jnp.int32)
    valid = (position < lengths[0]).astype(f32)[:, None]
    resid = tokens.astype(f32)
    scale1 = lax.rsqrt(jnp.mean(resid * resid, axis=-1, keepdims=True) + norm_eps)
    normed = (resid * scale1 * gain1).astype(bf16)
    low_rank = nn(normed, low_w).astype(bf16)
    logits = nt(low_rank, up_w) + bias
    log_gate = jax.nn.log_sigmoid(logits) / gate_norm
    q, k, v, swish_pre, mixed, state, scores, gated, hidden, normed2, *ffn_all = run_forward(
        normed, log_gate, tokens, hgain[None], gain2[None], sums, masks, weights, [w_ffn_gate, w_ffn_up, w_ffn_down],
        n_square, n_line, 2,
    )
    w_g, w_u = (g.reshape(D, -1) for g in ffn_all[:2])
    w_d = ffn_all[2].reshape(-1, D)
    ff = w_d.shape[0]
    output, grad_hidden, d_gain2, d_gate, d_up_proj, d_down = run_ffn(
        normed2, hidden, cotangent, valid, gain2[None], w_g, w_u, w_d
    )
    gqkvs, branch, grad_log, d_hgain, s_gate, s_up, s_down = run_backward(
        grad_hidden, swish_pre, mixed, hgain[None], q, k, v, log_gate, sums, masks, back_masks, state, scores, weights[4],
        [d_gate.reshape(n, D // n, ff), d_up_proj.reshape(n, D // n, ff), d_down.reshape(n, ff // n, D)],
        n_square, n_line, 3,
    )
    grad_logits = grad_log / gate_norm * jax.nn.sigmoid(-logits)
    d_bias = jnp.sum(grad_logits, axis=0)
    logits_high, logits_low = split_low(grad_logits)
    d_up = tn(logits_high, low_rank) + tn(logits_low, low_rank)
    grad_lowrank = (nn(logits_high, up_w) + nn(logits_low, up_w)).astype(bf16)
    d_low = tn(normed, grad_lowrank)
    base = pack_small(
        d_low.reshape(n, -1, 16), d_up.reshape(n, -1, 16), d_bias.reshape(n, -1), d_hgain[0].reshape(n, -1),
        jnp.zeros((n, D // n), f32), d_gain2[0].reshape(n, -1), f32,
    ).reshape(D, 128)
    s_q, s_k, s_v, s_swish, s_out, s_small, d_tokens = run_gradients(
        normed, gqkvs, gated, branch, base, nt(grad_lowrank, low_w), grad_hidden, tokens, gain1[None], weights[:4],
        n_square, n_line, 4,
    )
    o_low, o_up, o_bias, o_hgain, o_gain1, o_gain2 = unpack_small(s_small[None])
    return (
        output, d_tokens, o_gain1,
        s_q, s_k, s_v,
        o_low, o_up, o_bias, o_hgain,
        s_swish, s_out, o_gain2,
        s_gate, s_up, s_down,
    )


def solution(mesh):
    rows, row = P(("dp", "shard"), None), P(("dp", "shard"))
    placed = (rows, rows, P("dp"), row, rows, rows, rows, rows, rows, row, row, rows, rows, row, rows, rows, rows)
    out = (rows, rows, row, rows, rows, rows, rows, rows, row, row, rows, rows, row, rows, rows, rows)
    return jax.shard_map(
        functools.partial(per_device, mesh.shape["dp"] // 2, mesh.shape["shard"]),
        mesh=mesh,
        in_specs=placed,
        out_specs=out,
        check_vma=False,
    )
```

```python
import functools

import jax
import jax.numpy as jnp
import numpy as np
from jax import lax
from jax.experimental import pallas as pl
from jax.experimental.pallas import tpu as pltpu
from jax.sharding import PartitionSpec as P

D = 1024
HEADS = 4
HEAD = 256
SLOTS = 64
norm_eps = 1e-06
gate_norm = 8.0
MESH = pl.DeviceIdType.MESH


class Place:
    def __init__(self, n_square, n_line):
        self.n_square, self.n_line = n_square, n_line
        dp = lax.axis_index("dp")
        self.z = lax.axis_index("shard")
        self.c = lax.rem(dp, 2)
        self.a = lax.div(dp, 2)

    def slot(self, k):
        out = 0
        for z in range(self.n_line):
            near = sorted(range(self.n_line), key=lambda other: (abs(other - z), other))
            out = out + jnp.where(self.z == z, near[k], 0)
        return out

    def device(self, a, c, z):
        return {"dp": a * 2 + c, "shard": z}

    def slab(self, a, c, z):
        return (a * 2 + c) * self.n_line + z


def flip(value, bits):
    for b in range(8):
        if bits >> b & 1:
            digit = lax.rem(lax.div(value, 1 << b), 2)
            value = value + (1 - 2 * digit) * (1 << b)
    return value


LINE = "line"
LATE_LINE = 3.5


class Tree:
    def __init__(self, order, n_line):
        self.slabs = [(0, 0)]
        self.up, self.down, self.time = {}, {(0, 0): []}, {(0, 0): 0}
        late = order[0] != LINE
        for stage, dim in enumerate(order):
            for m, k in list(self.slabs):
                steps = range(1, n_line) if dim == LINE else [dim]
                for step in steps:
                    child = (m, step) if dim == LINE else (m ^ step, k)
                    self.slabs.append(child)
                    self.up[child] = (dim, step, (m, k))
                    self.down[child] = []
                    self.down[(m, k)].append(child)
                    if dim == LINE:
                        self.time[child] = step + (n_line + 1 if late else 0)
                    else:
                        self.time[child] = self.time[(m, k)] + 1


def orders(n_square):
    bits = [1 << b for b in range((n_square - 1).bit_length())]
    return {"a": (LINE, *bits), "b": (LINE, *bits[::-1]), "c": (*bits[::-1], LINE)}


def split_pieces(plan, n_square):
    by_name = orders(n_square)
    return [(i, start, width, by_name[name]) for i, start, width, name in plan]


MIXER_PLAN = [
    (0, 0, 1024, "a"), (1, 0, 1024, "b"), (2, 0, 1024, "a"), (3, 0, 1024, "b"), (4, 512, 512, "a"), (4, 0, 512, "c"),
]
FFN_PLAN = [(0, 0, 2816, "a"), (1, 0, 2816, "b"), (2, 0, 384, "a"), (2, 384, 384, "b"), (2, 768, 256, "c")]


def barrier(place):
    sem = pltpu.get_barrier_semaphore()
    peers = [place.device(place.a, 1 - place.c, place.z)]
    bit = 1
    while bit < place.n_square:
        peers.append(place.device(flip(place.a, bit), place.c, place.z))
        bit *= 2
    for k in range(1, place.n_line):
        peers.append(place.device(place.a, place.c, flip(place.z, k)))
    for peer in peers:
        pl.semaphore_signal(sem, inc=1, device_id=peer, device_id_type=MESH)
    pl.semaphore_wait(sem, len(peers))


class Gather:
    def __init__(self, pieces, ins, outs, sems, n_square, n_line):
        self.pieces, self.ins, self.outs = pieces, ins, outs
        self.local_sem, self.net_send, self.net_recv, self.core_send, self.core_recv, self.line_send = sems
        self.n_square, self.n_line = n_square, n_line
        self.p = Place(n_square, n_line)
        self.own = [
            pltpu.make_async_copy(
                ins[i], outs[i].at[self.p.slab(self.p.a, self.p.c, self.p.z)], self.local_sem.at[i]
            )
            for i in range(len(ins))
        ]
        self.trees = [Tree(order, n_line) for i, start, width, order in pieces]
        events = [(tree.time[slab], q, slab, False) for q, tree in enumerate(self.trees) for slab in tree.slabs]
        for q, tree in enumerate(self.trees):
            if pieces[q][3][0] != LINE:
                events += [(LATE_LINE + 0.1 * j, q, slab, True) for j, slab in enumerate(tree.slabs) if slab[1] == 0]
        self.todo = sorted(events, key=lambda e: e[0])
        self.started = []
        self.places = [self.p.slot(k) for k in range(n_line)]

    def at(self, q, m, k, c=None):
        i, start, width, order = self.pieces[q]
        p = self.p
        z = self.places[k] if order[0] == LINE else flip(p.z, k)
        s = p.slab(flip(p.a, m), p.c if c is None else c, z)
        return self.outs[i].at[s, :, pl.ds(start, width)]

    def source(self, q, m, k):
        if m == 0 and k == 0:
            i, start, width, _ = self.pieces[q]
            return self.ins[i].at[:, pl.ds(start, width)]
        return self.at(q, m, k)

    def go(self, q, m, k, sems, index, peer):
        copy = pltpu.make_async_remote_copy(
            src_ref=self.source(q, m, k),
            dst_ref=self.at(q, m, k),
            send_sem=sems[0].at[index],
            recv_sem=sems[1].at[index],
            device_id=peer,
            device_id_type=MESH,
        )
        copy.start()
        self.started.append((None, copy))

    def along(self, q, k):
        p = self.p
        z = self.places[k]
        for way, (step, more) in enumerate(((1, (z <= p.z) & (p.z < self.n_line - 1)), (-1, (z >= p.z) & (p.z > 0)))):
            copy = pltpu.make_async_remote_copy(
                src_ref=self.source(q, 0, k),
                dst_ref=self.at(q, 0, k),
                send_sem=self.line_send.at[q, way, k],
                recv_sem=self.net_recv.at[q, 0, z],
                device_id=p.device(p.a, p.c, p.z + step),
                device_id_type=MESH,
            )
            pl.when(more)(copy.start)
            self.started.append((more, copy))

    def arrived(self, q, m, k, sems, c, place=None):
        p = self.p
        pltpu.make_async_remote_copy(
            src_ref=self.at(q, m, k, c),
            dst_ref=self.at(q, m, k, c),
            send_sem=sems[0].at[q, m, k],
            recv_sem=sems[1].at[q, m, k if place is None else place],
            device_id=p.device(p.a, 1 - p.c, p.z),
            device_id_type=MESH,
        ).wait_recv()

    def load_own(self):
        for copy in self.own:
            copy.start()

    def start(self):
        for q, tree in enumerate(self.trees):
            if self.pieces[q][3][0] == LINE:
                self.along(q, 0)

    def pass_on(self, q, slab, child):
        p = self.p
        dim, step, _ = self.trees[q].up[child]
        peer = p.device(p.a, p.c, flip(p.z, step)) if dim == LINE else p.device(flip(p.a, step), p.c, p.z)
        self.go(q, *slab, (self.net_send, self.net_recv), (q, *child), peer)

    def until(self, time):
        self.run(sum(e[0] <= time for e in self.todo))

    def run(self, n):
        p = self.p
        net, core = (self.net_send, self.net_recv), (self.core_send, self.core_recv)
        for time, q, slab, line in self.todo[:n]:
            tree = self.trees[q]
            first = self.pieces[q][3][0] == LINE
            if line:
                for child in tree.down[slab]:
                    if tree.up[child][0] == LINE:
                        self.pass_on(q, slab, child)
                continue
            if slab != (0, 0):
                lined = first and slab[0] == 0
                self.arrived(q, *slab, net, p.c, self.places[slab[1]] if lined else None)
                if lined:
                    self.along(q, slab[1])
            for child in tree.down[slab]:
                if tree.up[child][0] != LINE:
                    self.pass_on(q, slab, child)
            self.go(q, *slab, core, (q, *slab), p.device(p.a, 1 - p.c, p.z))
        self.todo = self.todo[n:]

    def arrivals(self):
        self.run(len(self.todo))
        for copy in self.own:
            copy.wait()
        for k in range(self.n_line):
            for q in range(len(self.pieces)):
                for m in range(self.n_square):
                    self.arrived(q, m, k, (self.core_send, self.core_recv), 1 - self.p.c)

    def close(self):
        for more, copy in self.started:
            if more is None:
                copy.wait_send()
            else:
                pl.when(more)(copy.wait_send)


def gather_sems(n_pieces, n_arrays, n_square, n_line):
    sem = pltpu.SemaphoreType.DMA((n_pieces, n_square, n_line))
    line = pltpu.SemaphoreType.DMA((n_pieces, 2, n_line))
    return [pltpu.SemaphoreType.DMA((n_arrays,)), sem, sem, sem, sem, line]


def add_into(ref, other):
    ref[...] = ref[...] + other[...]


class Reduce:
    def __init__(self, pieces, mine, theirs, peer_part, landed, sems, n_square, n_line):
        self.pieces, self.mine, self.theirs = pieces, mine, theirs
        self.peer_part, self.landed = peer_part, landed
        self.net_send, self.net_recv, self.core_send, self.core_recv = sems
        self.n_square, self.n_line = n_square, n_line
        self.p = Place(n_square, n_line)
        self.ks = list(range(n_line))[::-1]
        self.trees = [Tree(order, n_line) for i, start, width, order in pieces]
        events = [
            (-tree.time[slab], q, slab)
            for q, tree in enumerate(self.trees)
            for slab in tree.slabs[::-1]
        ]
        self.todo = sorted((e for e in events if e[2] != (0, 0)), key=lambda e: e[0])
        self.sent, self.have = [], set()

    def core(self, q, k):
        p = self.p
        return pltpu.make_async_remote_copy(
            src_ref=self.theirs(q, k),
            dst_ref=self.peer_part[q].at[:, flip(p.z, k)],
            send_sem=self.core_send.at[q, k],
            recv_sem=self.core_recv.at[q, k],
            device_id=p.device(p.a, 1 - p.c, p.z),
            device_id_type=MESH,
        )

    def net(self, q, slab):
        p = self.p
        m, k = slab
        dim, step, _ = self.trees[q].up[slab]
        peer = p.device(p.a, p.c, flip(p.z, step)) if dim == LINE else p.device(flip(p.a, step), p.c, p.z)
        return pltpu.make_async_remote_copy(
            src_ref=self.mine(q, flip(p.a, m), flip(p.z, k)),
            dst_ref=self.landed[q].at[m, k],
            send_sem=self.net_send.at[q, m, k],
            recv_sem=self.net_recv.at[q, m, k],
            device_id=peer,
            device_id_type=MESH,
        )

    def start(self, pieces=None):
        for q in range(len(self.pieces)) if pieces is None else pieces:
            for k in self.ks[:1] if self.pieces[q][3][0] == LINE else self.ks:
                self.core(q, k).start()

    def from_core(self, q, k):
        if (q, k) not in self.have:
            self.have.add((q, k))
            self.core(q, k).wait_recv()
            if k and self.pieces[q][3][0] == LINE:
                self.core(q, k - 1).start()

    def until(self, time):
        self.run(sum(e[0] <= time for e in self.todo))

    def run(self, n, pieces=None):
        p = self.p
        now = [e for e in self.todo if pieces is None or e[1] in pieces][:n]
        self.todo = [e for e in self.todo if e not in now]
        for time, q, slab in now:
            m, k = slab
            self.from_core(q, k)
            a, z = flip(p.a, m), flip(p.z, k)
            add_into(self.mine(q, a, z), self.peer_part[q].at[a, z])
            for child in self.trees[q].down[slab]:
                self.net(q, child).wait_recv()
                add_into(self.mine(q, a, z), self.landed[q].at[child])
            copy = self.net(q, slab)
            copy.start()
            self.sent.append(copy)

    def finish(self, outs):
        self.run(len(self.todo))
        p = self.p
        for q in range(len(self.pieces)):
            i, start, width, _ = self.pieces[q]
            self.from_core(q, 0)
            total = self.mine(q, p.a, p.z)[...].astype(jnp.float32)
            total = total + self.peer_part[q][p.a, p.z].astype(jnp.float32)
            for child in self.trees[q].down[(0, 0)]:
                self.net(q, child).wait_recv()
                total = total + self.landed[q][child].astype(jnp.float32)
            outs[i][:, pl.ds(start, width)] = total
        for copy in self.sent:
            copy.wait_send()
        for k in self.ks:
            for q in range(len(self.pieces)):
                self.core(q, k).wait_send()


def reduce_boxes(pieces, shapes, dtypes, n_square, n_line):
    return [
        pltpu.VMEM((n_square, n_line, shapes[i][0], width), dtypes[i]) for i, start, width, _ in pieces
    ]


def reduce_sems(n_pieces, n_square, n_line):
    sem = pltpu.SemaphoreType.DMA((n_pieces, n_square, n_line))
    core_sem = pltpu.SemaphoreType.DMA((n_pieces, n_line))
    return [sem, sem, core_sem, core_sem]


class ReduceFromHbm(Reduce):
    def __init__(self, pieces, ins, mine, peer_part, landed, local_sem, sems, n_square, n_line):
        p = Place(n_square, n_line)

        def columns(q):
            i, start, width, _ = pieces[q]
            return ins[i], pl.ds(start, width)

        def theirs(q, k):
            ref, cols = columns(q)
            return ref.at[:, 1 - p.c, flip(p.z, k), :, cols]

        super().__init__(pieces, lambda q, a, z: mine[q].at[a, z], theirs, peer_part, landed, sems, n_square, n_line)
        self.loads = []
        for q in range(len(pieces)):
            ref, cols = columns(q)
            self.loads.append(pltpu.make_async_copy(ref.at[:, p.c, :, :, cols], mine[q], local_sem.at[q]))

    def load(self):
        for copy in self.loads:
            copy.start()

    def loaded(self):
        for copy in self.loads:
            copy.wait()


def reduce_body(pieces, n_arrays, n_square, n_line, *refs):
    n = len(pieces)
    ins, outs, rest = refs[:n_arrays], refs[n_arrays : 2 * n_arrays], refs[2 * n_arrays :]
    job = ReduceFromHbm(
        pieces, ins, rest[:n], rest[n : 2 * n], rest[2 * n : 3 * n], rest[3 * n], rest[3 * n + 1 :], n_square, n_line
    )
    job.load()
    barrier(job.p)
    job.start()
    job.loaded()
    job.finish(outs)


def reduce_scatter(arrays, plan, n_square, n_line, collective_id):
    shapes = [a.shape[1:] for a in arrays]
    pieces = split_pieces(plan, n_square)
    views = [a.reshape((n_square, 2, n_line) + s) for a, s in zip(arrays, shapes)]
    any_space = pl.BlockSpec(memory_space=pl.ANY)
    boxes = reduce_boxes(pieces, shapes, [x.dtype for x in arrays], n_square, n_line)
    return pl.pallas_call(
        functools.partial(reduce_body, pieces, len(arrays), n_square, n_line),
        out_shape=[jax.ShapeDtypeStruct(s, jnp.float32) for s in shapes],
        in_specs=[any_space] * len(arrays),
        out_specs=[pl.BlockSpec(memory_space=pltpu.VMEM)] * len(arrays),
        scratch_shapes=boxes * 3
        + [pltpu.SemaphoreType.DMA((len(pieces),))]
        + reduce_sems(len(pieces), n_square, n_line),
        compiler_params=pltpu.CompilerParams(
            collective_id=collective_id, has_side_effects=True, vmem_limit_bytes=60 << 20
        ),
        name="reduce_grads",
    )(*views)


f32, bf16 = jnp.float32, jnp.bfloat16
ROWS = 256
LEVELS = 8


def level_constants(rows):
    t, i = np.arange(rows)[:, None], np.arange(rows)[None, :]
    sums, masks = [], []
    for level in range((rows - 1).bit_length()):
        same = (t >> (level + 1)) == (i >> (level + 1))
        upper_t, upper_i = (t >> level) & 1, (i >> level) & 1
        sums.append(
            (same & (upper_t == 1) & (upper_i == 1) & (i <= t))
            | (same & (upper_t == 0) & (upper_i == 0) & (i > t))
        )
        masks.append((t > i) & (((t ^ i) >> level) == 1))
    sums += [i <= t, i > t]
    masks.append(t == i)
    return np.stack(sums).astype(bf16), np.stack(masks).astype(bf16)


def nn(a, b):
    return lax.dot_general(a, b, (((1,), (0,)), ((), ())), preferred_element_type=f32)


def nt(a, b):
    return lax.dot_general(a, b, (((1,), (1,)), ((), ())), preferred_element_type=f32)


def tn(a, b):
    return lax.dot_general(a, b, (((0,), (0,)), ((), ())), preferred_element_type=f32)


def split_low(x):
    high = x.astype(bf16)
    return high, (x - high.astype(f32)).astype(bf16)


def head_of_lane(shape):
    return lax.broadcasted_iota(jnp.int32, shape, 1) // SLOTS


def tall(x):
    head = head_of_lane(x.shape)
    zero = jnp.zeros_like(x)
    return jnp.concatenate([jnp.where(head == h, x, zero) for h in range(HEADS)], axis=0)


def wide(state):
    head = lax.broadcasted_iota(jnp.int32, state.shape, 0) // SLOTS
    zero = jnp.zeros_like(state)
    return jnp.concatenate([jnp.where(head == h, state, zero) for h in range(HEADS)], axis=1)


def of(x, h):
    return x[:, HEAD * h : HEAD * (h + 1)]


def slots(h):
    return slice(SLOTS * h, SLOTS * (h + 1))


def products(a, b):
    return jnp.concatenate([nt(of(a, h), of(b, h)) for h in range(HEADS)], axis=1).astype(bf16)


def masked(a, mask):
    return a * jnp.concatenate([mask] * HEADS, axis=1)


def share_of(log_gate):
    small = -log_gate * (1.0 + log_gate * (0.5 + log_gate * (1.0 / 6.0)))
    return jnp.where(log_gate > -0.01, small, 1.0 - jnp.exp(log_gate))


def head_sums(x):
    ones = (head_of_lane((256, 256)) == lax.broadcasted_iota(jnp.int32, (256, 256), 0) // SLOTS)
    ones = jnp.where(ones, 1.0, 0.0).astype(bf16)
    high, low = split_low(x)
    return nn(high, ones) + nn(low, ones)


SCALE = 1.5 * HEAD ** (-0.25)


def softmax_slots(scores):
    head = head_of_lane(scores.shape)
    peak = jnp.zeros_like(scores)
    for h in range(HEADS):
        top = jnp.max(jnp.where(head == h, scores, -jnp.inf), axis=1, keepdims=True)
        peak = jnp.where(head == h, top, peak)
    power = jnp.exp(scores - peak)
    return power / head_sums(power)


def decays(log_gate, sums_ref, decay_ref, tick):
    high, low = split_low(log_gate)
    for level in range(LEVELS + 2):
        m = sums_ref[level]
        decay_ref[level] = jnp.exp(nn(m, high) + nn(m, low))
        if level % 2:
            tick(1)
    ones = jnp.ones((ROWS, 256), bf16)
    return jnp.exp(tn(high, ones) + tn(low, ones))


def summaries(share_end, rows):
    return jnp.concatenate([tn(share_end, of(rows, h))[slots(h)] for h in range(HEADS)], axis=0)


def lower_scores(a_ref, share, decay_ref, masks_ref, total_ref, tick, parts_ref=None):
    total_ref[...] = nn(masked(a_ref[...], masks_ref[LEVELS]), tall(share.astype(bf16)))
    for level in range(LEVELS):
        decay = decay_ref[level]
        part = decay * nn(
            masked(a_ref[...], masks_ref[level]), tall((decay * share).astype(bf16))
        )
        if parts_ref is not None:
            parts_ref[level] = part.astype(bf16)
        total_ref[...] += part
        tick(1)


def mixing(coefficient, share, decay_ref, masks_ref, out_ref, tick):
    def pairs(x, f, mask):
        return masked(nt(x.astype(bf16), tall(f.astype(bf16))).astype(bf16), mask)

    out_ref[...] = pairs(coefficient, share, masks_ref[LEVELS])
    for level in range(LEVELS):
        decay = decay_ref[level]
        out_ref[...] += pairs(coefficient * decay, decay * share, masks_ref[level])
        tick(1)


class Chain:
    def __init__(self, n_line, backward, in_ref, out_ref, send_sem, recv_sem):
        self.z = lax.axis_index("shard")
        self.turn = n_line - 1 - self.z if backward else self.z
        self.next = self.z - 1 if backward else self.z + 1
        self.n_line, self.in_ref, self.out_ref = n_line, in_ref, out_ref
        self.send_sem, self.recv_sem = send_sem, recv_sem

    def copy(self, part):
        half = (part // 2, pl.ds(128 * (part % 2), 128))
        return pltpu.make_async_remote_copy(
            src_ref=self.out_ref.at[half],
            dst_ref=self.in_ref.at[half],
            send_sem=self.send_sem.at[part],
            recv_sem=self.recv_sem.at[part],
            device_id={"dp": lax.axis_index("dp"), "shard": self.next},
            device_id_type=MESH,
        )

    def step(self, i, through, sums_ref):
        if i >= self.n_line:
            return

        @pl.when(self.turn == i)
        def _():
            for part in range(4):
                which, rows = part // 2, slice(128 * (part % 2), 128 * (part % 2) + 128)
                if i == 0:
                    self.in_ref[which, rows] = jnp.zeros((128, HEAD), bf16)
                    new = sums_ref[which, rows]
                else:
                    self.copy(part).wait_recv()
                    new = through[rows] * self.in_ref[which, rows].astype(f32) + sums_ref[which, rows]
                if i < self.n_line - 1:
                    self.out_ref[which, rows] = new.astype(bf16)
                    self.copy(part).start()

    def finish(self):
        @pl.when(self.turn < self.n_line - 1)
        def _():
            for part in range(4):
                self.copy(part).wait_send()


def chain_scratch():
    box = pltpu.VMEM((2, 256, HEAD), bf16)
    sem = pltpu.SemaphoreType.DMA((4,))
    return [box, box, sem, sem, pltpu.VMEM((2, 256, HEAD), f32)]


def sigmoid(x):
    return 1.0 / (1.0 + jnp.exp(-x))


def spots(r):
    gate = lax.broadcasted_iota(jnp.int32, (256, D), 0)
    row = lax.broadcasted_iota(jnp.int32, (256, D), 1)
    per = r // 4
    return jnp.where((gate // per) * r + gate % per == row, 1.0, 0.0).astype(bf16)


def ones_where(shape, condition):
    i = lax.broadcasted_iota(jnp.int32, shape, 0)
    j = lax.broadcasted_iota(jnp.int32, shape, 1)
    return jnp.where(condition(i, j), 1.0, 0.0).astype(bf16)


def forward_kernel(mixer_pieces, pieces, n_mixer, n_ffn, n_square, n_line, *refs):
    tokens_ref, sums_ref, masks_ref = refs[:3]
    mixer_shards, shards, refs = refs[3 : 3 + n_mixer], refs[3 + n_mixer : 3 + n_mixer + n_ffn], refs[3 + n_mixer + n_ffn :]
    (
        q_ref, k_ref, v_ref, swish_ref, mixed_ref, state_ref, scores_ref, gated_ref, hidden_ref, normed2_ref,
        normed_ref, gate_ref, rank_ref, gains_ref, hgain_ref, up_pad_ref, low_pad_ref,
    ) = refs[:17]
    refs = refs[17:]
    w_refs, gathered, refs = refs[:n_mixer], refs[n_mixer : n_mixer + n_ffn], refs[n_mixer + n_ffn :]
    w_in, small, decay_ref, a_ref, b_ref, in_ref, out_ref, chain_send, chain_recv, part_ref, w_sem = refs[:11]
    refs = refs[11:]
    first = Gather(mixer_pieces, mixer_shards, w_refs, refs[:6], n_square, n_line)
    job = Gather(pieces, shards, gathered, refs[6:], n_square, n_line)
    chain = Chain(n_line, False, in_ref, out_ref, chain_send, chain_recv)
    first.load_own()
    job.load_own()
    barrier(job.p)
    first.start()
    first.until(3)
    job.start()
    first.until(3.9)
    job.until(0)
    first.arrivals()
    n = n_square * 2 * n_line
    loads = {}
    loads[5] = pltpu.make_async_copy(w_refs[5], small, w_sem.at[5])
    loads[5].start()
    for i in (1, 2, 0, 3, 4):
        loads[i] = pltpu.make_async_copy(w_refs[i], w_in.at[i], w_sem.at[i])
        loads[i].start()
    tick = job.run
    few = lambda n: job.run(2)
    x = tokens_ref[...].astype(f32)
    scale1 = lax.rsqrt(jnp.mean(x * x, axis=-1, keepdims=True) + norm_eps)
    loads[5].wait()
    packed = small[...].reshape(D, 128)
    rows = nt(ones_where((128, 128), lambda i, j: i == j), packed)
    gains_ref[...] = jnp.concatenate([rows[34:36], jnp.zeros((6, D), f32)], axis=0)
    by_gate = nn(spots(D // n), packed).astype(bf16)
    pair = nt(ones_where((8, 128), lambda i, j: j == i + 32), by_gate)
    bias = pair[:1]
    hgain = pair[1:2]
    hgain_ref[...] = jnp.broadcast_to(hgain, (8, HEAD))
    lane = lax.broadcasted_iota(jnp.int32, (D, 128), 1)
    low_pad = jnp.where(lane < 16, packed.astype(f32), 0.0).astype(bf16)
    low_pad_ref[...] = low_pad
    up_pad = nn(by_gate, ones_where((128, 128), lambda i, j: (i == j + 16) & (j < 16))).astype(bf16)
    up_pad_ref[...] = up_pad
    normed = (x * scale1 * rows[34:35]).astype(bf16)
    normed_ref[...] = normed
    low_rank = nn(normed, low_pad).astype(bf16)
    logits = nt(low_rank, up_pad) + bias
    log_gate = (jnp.minimum(logits, 0.0) - jnp.log1p(jnp.exp(-jnp.abs(logits)))) * (1.0 / gate_norm)
    gate_ref[...] = log_gate
    moved = nn(low_rank, ones_where((128, 128), lambda i, j: (j == i + 16) & (i < 16)))
    lane = lax.broadcasted_iota(jnp.int32, (ROWS, 128), 1)
    rank_ref[...] = jnp.where(lane == 32, 1.0, moved).astype(bf16)
    tick(2)

    def project(i):
        loads[i].wait()
        return nn(normed, w_in[i].reshape(D, D))

    share = share_of(log_gate)
    through = decays(log_gate, sums_ref, decay_ref, tick)
    share_end = (decay_ref[LEVELS + 1] * share).astype(bf16)
    k_ref[...] = project(1).astype(bf16)
    tick(2)
    v_ref[...] = project(2).astype(bf16)
    tick(2)
    part_ref[0] = summaries(share_end, k_ref[...])
    part_ref[1] = summaries(share_end, v_ref[...])
    chain.step(0, through, part_ref)
    tick(2)
    q_ref[...] = project(0).astype(bf16)
    tick(2)
    a_ref[...] = products(q_ref[...], k_ref[...])
    chain.step(1, through, part_ref)
    tick(2)
    swish_ref[...] = project(3)
    tick(2)
    lower_scores(a_ref, share, decay_ref, masks_ref, scores_ref, few)
    for i in range(2, n_line):
        chain.step(i, through, part_ref)
        tick(4)
    before = decay_ref[LEVELS]
    scores = scores_ref[...] + before * nt(q_ref[...], wide(in_ref[0]))
    scores_ref[...] = scores
    chance = softmax_slots(SCALE * scores)
    mixing(chance, share, decay_ref, masks_ref, b_ref, few)
    carried = nn((chance * before).astype(bf16), wide(in_ref[1]))
    state_ref[...] = in_ref[...]
    b, v = b_ref[...], v_ref[...]
    for h in range(HEADS):
        at = slice(HEAD * h, HEAD * (h + 1))
        mixed = nn(of(b, h), of(v, h)) + of(carried, h)
        mixed_ref[:, at] = mixed
        head_scale = lax.rsqrt(jnp.mean(mixed * mixed, axis=-1, keepdims=True) + norm_eps)
        swish = swish_ref[:, at]
        gated_ref[:, at] = (mixed * head_scale * hgain * (swish * sigmoid(swish))).astype(bf16)
        tick(2)
    loads[4].wait()
    hidden = tokens_ref[...].astype(f32) + nn(gated_ref[...], w_in[4].reshape(D, D))
    hidden_ref[...] = hidden
    scale2 = lax.rsqrt(jnp.mean(hidden * hidden, axis=-1, keepdims=True) + norm_eps)
    normed2_ref[...] = (hidden * scale2 * gains_ref[1:2]).astype(bf16)
    job.arrivals()
    first.close()
    job.close()
    chain.finish()


VMEM_BLOCK = pl.BlockSpec(memory_space=pltpu.VMEM)
ANY_BLOCK = pl.BlockSpec(memory_space=pl.ANY)


def run_forward(tokens, sums, masks, mixer_shards, shards, n_square, n_line, collective_id):
    rows = tokens.shape[0]
    n = n_square * 2 * n_line
    every = [*mixer_shards, *shards]
    mixer_pieces = split_pieces(MIXER_PLAN + [(5, 0, 128, "a")], n_square)
    pieces = split_pieces(FFN_PLAN, n_square)
    shape = lambda dtype, *dims: jax.ShapeDtypeStruct(dims, dtype)
    full = lambda dtype: shape(dtype, rows, D)
    pair = pltpu.VMEM((ROWS, HEADS * ROWS), bf16)
    return pl.pallas_call(
        functools.partial(forward_kernel, mixer_pieces, pieces, len(mixer_shards), len(shards), n_square, n_line),
        out_shape=[full(bf16)] * 3
        + [full(f32)] * 2
        + [shape(bf16, 2, 256, HEAD), shape(f32, rows, 256)]
        + [full(bf16), full(f32), full(bf16), full(bf16)]
        + [shape(f32, rows, 256), shape(bf16, rows, 128), shape(f32, 8, D), shape(f32, 8, HEAD)]
        + [shape(bf16, 256, 128), shape(bf16, D, 128)]
        + [shape(bf16, n, *s.shape) for s in every],
        in_specs=[VMEM_BLOCK] * 3 + [ANY_BLOCK] * len(every),
        out_specs=[VMEM_BLOCK] * 17 + [ANY_BLOCK] * len(every),
        scratch_shapes=[
            pltpu.VMEM((5, n, D // n, D), bf16),
            pltpu.VMEM((n, D // n, 128), bf16),
            pltpu.VMEM((LEVELS + 2, ROWS, 256), f32),
            pair,
            pair,
        ]
        + chain_scratch()
        + [pltpu.SemaphoreType.DMA((6,))]
        + gather_sems(len(mixer_pieces), len(mixer_shards), n_square, n_line)
        + gather_sems(len(pieces), len(shards), n_square, n_line),
        compiler_params=pltpu.CompilerParams(
            collective_id=collective_id, has_side_effects=True, vmem_limit_bytes=60 << 20
        ),
        name="mixer_forward",
    )(tokens, sums, masks, *every)


def backward_kernel(pieces, n_ffn, n_square, n_line, *refs):
    (
        gh_ref, swish_ref, mixed_ref, hgain_ref, q_ref, k_ref, v_ref, gate_ref, sums_ref, masks_ref, back_masks_ref,
        state_ref, scores_ref, normed_ref, gated_ref, tokens_ref, gain1_ref, dgain2_ref, up_pad_ref, low_pad_ref, rank_ref,
    ) = refs[:21]
    w_refs, refs = refs[21:26], refs[26:]
    partial, refs = refs[:n_ffn], refs[n_ffn:]
    dw_refs, small_ref, dtok_ref, refs = refs[:5], refs[5], refs[6], refs[7:]
    reduced, refs = refs[:n_ffn], refs[n_ffn:]
    (
        gqkvs_ref, dgate_ref, w_buf, stage, decay_ref, a_ref, av_ref, at_ref, avt_ref, s_parts, d_parts,
        s_sum, d_sum, shares_ref, g_ref, in_ref, out_ref, chain_send, chain_recv, part_ref, w_sem, stage_sem,
    ) = refs[:22]
    refs = refs[22:]
    b_ref, bk_ref = a_ref, av_ref
    m = len(pieces)
    job = ReduceFromHbm(
        pieces, partial, refs[:m], refs[m : 2 * m], refs[2 * m : 3 * m], refs[3 * m], refs[3 * m + 1 :], n_square, n_line
    )
    chain = Chain(n_line, True, in_ref, out_ref, chain_send, chain_recv)

    def w_load(i):
        slot = {4: 0, 3: 1, 0: 0, 1: 1, 2: 0}[i]
        return pltpu.make_async_copy(w_refs[i], w_buf.at[slot], w_sem.at[slot]), w_buf.at[slot]

    def w_store(i):
        slot = {4: 0, 3: 1, 0: 0, 1: 1, 2: 0}[i]
        return pltpu.make_async_copy(stage.at[slot], dw_refs[i], stage_sem.at[slot])

    def weight(i, left, right, wait=None):
        slot = {4: 0, 3: 1, 0: 0, 1: 1, 2: 0}[i]
        if wait is not None:
            w_store(wait).wait()
        stage[slot] = tn(left, right).astype(bf16)
        w_store(i).start()

    w_load(4)[0].start()
    w_load(3)[0].start()
    job.load()
    barrier(job.p)
    job.start()
    job.loaded()
    tick = job.run
    few = job.run
    none = lambda n: None

    log_gate = gate_ref[...]
    share = share_of(log_gate)
    through = decays(log_gate, sums_ref, decay_ref, none)
    branch = gh_ref[...].astype(bf16)
    load, w = w_load(4)
    load.wait()
    tick(8)
    grad_gated = nt(branch, w[...]).astype(bf16)
    w_load(0)[0].start()
    gain = hgain_ref[:1]
    dhgain = jnp.zeros((1, HEAD), f32)
    for h in range(HEADS):
        at = slice(HEAD * h, HEAD * (h + 1))
        mixed, swish = mixed_ref[:, at], swish_ref[:, at]
        gg = of(grad_gated, h).astype(f32)
        sig = sigmoid(swish)
        head_scale = lax.rsqrt(jnp.mean(mixed * mixed, axis=-1, keepdims=True) + norm_eps)
        scaled = mixed * head_scale
        g_head = gg * (swish * sig)
        dhgain += jnp.sum(g_head * scaled, axis=0, keepdims=True)
        gqkvs_ref[1, :, at] = (
            gg * (scaled * gain) * (sig * (1.0 + swish * (1.0 - sig)))
        ).astype(bf16)
        u = g_head * gain
        g_ref[:, at] = (
            head_scale * (u - scaled * (head_scale * jnp.mean(u * mixed, axis=-1, keepdims=True)))
        ).astype(bf16)
        tick(3)
    q, k, v, g = q_ref[...], k_ref[...], v_ref[...], g_ref[...]
    before, after = decay_ref[LEVELS], decay_ref[LEVELS + 1]
    key_in, value_in = state_ref[0], state_ref[1]
    chance = softmax_slots(SCALE * scores_ref[...])
    av_ref[...] = products(g, v)
    lower_scores(av_ref, share, decay_ref, masks_ref, d_sum, none, d_parts)
    d_state = before * nt(g, wide(value_in))
    slope = d_sum[...] + d_state
    spread = SCALE * chance * (slope - head_sums(chance * slope))
    chance_before = (chance * before).astype(bf16)
    spread_before = (spread * before).astype(bf16)
    part_ref[0] = summaries(spread_before, q)
    part_ref[1] = summaries(chance_before, g)
    chain.step(0, through, part_ref)
    tick(12)
    weight(4, gated_ref[...], branch)
    load, w = w_load(3)
    load.wait()
    grad_swish = gqkvs_ref[1]
    dtok_ref[...] = nt(grad_swish, w[...])
    w_load(1)[0].start()
    tick(1)
    weight(3, normed_ref[...], grad_swish)
    tick(1)
    a_ref[...] = products(q, k)
    tick(1)
    at_ref[...] = products(k, q)
    tick(1)
    avt_ref[...] = products(v, g)
    lower_scores(a_ref, share, decay_ref, masks_ref, s_sum, none, s_parts)
    s_state = before * nt(q, wide(key_in))
    mixing(chance, share, decay_ref, masks_ref, b_ref, none)
    chain.step(1, through, part_ref)
    tick(8)
    mixing(spread, share, decay_ref, masks_ref, bk_ref, none)
    chain.step(2, through, part_ref)
    dgate_ref[...] = tn(sums_ref[LEVELS], (spread * s_state + chance * d_state).astype(bf16))
    diagonal = back_masks_ref[LEVELS]
    shares_ref[...] = nn(masked(at_ref[...], diagonal), tall(spread.astype(bf16))) + nn(
        masked(avt_ref[...], diagonal), tall(chance.astype(bf16))
    )

    for level in range(LEVELS):
        decay = decay_ref[level]
        mask = back_masks_ref[level]
        taken = decay * (
            nn(masked(at_ref[...], mask), tall((spread * decay).astype(bf16)))
            + nn(masked(avt_ref[...], mask), tall((chance * decay).astype(bf16)))
        )
        shares_ref[...] += taken
        given = spread * s_parts[level].astype(f32) + chance * d_parts[level].astype(f32)
        place = lax.broadcasted_iota(jnp.int32, (ROWS, 256), 0)
        upper = lax.bitwise_and(lax.shift_right_logical(place, level), 1) == 1
        both = jnp.where(upper, given, taken * share).astype(bf16)
        dgate_ref[...] += tn(sums_ref[level], both)
        if level >= 3:
            tick(2)
    for i in range(3, n_line):
        chain.step(i, through, part_ref)
    out_key, out_value = in_ref[0], in_ref[1]
    wide_key, wide_value = wide(out_key), wide(out_value)
    taken = after * (nt(k, wide_key) + nt(v, wide_value))
    shares = shares_ref[...] + taken
    kept = key_in.astype(f32) * out_key.astype(f32) + value_in.astype(f32) * out_value.astype(f32)
    high, low = split_low(kept * through)
    ones = jnp.ones((8, 256), bf16)
    kept_row = (nt(ones, high) + nt(ones, low))[:1]
    dgate = dgate_ref[...] + tn(sums_ref[LEVELS + 1], (taken * share).astype(bf16)) + kept_row
    dgate = dgate - jnp.exp(log_gate) * shares
    grad_logits = dgate * (1.0 / gate_norm) * share_of(gate_norm * log_gate)
    tick(2)
    end = (after * share).astype(bf16)
    q_state = nn(spread_before, wide(key_in))
    k_state = nn(end, wide_key)
    v_state = nn(end, wide_value)
    b, bk = b_ref[...], bk_ref[...]
    normed = normed_ref[...]
    for i in range(3):
        for h in range(HEADS):
            if i == 0:
                new = nn(of(bk, h), of(k, h)) + of(q_state, h)
            elif i == 1:
                new = tn(of(bk, h), of(q, h)) + of(k_state, h)
            else:
                new = tn(of(b, h), of(g, h)) + of(v_state, h)
            gqkvs_ref[0, :, HEAD * h : HEAD * (h + 1)] = new.astype(bf16)
        tick(1)
        grad = gqkvs_ref[0]
        weight(i, normed, grad, (4, 3, 0)[i])
        tick(1)
        load, w = w_load(i)
        load.wait()
        dtok_ref[...] += nt(grad, w[...])
        if i == 0:
            w_load(2)[0].start()
        tick(1)
    high, low = split_low(grad_logits)
    up_pad, rank = up_pad_ref[...], rank_ref[...]
    grad_low = (nn(high, up_pad) + nn(low, up_pad)).astype(bf16)
    g_normed = dtok_ref[...] + nt(grad_low, low_pad_ref[...])
    x = tokens_ref[...].astype(f32)
    scale1 = lax.rsqrt(jnp.mean(x * x, axis=-1, keepdims=True) + norm_eps)
    u = g_normed * gain1_ref[:1]
    dtok_ref[...] = (
        gh_ref[...] + scale1 * u - x * (scale1 * scale1 * scale1 * jnp.mean(u * x, axis=-1, keepdims=True))
    )
    tick(1)

    def at_lane(rows, which):
        lane = lax.broadcasted_iota(jnp.int32, (rows, 128), 1)
        return jnp.where(lane == which, 1.0, 0.0).astype(bf16)

    def column(row, which):
        row_high, row_low = split_low(row)
        place = lax.broadcasted_iota(jnp.int32, (8, row.shape[1]), 0)
        pair = jnp.where(place == 0, row_high.astype(f32), jnp.where(place == 1, row_low.astype(f32), 0.0)).astype(bf16)
        return tn(pair, at_lane(8, which))

    few = tn(high, rank) + tn(low, rank) + column(dhgain, 33)
    r = D // (n_square * 2 * n_line)
    gates = lax.broadcasted_iota(jnp.int32, (256, D), 0)
    rows = lax.broadcasted_iota(jnp.int32, (256, D), 1)
    per = r // 4
    spot = jnp.where((gates // per) * r + gates % per == rows, 1.0, 0.0).astype(bf16)
    few_high, few_low = split_low(few)
    total = tn(spot, few_high) + tn(spot, few_low)
    total = total + tn(normed, grad_low)
    scaled_high, scaled_low = split_low(g_normed * x * scale1)
    gain1_lane = at_lane(ROWS, 34)
    total = total + tn(scaled_high, gain1_lane) + tn(scaled_low, gain1_lane)
    small_ref[...] = total + column(dgain2_ref[:1], 35)
    tick(2)
    job.finish(reduced)
    chain.finish()
    w_store(1).wait()
    w_store(2).wait()


def run_backward(operands, weights, partial, n_square, n_line, collective_id):
    rows = operands[0].shape[0]
    shapes = [a.shape[1:] for a in partial]
    pieces = split_pieces(FFN_PLAN, n_square)
    views = [a.reshape((n_square, 2, n_line) + s) for a, s in zip(partial, shapes)]
    boxes = reduce_boxes(pieces, shapes, [a.dtype for a in partial], n_square, n_line)
    pair = pltpu.VMEM((ROWS, HEADS * ROWS), bf16)
    parts = pltpu.VMEM((LEVELS, ROWS, 256), bf16)
    flat = pltpu.VMEM((ROWS, 256), f32)
    two = pltpu.VMEM((2, D, D), bf16)
    return pl.pallas_call(
        functools.partial(backward_kernel, pieces, len(partial), n_square, n_line),
        out_shape=[jax.ShapeDtypeStruct((D, D), bf16)] * 5
        + [jax.ShapeDtypeStruct((D, 128), f32), jax.ShapeDtypeStruct((rows, D), f32)]
        + [jax.ShapeDtypeStruct(s, f32) for s in shapes],
        in_specs=[VMEM_BLOCK] * 21 + [ANY_BLOCK] * (5 + len(partial)),
        out_specs=[ANY_BLOCK] * 5 + [VMEM_BLOCK] * (2 + len(partial)),
        scratch_shapes=[pltpu.VMEM((2, rows, D), bf16), flat, two, two, pltpu.VMEM((LEVELS + 2, ROWS, 256), f32)]
        + [pair] * 4
        + [parts, parts, flat, flat, flat, pltpu.VMEM((ROWS, D), bf16)]
        + chain_scratch()
        + [pltpu.SemaphoreType.DMA((2,)), pltpu.SemaphoreType.DMA((2,))]
        + boxes * 3
        + [pltpu.SemaphoreType.DMA((len(pieces),))]
        + reduce_sems(len(pieces), n_square, n_line),
        compiler_params=pltpu.CompilerParams(
            collective_id=collective_id, has_side_effects=True, vmem_limit_bytes=63 << 20
        ),
        name="mixer_backward",
    )(*operands, *weights, *views)


FF_TILE = 256


def ffn_kernel(
    normed2_ref, hidden_ref, cot_ref, valid_ref, gain2_ref, wg_ref, wu_ref, wd_ref,
    output_ref, gh_ref, dgain2_ref, dg_ref, du_ref, dd_ref,
    low_ref, out_acc, back_acc,
):
    step = pl.program_id(0)

    @pl.when(step == 0)
    def _():
        low_ref[...] = (cot_ref[...].astype(f32) * valid_ref[...]).astype(bf16)
        out_acc[...] = jnp.zeros_like(out_acc)
        back_acc[...] = jnp.zeros_like(back_acc)

    x, low = normed2_ref[...], low_ref[...]
    wg, wu, wd = wg_ref[...], wu_ref[...], wd_ref[...]
    gate, up = nn(x, wg), nn(x, wu)
    inside = nt(low, wd).astype(bf16).astype(f32)
    sig = sigmoid(gate)
    act = gate * sig
    inner = (act * up).astype(bf16)
    g_gate = (inside * up * (sig * (1.0 + gate * (1.0 - sig)))).astype(bf16)
    g_up = (inside * act).astype(bf16)
    out_acc[...] += nn(inner, wd)
    dd_ref[...] = tn(inner, low).astype(bf16)
    dg_ref[...] = tn(x, g_gate).astype(bf16)
    du_ref[...] = tn(x, g_up).astype(bf16)
    back_acc[...] += nt(g_gate, wg) + nt(g_up, wu)

    @pl.when(step == pl.num_programs(0) - 1)
    def _():
        hidden, valid = hidden_ref[...], valid_ref[...]
        output_ref[...] = (valid * (hidden + out_acc[...])).astype(bf16)
        scale2 = lax.rsqrt(jnp.mean(hidden * hidden, axis=-1, keepdims=True) + norm_eps)
        back = back_acc[...]
        scaled = hidden * scale2
        dgain2_ref[...] = jnp.broadcast_to(jnp.sum(back * scaled, axis=0, keepdims=True), dgain2_ref.shape)
        u = back * gain2_ref[1:2]
        gh_ref[...] = cot_ref[...].astype(f32) * valid + scale2 * (
            u - scaled * (scale2 * jnp.mean(u * hidden, axis=-1, keepdims=True))
        )


def run_ffn(normed2, hidden, cotangent, valid, gain2, w_gate, w_up, w_down):
    rows = normed2.shape[0]
    ff = w_down.shape[0]
    tile = FF_TILE
    fixed = lambda *shape: pl.BlockSpec(shape, lambda j: (0, 0))
    cols = pl.BlockSpec((D, tile), lambda j: (0, j))
    down = pl.BlockSpec((tile, D), lambda j: (j, 0))
    return pl.pallas_call(
        ffn_kernel,
        grid=(ff // tile,),
        out_shape=[
            jax.ShapeDtypeStruct((rows, D), bf16),
            jax.ShapeDtypeStruct((rows, D), f32),
            jax.ShapeDtypeStruct((8, D), f32),
            jax.ShapeDtypeStruct((D, ff), bf16),
            jax.ShapeDtypeStruct((D, ff), bf16),
            jax.ShapeDtypeStruct((ff, D), bf16),
        ],
        in_specs=[fixed(rows, D)] * 3 + [fixed(rows, 1), fixed(8, D), cols, cols, down],
        out_specs=[fixed(rows, D), fixed(rows, D), fixed(8, D), cols, cols, down],
        scratch_shapes=[pltpu.VMEM((rows, D), bf16), pltpu.VMEM((rows, D), f32), pltpu.VMEM((rows, D), f32)],
        compiler_params=pltpu.CompilerParams(vmem_limit_bytes=40 << 20),
        name="ffn",
    )(normed2, hidden, cotangent, valid, gain2, w_gate, w_up, w_down)


def pack_small(low, up, bias, hgain, gain1, gain2, dtype):
    n, rows = low.shape[0], low.shape[1]
    fill = lambda a: jnp.pad(a.astype(dtype), ((0, 0), (0, rows - a.shape[1]), (0, 0)))
    parts = [fill(low), fill(up)] + [fill(a[:, :, None]) for a in (bias, hgain, gain1, gain2)]
    out = jnp.concatenate(parts, axis=2)
    return jnp.pad(out, ((0, 0), (0, 0), (0, 128 - out.shape[2])))


def unpack_small(packed):
    n, rows = packed.shape[0], packed.shape[1]
    few = rows // 4
    low = packed[:, :, :16].reshape(n * rows, 16)
    up = packed[:, :few, 16:32].reshape(n * few, 16)
    bias, hgain = (packed[:, :few, lane].reshape(n * few) for lane in (32, 33))
    gain1, gain2 = (packed[:, :, lane].reshape(n * rows) for lane in (34, 35))
    return low, up, bias, hgain, gain1, gain2


def per_device(
    n_square, n_line,
    tokens, cotangent, lengths, norm1_gain, w_query, w_key, w_value, w_gate_low, w_gate_up,
    gate_bias, head_gain, w_swish, w_out, norm2_gain, w_ffn_gate, w_ffn_up, w_ffn_down,
):
    count = tokens.shape[0]
    n = n_square * 2 * n_line
    small = pack_small(
        *(a[None] for a in (w_gate_low, w_gate_up, gate_bias, head_gain, norm1_gain, norm2_gain)), bf16
    )[0]
    sums, masks = level_constants(count)
    back_masks = np.ascontiguousarray(np.swapaxes(masks, 1, 2))
    position = lax.axis_index("shard") * count + jnp.arange(count, dtype=jnp.int32)
    valid = (position < lengths[0]).astype(f32)[:, None]
    (
        q, k, v, swish_pre, mixed, state, scores, gated, hidden, normed2, normed, log_gate, rank, gains, hgain, up_pad,
        low_pad, *got,
    ) = run_forward(
        tokens, sums, masks, [w_query, w_key, w_value, w_swish, w_out, small], [w_ffn_gate, w_ffn_up, w_ffn_down],
        n_square, n_line, 2,
    )
    weights = [g.reshape(D, D) for g in got[:5]]
    ffn_all = got[6:]
    w_g, w_u = (g.reshape(D, -1) for g in ffn_all[:2])
    w_d = ffn_all[2].reshape(-1, D)
    ff = w_d.shape[0]
    output, grad_hidden, d_gain2, d_gate, d_up_proj, d_down = run_ffn(
        normed2, hidden, cotangent, valid, gains, w_g, w_u, w_d
    )
    operands = [
        grad_hidden, swish_pre, mixed, hgain, q, k, v, log_gate, sums, masks, back_masks, state, scores,
        normed, gated, tokens, gains, d_gain2, up_pad, low_pad, rank,
    ]
    *dw, d_small, d_tokens, s_gate, s_up, s_down = run_backward(
        operands, weights,
        [d_gate.reshape(n, D // n, ff), d_up_proj.reshape(n, D // n, ff), d_down.reshape(n, ff // n, D)],
        n_square, n_line, 3,
    )
    s_q, s_k, s_v, s_swish, s_out, s_small = reduce_scatter(
        [a.reshape(n, D // n, -1) for a in (*dw, d_small)], MIXER_PLAN + [(5, 0, 128, "a")], n_square, n_line, 4
    )
    o_low, o_up, o_bias, o_hgain, o_gain1, o_gain2 = unpack_small(s_small[None])
    return (
        output, d_tokens, o_gain1,
        s_q, s_k, s_v,
        o_low, o_up, o_bias, o_hgain,
        s_swish, s_out, o_gain2,
        s_gate, s_up, s_down,
    )


def solution(mesh):
    rows, row = P(("dp", "shard"), None), P(("dp", "shard"))
    placed = (rows, rows, P("dp"), row, rows, rows, rows, rows, rows, row, row, rows, rows, row, rows, rows, rows)
    out = (rows, rows, row, rows, rows, rows, rows, rows, row, row, rows, rows, row, rows, rows, rows)
    return jax.shard_map(
        functools.partial(per_device, mesh.shape["dp"] // 2, mesh.shape["shard"]),
        mesh=mesh,
        in_specs=placed,
        out_specs=out,
        check_vma=False,
    )
```

```python
import functools

import jax
import jax.numpy as jnp
import numpy as np
from jax import lax
from jax.experimental import pallas as pl
from jax.experimental.pallas import tpu as pltpu
from jax.sharding import PartitionSpec as P

D = 1024
HEADS = 4
HEAD = 256
SLOTS = 64
norm_eps = 1e-06
gate_norm = 8.0
MESH = pl.DeviceIdType.MESH


class Place:
    def __init__(self, n_square, n_line):
        self.n_square, self.n_line = n_square, n_line
        dp = lax.axis_index("dp")
        self.z = lax.axis_index("shard")
        self.c = lax.rem(dp, 2)
        self.a = lax.div(dp, 2)

    def slot(self, k):
        out = 0
        for z in range(self.n_line):
            near = sorted(range(self.n_line), key=lambda other: (abs(other - z), other))
            out = out + jnp.where(self.z == z, near[k], 0)
        return out

    def device(self, a, c, z):
        return {"dp": a * 2 + c, "shard": z}

    def slab(self, a, c, z):
        return (a * 2 + c) * self.n_line + z


def flip(value, bits):
    for b in range(8):
        if bits >> b & 1:
            digit = lax.rem(lax.div(value, 1 << b), 2)
            value = value + (1 - 2 * digit) * (1 << b)
    return value


LINE = "line"
LATE_LINE = 3.5


class Tree:
    def __init__(self, order, n_line):
        self.slabs = [(0, 0)]
        self.up, self.down, self.time = {}, {(0, 0): []}, {(0, 0): 0}
        late = order[0] != LINE
        for stage, dim in enumerate(order):
            for m, k in list(self.slabs):
                steps = range(1, n_line) if dim == LINE else [dim]
                for step in steps:
                    child = (m, step) if dim == LINE else (m ^ step, k)
                    self.slabs.append(child)
                    self.up[child] = (dim, step, (m, k))
                    self.down[child] = []
                    self.down[(m, k)].append(child)
                    if dim == LINE:
                        self.time[child] = step + (n_line + 1 if late else 0)
                    else:
                        self.time[child] = self.time[(m, k)] + 1


def orders(n_square):
    bits = [1 << b for b in range((n_square - 1).bit_length())]
    return {"a": (LINE, *bits), "b": (LINE, *bits[::-1]), "c": (*bits[::-1], LINE)}


def split_pieces(plan, n_square):
    by_name = orders(n_square)
    return [(i, start, width, by_name[name]) for i, start, width, name in plan]


MIXER_PLAN = [
    (0, 0, 1024, "a"), (1, 0, 1024, "b"), (2, 0, 1024, "a"), (3, 0, 1024, "b"), (4, 512, 512, "a"), (4, 0, 512, "c"),
]
FFN_PLAN = [(0, 0, 2816, "a"), (1, 0, 2816, "b"), (2, 0, 384, "a"), (2, 384, 384, "b"), (2, 768, 256, "c")]
FFN_REDUCE_PLAN = [
    (0, 0, 2816, "a"), (1, 0, 2816, "b"), (2, 0, 384, "a"), (2, 384, 512, "b"), (2, 896, 128, "c"),
]


def barrier(place):
    sem = pltpu.get_barrier_semaphore()
    peers = [place.device(place.a, 1 - place.c, place.z)]
    bit = 1
    while bit < place.n_square:
        peers.append(place.device(flip(place.a, bit), place.c, place.z))
        bit *= 2
    for k in range(1, place.n_line):
        peers.append(place.device(place.a, place.c, flip(place.z, k)))
    for peer in peers:
        pl.semaphore_signal(sem, inc=1, device_id=peer, device_id_type=MESH)
    pl.semaphore_wait(sem, len(peers))


class Gather:
    def __init__(self, pieces, ins, outs, sems, n_square, n_line):
        self.pieces, self.ins, self.outs = pieces, ins, outs
        self.local_sem, self.net_send, self.net_recv, self.core_send, self.core_recv, self.line_send = sems
        self.n_square, self.n_line = n_square, n_line
        self.p = Place(n_square, n_line)
        self.own = [
            pltpu.make_async_copy(
                ins[i], outs[i].at[self.p.slab(self.p.a, self.p.c, self.p.z)], self.local_sem.at[i]
            )
            for i in range(len(ins))
        ]
        self.trees = [Tree(order, n_line) for i, start, width, order in pieces]
        events = [(tree.time[slab], q, slab, False) for q, tree in enumerate(self.trees) for slab in tree.slabs]
        for q, tree in enumerate(self.trees):
            if pieces[q][3][0] != LINE:
                events += [(LATE_LINE + 0.1 * j, q, slab, True) for j, slab in enumerate(tree.slabs) if slab[1] == 0]
        self.todo = sorted(events, key=lambda e: e[0])
        self.started = []
        self.places = [self.p.slot(k) for k in range(n_line)]

    def at(self, q, m, k, c=None):
        i, start, width, order = self.pieces[q]
        p = self.p
        z = self.places[k] if order[0] == LINE else flip(p.z, k)
        s = p.slab(flip(p.a, m), p.c if c is None else c, z)
        return self.outs[i].at[s, :, pl.ds(start, width)]

    def source(self, q, m, k):
        if m == 0 and k == 0:
            i, start, width, _ = self.pieces[q]
            return self.ins[i].at[:, pl.ds(start, width)]
        return self.at(q, m, k)

    def go(self, q, m, k, sems, index, peer):
        copy = pltpu.make_async_remote_copy(
            src_ref=self.source(q, m, k),
            dst_ref=self.at(q, m, k),
            send_sem=sems[0].at[index],
            recv_sem=sems[1].at[index],
            device_id=peer,
            device_id_type=MESH,
        )
        copy.start()
        self.started.append((None, copy))

    def along(self, q, k):
        p = self.p
        z = self.places[k]
        for way, (step, more) in enumerate(((1, (z <= p.z) & (p.z < self.n_line - 1)), (-1, (z >= p.z) & (p.z > 0)))):
            copy = pltpu.make_async_remote_copy(
                src_ref=self.source(q, 0, k),
                dst_ref=self.at(q, 0, k),
                send_sem=self.line_send.at[q, way, k],
                recv_sem=self.net_recv.at[q, 0, z],
                device_id=p.device(p.a, p.c, p.z + step),
                device_id_type=MESH,
            )
            pl.when(more)(copy.start)
            self.started.append((more, copy))

    def arrived(self, q, m, k, sems, c, place=None):
        p = self.p
        pltpu.make_async_remote_copy(
            src_ref=self.at(q, m, k, c),
            dst_ref=self.at(q, m, k, c),
            send_sem=sems[0].at[q, m, k],
            recv_sem=sems[1].at[q, m, k if place is None else place],
            device_id=p.device(p.a, 1 - p.c, p.z),
            device_id_type=MESH,
        ).wait_recv()

    def load_own(self):
        for copy in self.own:
            copy.start()

    def start(self):
        for q, tree in enumerate(self.trees):
            if self.pieces[q][3][0] == LINE:
                self.along(q, 0)

    def pass_on(self, q, slab, child):
        p = self.p
        dim, step, _ = self.trees[q].up[child]
        peer = p.device(p.a, p.c, flip(p.z, step)) if dim == LINE else p.device(flip(p.a, step), p.c, p.z)
        self.go(q, *slab, (self.net_send, self.net_recv), (q, *child), peer)

    def until(self, time):
        self.run(sum(e[0] <= time for e in self.todo))

    def run(self, n):
        p = self.p
        net, core = (self.net_send, self.net_recv), (self.core_send, self.core_recv)
        for time, q, slab, line in self.todo[:n]:
            tree = self.trees[q]
            first = self.pieces[q][3][0] == LINE
            if line:
                for child in tree.down[slab]:
                    if tree.up[child][0] == LINE:
                        self.pass_on(q, slab, child)
                continue
            if slab != (0, 0):
                lined = first and slab[0] == 0
                self.arrived(q, *slab, net, p.c, self.places[slab[1]] if lined else None)
                if lined:
                    self.along(q, slab[1])
            for child in tree.down[slab]:
                if tree.up[child][0] != LINE:
                    self.pass_on(q, slab, child)
            self.go(q, *slab, core, (q, *slab), p.device(p.a, 1 - p.c, p.z))
        self.todo = self.todo[n:]

    def arrivals(self):
        self.run(len(self.todo))
        for copy in self.own:
            copy.wait()
        for k in range(self.n_line):
            for q in range(len(self.pieces)):
                for m in range(self.n_square):
                    self.arrived(q, m, k, (self.core_send, self.core_recv), 1 - self.p.c)

    def close(self):
        for more, copy in self.started:
            if more is None:
                copy.wait_send()
            else:
                pl.when(more)(copy.wait_send)


def gather_sems(n_pieces, n_arrays, n_square, n_line):
    sem = pltpu.SemaphoreType.DMA((n_pieces, n_square, n_line))
    line = pltpu.SemaphoreType.DMA((n_pieces, 2, n_line))
    return [pltpu.SemaphoreType.DMA((n_arrays,)), sem, sem, sem, sem, line]


def add_into(ref, other):
    ref[...] = ref[...] + other[...]


class Reduce:
    def __init__(self, pieces, mine, theirs, peer_part, landed, sems, n_square, n_line):
        self.pieces, self.mine, self.theirs = pieces, mine, theirs
        self.peer_part, self.landed = peer_part, landed
        self.net_send, self.net_recv, self.core_send, self.core_recv = sems
        self.n_square, self.n_line = n_square, n_line
        self.p = Place(n_square, n_line)
        self.ks = list(range(n_line))[::-1]
        self.trees = [Tree(order, n_line) for i, start, width, order in pieces]
        events = [
            (-tree.time[slab], q, slab)
            for q, tree in enumerate(self.trees)
            for slab in tree.slabs[::-1]
        ]
        self.todo = sorted((e for e in events if e[2] != (0, 0)), key=lambda e: e[0])
        self.sent, self.have = [], set()

    def core(self, q, k):
        p = self.p
        return pltpu.make_async_remote_copy(
            src_ref=self.theirs(q, k),
            dst_ref=self.peer_part[q].at[:, flip(p.z, k)],
            send_sem=self.core_send.at[q, k],
            recv_sem=self.core_recv.at[q, k],
            device_id=p.device(p.a, 1 - p.c, p.z),
            device_id_type=MESH,
        )

    def net(self, q, slab):
        p = self.p
        m, k = slab
        dim, step, _ = self.trees[q].up[slab]
        peer = p.device(p.a, p.c, flip(p.z, step)) if dim == LINE else p.device(flip(p.a, step), p.c, p.z)
        return pltpu.make_async_remote_copy(
            src_ref=self.mine(q, flip(p.a, m), flip(p.z, k)),
            dst_ref=self.landed[q].at[m, k],
            send_sem=self.net_send.at[q, m, k],
            recv_sem=self.net_recv.at[q, m, k],
            device_id=peer,
            device_id_type=MESH,
        )

    def start(self, pieces=None):
        for q in range(len(self.pieces)) if pieces is None else pieces:
            for k in self.ks[:1] if self.pieces[q][3][0] == LINE else self.ks:
                self.core(q, k).start()

    def from_core(self, q, k):
        if (q, k) not in self.have:
            self.have.add((q, k))
            self.core(q, k).wait_recv()
            if k and self.pieces[q][3][0] == LINE:
                self.core(q, k - 1).start()

    def until(self, time):
        self.run(sum(e[0] <= time for e in self.todo))

    def run(self, n, pieces=None):
        p = self.p
        now = [e for e in self.todo if pieces is None or e[1] in pieces][:n]
        self.todo = [e for e in self.todo if e not in now]
        for time, q, slab in now:
            m, k = slab
            self.from_core(q, k)
            a, z = flip(p.a, m), flip(p.z, k)
            add_into(self.mine(q, a, z), self.peer_part[q].at[a, z])
            for child in self.trees[q].down[slab]:
                self.net(q, child).wait_recv()
                add_into(self.mine(q, a, z), self.landed[q].at[child])
            copy = self.net(q, slab)
            copy.start()
            self.sent.append(copy)

    def finish(self, outs):
        self.run(len(self.todo))
        p = self.p
        for q in range(len(self.pieces)):
            i, start, width, _ = self.pieces[q]
            self.from_core(q, 0)
            total = self.mine(q, p.a, p.z)[...].astype(jnp.float32)
            total = total + self.peer_part[q][p.a, p.z].astype(jnp.float32)
            for child in self.trees[q].down[(0, 0)]:
                self.net(q, child).wait_recv()
                total = total + self.landed[q][child].astype(jnp.float32)
            outs[i][:, pl.ds(start, width)] = total
        for copy in self.sent:
            copy.wait_send()
        for k in self.ks:
            for q in range(len(self.pieces)):
                self.core(q, k).wait_send()


def reduce_boxes(pieces, shapes, dtypes, n_square, n_line):
    return [
        pltpu.VMEM((n_square, n_line, shapes[i][0], width), dtypes[i]) for i, start, width, _ in pieces
    ]


def reduce_sems(n_pieces, n_square, n_line):
    sem = pltpu.SemaphoreType.DMA((n_pieces, n_square, n_line))
    core_sem = pltpu.SemaphoreType.DMA((n_pieces, n_line))
    return [sem, sem, core_sem, core_sem]


class ReduceFromHbm(Reduce):
    def __init__(self, pieces, ins, mine, peer_part, landed, local_sem, sems, n_square, n_line):
        p = Place(n_square, n_line)

        def columns(q):
            i, start, width, _ = pieces[q]
            return ins[i], pl.ds(start, width)

        def theirs(q, k):
            ref, cols = columns(q)
            return ref.at[:, 1 - p.c, flip(p.z, k), :, cols]

        super().__init__(pieces, lambda q, a, z: mine[q].at[a, z], theirs, peer_part, landed, sems, n_square, n_line)
        self.loads = []
        for q in range(len(pieces)):
            ref, cols = columns(q)
            self.loads.append(pltpu.make_async_copy(ref.at[:, p.c, :, :, cols], mine[q], local_sem.at[q]))

    def load(self):
        for copy in self.loads:
            copy.start()

    def loaded(self):
        for copy in self.loads:
            copy.wait()


def reduce_body(pieces, n_arrays, n_square, n_line, *refs):
    n = len(pieces)
    ins, outs, rest = refs[:n_arrays], refs[n_arrays : 2 * n_arrays], refs[2 * n_arrays :]
    job = ReduceFromHbm(
        pieces, ins, rest[:n], rest[n : 2 * n], rest[2 * n : 3 * n], rest[3 * n], rest[3 * n + 1 :], n_square, n_line
    )
    job.load()
    barrier(job.p)
    job.start()
    job.loaded()
    job.finish(outs)


def reduce_scatter(arrays, plan, n_square, n_line, collective_id):
    shapes = [a.shape[1:] for a in arrays]
    pieces = split_pieces(plan, n_square)
    views = [a.reshape((n_square, 2, n_line) + s) for a, s in zip(arrays, shapes)]
    any_space = pl.BlockSpec(memory_space=pl.ANY)
    boxes = reduce_boxes(pieces, shapes, [x.dtype for x in arrays], n_square, n_line)
    return pl.pallas_call(
        functools.partial(reduce_body, pieces, len(arrays), n_square, n_line),
        out_shape=[jax.ShapeDtypeStruct(s, jnp.float32) for s in shapes],
        in_specs=[any_space] * len(arrays),
        out_specs=[pl.BlockSpec(memory_space=pltpu.VMEM)] * len(arrays),
        scratch_shapes=boxes * 3
        + [pltpu.SemaphoreType.DMA((len(pieces),))]
        + reduce_sems(len(pieces), n_square, n_line),
        compiler_params=pltpu.CompilerParams(
            collective_id=collective_id, has_side_effects=True, vmem_limit_bytes=60 << 20
        ),
        name="reduce_grads",
    )(*views)


f32, bf16 = jnp.float32, jnp.bfloat16
ROWS = 256
LEVELS = 8


def level_constants(rows):
    t, i = np.arange(rows)[:, None], np.arange(rows)[None, :]
    sums, masks = [], []
    for level in range((rows - 1).bit_length()):
        same = (t >> (level + 1)) == (i >> (level + 1))
        upper_t, upper_i = (t >> level) & 1, (i >> level) & 1
        sums.append(
            (same & (upper_t == 1) & (upper_i == 1) & (i <= t))
            | (same & (upper_t == 0) & (upper_i == 0) & (i > t))
        )
        masks.append((t > i) & (((t ^ i) >> level) == 1))
    sums += [i <= t, i > t]
    masks.append(t == i)
    return np.stack(sums).astype(bf16), np.stack(masks).astype(bf16)


def nn(a, b):
    return lax.dot_general(a, b, (((1,), (0,)), ((), ())), preferred_element_type=f32)


def nt(a, b):
    return lax.dot_general(a, b, (((1,), (1,)), ((), ())), preferred_element_type=f32)


def tn(a, b):
    return lax.dot_general(a, b, (((0,), (0,)), ((), ())), preferred_element_type=f32)


def split_low(x):
    high = x.astype(bf16)
    return high, (x - high.astype(f32)).astype(bf16)


def head_of_lane(shape):
    return lax.broadcasted_iota(jnp.int32, shape, 1) // SLOTS


def tall(x):
    head = head_of_lane(x.shape)
    zero = jnp.zeros_like(x)
    return jnp.concatenate([jnp.where(head == h, x, zero) for h in range(HEADS)], axis=0)


def wide(state):
    head = lax.broadcasted_iota(jnp.int32, state.shape, 0) // SLOTS
    zero = jnp.zeros_like(state)
    return jnp.concatenate([jnp.where(head == h, state, zero) for h in range(HEADS)], axis=1)


def of(x, h):
    return x[:, HEAD * h : HEAD * (h + 1)]


def slots(h):
    return slice(SLOTS * h, SLOTS * (h + 1))


def products(a, b):
    return jnp.concatenate([nt(of(a, h), of(b, h)) for h in range(HEADS)], axis=1).astype(bf16)


def masked(a, mask):
    return a * jnp.concatenate([mask] * HEADS, axis=1)


def share_of(log_gate):
    small = -log_gate * (1.0 + log_gate * (0.5 + log_gate * (1.0 / 6.0)))
    return jnp.where(log_gate > -0.01, small, 1.0 - jnp.exp(log_gate))


def head_sums(x):
    ones = (head_of_lane((256, 256)) == lax.broadcasted_iota(jnp.int32, (256, 256), 0) // SLOTS)
    ones = jnp.where(ones, 1.0, 0.0).astype(bf16)
    high, low = split_low(x)
    return nn(high, ones) + nn(low, ones)


SCALE = 1.5 * HEAD ** (-0.25)


def softmax_slots(scores):
    head = head_of_lane(scores.shape)
    peak = jnp.zeros_like(scores)
    for h in range(HEADS):
        top = jnp.max(jnp.where(head == h, scores, -jnp.inf), axis=1, keepdims=True)
        peak = jnp.where(head == h, top, peak)
    power = jnp.exp(scores - peak)
    return power / head_sums(power)


def decays(log_gate, sums_ref, decay_ref, tick):
    high, low = split_low(log_gate)
    for level in range(LEVELS + 2):
        m = sums_ref[level]
        decay_ref[level] = jnp.exp(nn(m, high) + nn(m, low))
        if level % 2:
            tick(1)
    ones = jnp.ones((ROWS, 256), bf16)
    return jnp.exp(tn(high, ones) + tn(low, ones))


def summaries(share_end, rows):
    return jnp.concatenate([tn(share_end, of(rows, h))[slots(h)] for h in range(HEADS)], axis=0)


def lower_scores(a_ref, share, decay_ref, masks_ref, total_ref, tick, parts_ref=None):
    total_ref[...] = nn(masked(a_ref[...], masks_ref[LEVELS]), tall(share.astype(bf16)))
    for level in range(LEVELS):
        decay = decay_ref[level]
        part = decay * nn(
            masked(a_ref[...], masks_ref[level]), tall((decay * share).astype(bf16))
        )
        if parts_ref is not None:
            parts_ref[level] = part.astype(bf16)
        total_ref[...] += part
        tick(1)


def mixing(coefficient, share, decay_ref, masks_ref, out_ref, tick):
    def pairs(x, f, mask):
        return masked(nt(x.astype(bf16), tall(f.astype(bf16))).astype(bf16), mask)

    out_ref[...] = pairs(coefficient, share, masks_ref[LEVELS])
    for level in range(LEVELS):
        decay = decay_ref[level]
        out_ref[...] += pairs(coefficient * decay, decay * share, masks_ref[level])
        tick(1)


class Chain:
    def __init__(self, n_line, backward, in_ref, out_ref, send_sem, recv_sem):
        self.z = lax.axis_index("shard")
        self.turn = n_line - 1 - self.z if backward else self.z
        self.next = self.z - 1 if backward else self.z + 1
        self.n_line, self.in_ref, self.out_ref = n_line, in_ref, out_ref
        self.send_sem, self.recv_sem = send_sem, recv_sem

    def copy(self, part):
        half = (part // 2, pl.ds(128 * (part % 2), 128))
        return pltpu.make_async_remote_copy(
            src_ref=self.out_ref.at[half],
            dst_ref=self.in_ref.at[half],
            send_sem=self.send_sem.at[part],
            recv_sem=self.recv_sem.at[part],
            device_id={"dp": lax.axis_index("dp"), "shard": self.next},
            device_id_type=MESH,
        )

    def step(self, i, through, sums_ref):
        if i >= self.n_line:
            return

        @pl.when(self.turn == i)
        def _():
            for part in range(4):
                which, rows = part // 2, slice(128 * (part % 2), 128 * (part % 2) + 128)
                if i == 0:
                    self.in_ref[which, rows] = jnp.zeros((128, HEAD), bf16)
                    new = sums_ref[which, rows]
                else:
                    self.copy(part).wait_recv()
                    new = through[rows] * self.in_ref[which, rows].astype(f32) + sums_ref[which, rows]
                if i < self.n_line - 1:
                    self.out_ref[which, rows] = new.astype(bf16)
                    self.copy(part).start()

    def finish(self):
        @pl.when(self.turn < self.n_line - 1)
        def _():
            for part in range(4):
                self.copy(part).wait_send()


def chain_scratch():
    box = pltpu.VMEM((2, 256, HEAD), bf16)
    sem = pltpu.SemaphoreType.DMA((4,))
    return [box, box, sem, sem, pltpu.VMEM((2, 256, HEAD), f32)]


def sigmoid(x):
    return 1.0 / (1.0 + jnp.exp(-x))


def spots(r):
    gate = lax.broadcasted_iota(jnp.int32, (256, D), 0)
    row = lax.broadcasted_iota(jnp.int32, (256, D), 1)
    per = r // 4
    return jnp.where((gate // per) * r + gate % per == row, 1.0, 0.0).astype(bf16)


def ones_where(shape, condition):
    i = lax.broadcasted_iota(jnp.int32, shape, 0)
    j = lax.broadcasted_iota(jnp.int32, shape, 1)
    return jnp.where(condition(i, j), 1.0, 0.0).astype(bf16)


def forward_kernel(mixer_pieces, pieces, n_mixer, n_ffn, n_square, n_line, *refs):
    tokens_ref, sums_ref, masks_ref = refs[:3]
    mixer_shards, shards, refs = refs[3 : 3 + n_mixer], refs[3 + n_mixer : 3 + n_mixer + n_ffn], refs[3 + n_mixer + n_ffn :]
    (
        q_ref, k_ref, v_ref, swish_ref, mixed_ref, state_ref, scores_ref, gated_ref, hidden_ref, normed2_ref,
        normed_ref, gate_ref, rank_ref, gains_ref, hgain_ref, up_pad_ref, low_pad_ref,
    ) = refs[:17]
    refs = refs[17:]
    w_refs, gathered, refs = refs[:n_mixer], refs[n_mixer : n_mixer + n_ffn], refs[n_mixer + n_ffn :]
    w_in, small, decay_ref, a_ref, b_ref, in_ref, out_ref, chain_send, chain_recv, part_ref, w_sem = refs[:11]
    refs = refs[11:]
    first = Gather(mixer_pieces, mixer_shards, w_refs, refs[:6], n_square, n_line)
    job = Gather(pieces, shards, gathered, refs[6:], n_square, n_line)
    chain = Chain(n_line, False, in_ref, out_ref, chain_send, chain_recv)
    first.load_own()
    job.load_own()
    barrier(job.p)
    first.start()
    first.until(3)
    job.start()
    first.until(3.9)
    job.until(0)
    first.arrivals()
    n = n_square * 2 * n_line
    loads = {}
    loads[5] = pltpu.make_async_copy(w_refs[5], small, w_sem.at[5])
    loads[5].start()
    for i in (1, 2, 0, 3, 4):
        loads[i] = pltpu.make_async_copy(w_refs[i], w_in.at[i], w_sem.at[i])
        loads[i].start()
    tick = job.run
    few = job.run
    tick(10)
    x = tokens_ref[...].astype(f32)
    scale1 = lax.rsqrt(jnp.mean(x * x, axis=-1, keepdims=True) + norm_eps)
    loads[5].wait()
    packed = small[...].reshape(D, 128)
    rows = nt(ones_where((128, 128), lambda i, j: i == j), packed)
    gains_ref[...] = jnp.concatenate([rows[34:36], jnp.zeros((6, D), f32)], axis=0)
    by_gate = nn(spots(D // n), packed).astype(bf16)
    pair = nt(ones_where((8, 128), lambda i, j: j == i + 32), by_gate)
    bias = pair[:1]
    hgain = pair[1:2]
    hgain_ref[...] = jnp.broadcast_to(hgain, (8, HEAD))
    lane = lax.broadcasted_iota(jnp.int32, (D, 128), 1)
    low_pad = jnp.where(lane < 16, packed.astype(f32), 0.0).astype(bf16)
    low_pad_ref[...] = low_pad
    up_pad = nn(by_gate, ones_where((128, 128), lambda i, j: (i == j + 16) & (j < 16))).astype(bf16)
    up_pad_ref[...] = up_pad
    normed = (x * scale1 * rows[34:35]).astype(bf16)
    normed_ref[...] = normed
    low_rank = nn(normed, low_pad).astype(bf16)
    logits = nt(low_rank, up_pad) + bias
    log_gate = (jnp.minimum(logits, 0.0) - jnp.log1p(jnp.exp(-jnp.abs(logits)))) * (1.0 / gate_norm)
    gate_ref[...] = log_gate
    moved = nn(low_rank, ones_where((128, 128), lambda i, j: (j == i + 16) & (i < 16)))
    lane = lax.broadcasted_iota(jnp.int32, (ROWS, 128), 1)
    rank_ref[...] = jnp.where(lane == 32, 1.0, moved).astype(bf16)
    tick(2)

    def project(i):
        loads[i].wait()
        return nn(normed, w_in[i].reshape(D, D))

    share = share_of(log_gate)
    through = decays(log_gate, sums_ref, decay_ref, tick)
    share_end = (decay_ref[LEVELS + 1] * share).astype(bf16)
    k_ref[...] = project(1).astype(bf16)
    tick(2)
    v_ref[...] = project(2).astype(bf16)
    tick(2)
    part_ref[0] = summaries(share_end, k_ref[...])
    part_ref[1] = summaries(share_end, v_ref[...])
    chain.step(0, through, part_ref)
    tick(2)
    q_ref[...] = project(0).astype(bf16)
    tick(2)
    a_ref[...] = products(q_ref[...], k_ref[...])
    chain.step(1, through, part_ref)
    tick(2)
    swish_ref[...] = project(3)
    tick(2)
    lower_scores(a_ref, share, decay_ref, masks_ref, scores_ref, few)
    for i in range(2, n_line):
        chain.step(i, through, part_ref)
        tick(4)
    before = decay_ref[LEVELS]
    scores = scores_ref[...] + before * nt(q_ref[...], wide(in_ref[0]))
    scores_ref[...] = scores
    chance = softmax_slots(SCALE * scores)
    mixing(chance, share, decay_ref, masks_ref, b_ref, few)
    carried = nn((chance * before).astype(bf16), wide(in_ref[1]))
    state_ref[...] = in_ref[...]
    b, v = b_ref[...], v_ref[...]
    for h in range(HEADS):
        at = slice(HEAD * h, HEAD * (h + 1))
        mixed = nn(of(b, h), of(v, h)) + of(carried, h)
        mixed_ref[:, at] = mixed
        head_scale = lax.rsqrt(jnp.mean(mixed * mixed, axis=-1, keepdims=True) + norm_eps)
        swish = swish_ref[:, at]
        gated_ref[:, at] = (mixed * head_scale * hgain * (swish * sigmoid(swish))).astype(bf16)
        tick(2)
    loads[4].wait()
    hidden = tokens_ref[...].astype(f32) + nn(gated_ref[...], w_in[4].reshape(D, D))
    hidden_ref[...] = hidden
    scale2 = lax.rsqrt(jnp.mean(hidden * hidden, axis=-1, keepdims=True) + norm_eps)
    normed2_ref[...] = (hidden * scale2 * gains_ref[1:2]).astype(bf16)
    job.arrivals()
    first.close()
    job.close()
    chain.finish()


VMEM_BLOCK = pl.BlockSpec(memory_space=pltpu.VMEM)
ANY_BLOCK = pl.BlockSpec(memory_space=pl.ANY)


def run_forward(tokens, sums, masks, mixer_shards, shards, n_square, n_line, collective_id):
    rows = tokens.shape[0]
    n = n_square * 2 * n_line
    every = [*mixer_shards, *shards]
    mixer_pieces = split_pieces(MIXER_PLAN + [(5, 0, 128, "a")], n_square)
    pieces = split_pieces(FFN_PLAN, n_square)
    shape = lambda dtype, *dims: jax.ShapeDtypeStruct(dims, dtype)
    full = lambda dtype: shape(dtype, rows, D)
    pair = pltpu.VMEM((ROWS, HEADS * ROWS), bf16)
    return pl.pallas_call(
        functools.partial(forward_kernel, mixer_pieces, pieces, len(mixer_shards), len(shards), n_square, n_line),
        out_shape=[full(bf16)] * 3
        + [full(f32)] * 2
        + [shape(bf16, 2, 256, HEAD), shape(f32, rows, 256)]
        + [full(bf16), full(f32), full(bf16), full(bf16)]
        + [shape(f32, rows, 256), shape(bf16, rows, 128), shape(f32, 8, D), shape(f32, 8, HEAD)]
        + [shape(bf16, 256, 128), shape(bf16, D, 128)]
        + [shape(bf16, n, *s.shape) for s in every],
        in_specs=[VMEM_BLOCK] * 3 + [ANY_BLOCK] * len(every),
        out_specs=[VMEM_BLOCK] * 17 + [ANY_BLOCK] * len(every),
        scratch_shapes=[
            pltpu.VMEM((5, n, D // n, D), bf16),
            pltpu.VMEM((n, D // n, 128), bf16),
            pltpu.VMEM((LEVELS + 2, ROWS, 256), f32),
            pair,
            pair,
        ]
        + chain_scratch()
        + [pltpu.SemaphoreType.DMA((6,))]
        + gather_sems(len(mixer_pieces), len(mixer_shards), n_square, n_line)
        + gather_sems(len(pieces), len(shards), n_square, n_line),
        compiler_params=pltpu.CompilerParams(
            collective_id=collective_id, has_side_effects=True, vmem_limit_bytes=60 << 20
        ),
        name="mixer_forward",
    )(tokens, sums, masks, *every)


def backward_kernel(pieces, n_ffn, n_square, n_line, *refs):
    (
        gh_ref, swish_ref, mixed_ref, hgain_ref, q_ref, k_ref, v_ref, gate_ref, sums_ref, masks_ref, back_masks_ref,
        state_ref, scores_ref, normed_ref, gated_ref, tokens_ref, gain1_ref, dgain2_ref, up_pad_ref, low_pad_ref, rank_ref,
    ) = refs[:21]
    w_refs, refs = refs[21:26], refs[26:]
    partial, refs = refs[:n_ffn], refs[n_ffn:]
    dw_refs, small_ref, dtok_ref, refs = refs[:5], refs[5], refs[6], refs[7:]
    reduced, refs = refs[:n_ffn], refs[n_ffn:]
    (
        gqkvs_ref, dgate_ref, w_buf, stage, decay_ref, a_ref, av_ref, at_ref, avt_ref, s_parts, d_parts,
        s_sum, d_sum, shares_ref, g_ref, in_ref, out_ref, chain_send, chain_recv, part_ref, w_sem, stage_sem,
    ) = refs[:22]
    refs = refs[22:]
    b_ref, bk_ref = a_ref, av_ref
    m = len(pieces)
    job = ReduceFromHbm(
        pieces, partial, refs[:m], refs[m : 2 * m], refs[2 * m : 3 * m], refs[3 * m], refs[3 * m + 1 :], n_square, n_line
    )
    chain = Chain(n_line, True, in_ref, out_ref, chain_send, chain_recv)

    def w_load(i):
        slot = {4: 0, 3: 1, 0: 0, 1: 1, 2: 0}[i]
        return pltpu.make_async_copy(w_refs[i], w_buf.at[slot], w_sem.at[slot]), w_buf.at[slot]

    def w_store(i):
        slot = {4: 0, 3: 1, 0: 0, 1: 1, 2: 0}[i]
        return pltpu.make_async_copy(stage.at[slot], dw_refs[i], stage_sem.at[slot])

    def weight(i, left, right, wait=None):
        slot = {4: 0, 3: 1, 0: 0, 1: 1, 2: 0}[i]
        if wait is not None:
            w_store(wait).wait()
        stage[slot] = tn(left, right).astype(bf16)
        w_store(i).start()

    w_load(4)[0].start()
    w_load(3)[0].start()
    job.load()
    barrier(job.p)
    job.start()
    job.loaded()
    tick = job.run
    few = job.run
    none = lambda n: None

    log_gate = gate_ref[...]
    share = share_of(log_gate)
    through = decays(log_gate, sums_ref, decay_ref, none)
    branch = gh_ref[...].astype(bf16)
    load, w = w_load(4)
    load.wait()
    tick(8)
    grad_gated = nt(branch, w[...]).astype(bf16)
    w_load(0)[0].start()
    gain = hgain_ref[:1]
    dhgain = jnp.zeros((1, HEAD), f32)
    for h in range(HEADS):
        at = slice(HEAD * h, HEAD * (h + 1))
        mixed, swish = mixed_ref[:, at], swish_ref[:, at]
        gg = of(grad_gated, h).astype(f32)
        sig = sigmoid(swish)
        head_scale = lax.rsqrt(jnp.mean(mixed * mixed, axis=-1, keepdims=True) + norm_eps)
        scaled = mixed * head_scale
        g_head = gg * (swish * sig)
        dhgain += jnp.sum(g_head * scaled, axis=0, keepdims=True)
        gqkvs_ref[1, :, at] = (
            gg * (scaled * gain) * (sig * (1.0 + swish * (1.0 - sig)))
        ).astype(bf16)
        u = g_head * gain
        g_ref[:, at] = (
            head_scale * (u - scaled * (head_scale * jnp.mean(u * mixed, axis=-1, keepdims=True)))
        ).astype(bf16)
        tick(3)
    q, k, v, g = q_ref[...], k_ref[...], v_ref[...], g_ref[...]
    before, after = decay_ref[LEVELS], decay_ref[LEVELS + 1]
    key_in, value_in = state_ref[0], state_ref[1]
    chance = softmax_slots(SCALE * scores_ref[...])
    av_ref[...] = products(g, v)
    lower_scores(av_ref, share, decay_ref, masks_ref, d_sum, none, d_parts)
    d_state = before * nt(g, wide(value_in))
    slope = d_sum[...] + d_state
    spread = SCALE * chance * (slope - head_sums(chance * slope))
    chance_before = (chance * before).astype(bf16)
    spread_before = (spread * before).astype(bf16)
    part_ref[0] = summaries(spread_before, q)
    part_ref[1] = summaries(chance_before, g)
    chain.step(0, through, part_ref)
    tick(4)
    weight(4, gated_ref[...], branch)
    load, w = w_load(3)
    load.wait()
    grad_swish = gqkvs_ref[1]
    dtok_ref[...] = nt(grad_swish, w[...])
    w_load(1)[0].start()
    tick(1)
    weight(3, normed_ref[...], grad_swish)
    tick(1)
    chain.step(1, through, part_ref)
    a_ref[...] = products(q, k)
    tick(1)
    at_ref[...] = products(k, q)
    tick(1)
    avt_ref[...] = products(v, g)
    tick(8)
    lower_scores(a_ref, share, decay_ref, masks_ref, s_sum, none, s_parts)
    s_state = before * nt(q, wide(key_in))
    mixing(chance, share, decay_ref, masks_ref, b_ref, none)
    tick(8)
    mixing(spread, share, decay_ref, masks_ref, bk_ref, none)
    dgate_ref[...] = tn(sums_ref[LEVELS], (spread * s_state + chance * d_state).astype(bf16))
    diagonal = back_masks_ref[LEVELS]
    shares_ref[...] = nn(masked(at_ref[...], diagonal), tall(spread.astype(bf16))) + nn(
        masked(avt_ref[...], diagonal), tall(chance.astype(bf16))
    )

    for level in range(LEVELS):
        decay = decay_ref[level]
        mask = back_masks_ref[level]
        taken = decay * (
            nn(masked(at_ref[...], mask), tall((spread * decay).astype(bf16)))
            + nn(masked(avt_ref[...], mask), tall((chance * decay).astype(bf16)))
        )
        shares_ref[...] += taken
        given = spread * s_parts[level].astype(f32) + chance * d_parts[level].astype(f32)
        place = lax.broadcasted_iota(jnp.int32, (ROWS, 256), 0)
        upper = lax.bitwise_and(lax.shift_right_logical(place, level), 1) == 1
        both = jnp.where(upper, given, taken * share).astype(bf16)
        dgate_ref[...] += tn(sums_ref[level], both)
        if level >= 3:
            tick(2)
    q_state = nn(spread_before, wide(key_in))
    b, bk = b_ref[...], bk_ref[...]
    normed = normed_ref[...]

    def finish_rows(i, new_of):
        for h in range(HEADS):
            gqkvs_ref[0, :, HEAD * h : HEAD * (h + 1)] = new_of(h).astype(bf16)
        tick(1)
        grad = gqkvs_ref[0]
        weight(i, normed, grad, (4, 3, 0)[i])
        tick(1)
        load, w = w_load(i)
        load.wait()
        dtok_ref[...] += nt(grad, w[...])
        if i == 0:
            w_load(2)[0].start()
        tick(1)

    finish_rows(0, lambda h: nn(of(bk, h), of(k, h)) + of(q_state, h))
    job.until(-3)
    chain.step(2, through, part_ref)
    job.until(-2)
    for i in range(3, n_line):
        chain.step(i, through, part_ref)
    out_key, out_value = in_ref[0], in_ref[1]
    wide_key, wide_value = wide(out_key), wide(out_value)
    taken = after * (nt(k, wide_key) + nt(v, wide_value))
    shares = shares_ref[...] + taken
    kept = key_in.astype(f32) * out_key.astype(f32) + value_in.astype(f32) * out_value.astype(f32)
    high, low = split_low(kept * through)
    ones = jnp.ones((8, 256), bf16)
    kept_row = (nt(ones, high) + nt(ones, low))[:1]
    dgate = dgate_ref[...] + tn(sums_ref[LEVELS + 1], (taken * share).astype(bf16)) + kept_row
    dgate = dgate - jnp.exp(log_gate) * shares
    grad_logits = dgate * (1.0 / gate_norm) * share_of(gate_norm * log_gate)
    tick(2)
    end = (after * share).astype(bf16)
    k_state = nn(end, wide_key)
    v_state = nn(end, wide_value)
    finish_rows(1, lambda h: tn(of(bk, h), of(q, h)) + of(k_state, h))
    finish_rows(2, lambda h: tn(of(b, h), of(g, h)) + of(v_state, h))
    high, low = split_low(grad_logits)
    up_pad, rank = up_pad_ref[...], rank_ref[...]
    grad_low = (nn(high, up_pad) + nn(low, up_pad)).astype(bf16)
    g_normed = dtok_ref[...] + nt(grad_low, low_pad_ref[...])
    x = tokens_ref[...].astype(f32)
    scale1 = lax.rsqrt(jnp.mean(x * x, axis=-1, keepdims=True) + norm_eps)
    u = g_normed * gain1_ref[:1]
    dtok_ref[...] = (
        gh_ref[...] + scale1 * u - x * (scale1 * scale1 * scale1 * jnp.mean(u * x, axis=-1, keepdims=True))
    )
    tick(1)

    def at_lane(rows, which):
        lane = lax.broadcasted_iota(jnp.int32, (rows, 128), 1)
        return jnp.where(lane == which, 1.0, 0.0).astype(bf16)

    def column(row, which):
        row_high, row_low = split_low(row)
        place = lax.broadcasted_iota(jnp.int32, (8, row.shape[1]), 0)
        pair = jnp.where(place == 0, row_high.astype(f32), jnp.where(place == 1, row_low.astype(f32), 0.0)).astype(bf16)
        return tn(pair, at_lane(8, which))

    few = tn(high, rank) + tn(low, rank) + column(dhgain, 33)
    r = D // (n_square * 2 * n_line)
    gates = lax.broadcasted_iota(jnp.int32, (256, D), 0)
    rows = lax.broadcasted_iota(jnp.int32, (256, D), 1)
    per = r // 4
    spot = jnp.where((gates // per) * r + gates % per == rows, 1.0, 0.0).astype(bf16)
    few_high, few_low = split_low(few)
    total = tn(spot, few_high) + tn(spot, few_low)
    total = total + tn(normed, grad_low)
    scaled_high, scaled_low = split_low(g_normed * x * scale1)
    gain1_lane = at_lane(ROWS, 34)
    total = total + tn(scaled_high, gain1_lane) + tn(scaled_low, gain1_lane)
    small_ref[...] = total + column(dgain2_ref[:1], 35)
    tick(2)
    job.finish(reduced)
    chain.finish()
    w_store(1).wait()
    w_store(2).wait()


def run_backward(operands, weights, partial, n_square, n_line, collective_id):
    rows = operands[0].shape[0]
    shapes = [a.shape[1:] for a in partial]
    pieces = split_pieces(FFN_REDUCE_PLAN, n_square)
    views = [a.reshape((n_square, 2, n_line) + s) for a, s in zip(partial, shapes)]
    boxes = reduce_boxes(pieces, shapes, [a.dtype for a in partial], n_square, n_line)
    pair = pltpu.VMEM((ROWS, HEADS * ROWS), bf16)
    parts = pltpu.VMEM((LEVELS, ROWS, 256), bf16)
    flat = pltpu.VMEM((ROWS, 256), f32)
    two = pltpu.VMEM((2, D, D), bf16)
    return pl.pallas_call(
        functools.partial(backward_kernel, pieces, len(partial), n_square, n_line),
        out_shape=[jax.ShapeDtypeStruct((D, D), bf16)] * 5
        + [jax.ShapeDtypeStruct((D, 128), f32), jax.ShapeDtypeStruct((rows, D), f32)]
        + [jax.ShapeDtypeStruct(s, f32) for s in shapes],
        in_specs=[VMEM_BLOCK] * 21 + [ANY_BLOCK] * (5 + len(partial)),
        out_specs=[ANY_BLOCK] * 5 + [VMEM_BLOCK] * (2 + len(partial)),
        scratch_shapes=[pltpu.VMEM((2, rows, D), bf16), flat, two, two, pltpu.VMEM((LEVELS + 2, ROWS, 256), f32)]
        + [pair] * 4
        + [parts, parts, flat, flat, flat, pltpu.VMEM((ROWS, D), bf16)]
        + chain_scratch()
        + [pltpu.SemaphoreType.DMA((2,)), pltpu.SemaphoreType.DMA((2,))]
        + boxes * 3
        + [pltpu.SemaphoreType.DMA((len(pieces),))]
        + reduce_sems(len(pieces), n_square, n_line),
        compiler_params=pltpu.CompilerParams(
            collective_id=collective_id, has_side_effects=True, vmem_limit_bytes=63 << 20
        ),
        name="mixer_backward",
    )(*operands, *weights, *views)


FF_TILE = 256


def ffn_kernel(
    normed2_ref, hidden_ref, cot_ref, valid_ref, gain2_ref, wg_ref, wu_ref, wd_ref,
    output_ref, gh_ref, dgain2_ref, dg_ref, du_ref, dd_ref,
    low_ref, out_acc, back_acc,
):
    step = pl.program_id(0)

    @pl.when(step == 0)
    def _():
        low_ref[...] = (cot_ref[...].astype(f32) * valid_ref[...]).astype(bf16)
        out_acc[...] = jnp.zeros_like(out_acc)
        back_acc[...] = jnp.zeros_like(back_acc)

    x, low = normed2_ref[...], low_ref[...]
    wg, wu, wd = wg_ref[...], wu_ref[...], wd_ref[...]
    gate, up = nn(x, wg), nn(x, wu)
    inside = nt(low, wd).astype(bf16).astype(f32)
    sig = sigmoid(gate)
    act = gate * sig
    inner = (act * up).astype(bf16)
    g_gate = (inside * up * (sig * (1.0 + gate * (1.0 - sig)))).astype(bf16)
    g_up = (inside * act).astype(bf16)
    out_acc[...] += nn(inner, wd)
    dd_ref[...] = tn(inner, low).astype(bf16)
    dg_ref[...] = tn(x, g_gate).astype(bf16)
    du_ref[...] = tn(x, g_up).astype(bf16)
    back_acc[...] += nt(g_gate, wg) + nt(g_up, wu)

    @pl.when(step == pl.num_programs(0) - 1)
    def _():
        hidden, valid = hidden_ref[...], valid_ref[...]
        output_ref[...] = (valid * (hidden + out_acc[...])).astype(bf16)
        scale2 = lax.rsqrt(jnp.mean(hidden * hidden, axis=-1, keepdims=True) + norm_eps)
        back = back_acc[...]
        scaled = hidden * scale2
        dgain2_ref[...] = jnp.broadcast_to(jnp.sum(back * scaled, axis=0, keepdims=True), dgain2_ref.shape)
        u = back * gain2_ref[1:2]
        gh_ref[...] = cot_ref[...].astype(f32) * valid + scale2 * (
            u - scaled * (scale2 * jnp.mean(u * hidden, axis=-1, keepdims=True))
        )


def run_ffn(normed2, hidden, cotangent, valid, gain2, w_gate, w_up, w_down):
    rows = normed2.shape[0]
    ff = w_down.shape[0]
    tile = FF_TILE
    fixed = lambda *shape: pl.BlockSpec(shape, lambda j: (0, 0))
    cols = pl.BlockSpec((D, tile), lambda j: (0, j))
    down = pl.BlockSpec((tile, D), lambda j: (j, 0))
    return pl.pallas_call(
        ffn_kernel,
        grid=(ff // tile,),
        out_shape=[
            jax.ShapeDtypeStruct((rows, D), bf16),
            jax.ShapeDtypeStruct((rows, D), f32),
            jax.ShapeDtypeStruct((8, D), f32),
            jax.ShapeDtypeStruct((D, ff), bf16),
            jax.ShapeDtypeStruct((D, ff), bf16),
            jax.ShapeDtypeStruct((ff, D), bf16),
        ],
        in_specs=[fixed(rows, D)] * 3 + [fixed(rows, 1), fixed(8, D), cols, cols, down],
        out_specs=[fixed(rows, D), fixed(rows, D), fixed(8, D), cols, cols, down],
        scratch_shapes=[pltpu.VMEM((rows, D), bf16), pltpu.VMEM((rows, D), f32), pltpu.VMEM((rows, D), f32)],
        compiler_params=pltpu.CompilerParams(vmem_limit_bytes=40 << 20),
        name="ffn",
    )(normed2, hidden, cotangent, valid, gain2, w_gate, w_up, w_down)


def pack_small(low, up, bias, hgain, gain1, gain2, dtype):
    n, rows = low.shape[0], low.shape[1]
    fill = lambda a: jnp.pad(a.astype(dtype), ((0, 0), (0, rows - a.shape[1]), (0, 0)))
    parts = [fill(low), fill(up)] + [fill(a[:, :, None]) for a in (bias, hgain, gain1, gain2)]
    out = jnp.concatenate(parts, axis=2)
    return jnp.pad(out, ((0, 0), (0, 0), (0, 128 - out.shape[2])))


def unpack_small(packed):
    n, rows = packed.shape[0], packed.shape[1]
    few = rows // 4
    low = packed[:, :, :16].reshape(n * rows, 16)
    up = packed[:, :few, 16:32].reshape(n * few, 16)
    bias, hgain = (packed[:, :few, lane].reshape(n * few) for lane in (32, 33))
    gain1, gain2 = (packed[:, :, lane].reshape(n * rows) for lane in (34, 35))
    return low, up, bias, hgain, gain1, gain2


def per_device(
    n_square, n_line,
    tokens, cotangent, lengths, norm1_gain, w_query, w_key, w_value, w_gate_low, w_gate_up,
    gate_bias, head_gain, w_swish, w_out, norm2_gain, w_ffn_gate, w_ffn_up, w_ffn_down,
):
    count = tokens.shape[0]
    n = n_square * 2 * n_line
    small = pack_small(
        *(a[None] for a in (w_gate_low, w_gate_up, gate_bias, head_gain, norm1_gain, norm2_gain)), bf16
    )[0]
    sums, masks = level_constants(count)
    back_masks = np.ascontiguousarray(np.swapaxes(masks, 1, 2))
    position = lax.axis_index("shard") * count + jnp.arange(count, dtype=jnp.int32)
    valid = (position < lengths[0]).astype(f32)[:, None]
    (
        q, k, v, swish_pre, mixed, state, scores, gated, hidden, normed2, normed, log_gate, rank, gains, hgain, up_pad,
        low_pad, *got,
    ) = run_forward(
        tokens, sums, masks, [w_query, w_key, w_value, w_swish, w_out, small], [w_ffn_gate, w_ffn_up, w_ffn_down],
        n_square, n_line, 2,
    )
    weights = [g.reshape(D, D) for g in got[:5]]
    ffn_all = got[6:]
    w_g, w_u = (g.reshape(D, -1) for g in ffn_all[:2])
    w_d = ffn_all[2].reshape(-1, D)
    ff = w_d.shape[0]
    output, grad_hidden, d_gain2, d_gate, d_up_proj, d_down = run_ffn(
        normed2, hidden, cotangent, valid, gains, w_g, w_u, w_d
    )
    operands = [
        grad_hidden, swish_pre, mixed, hgain, q, k, v, log_gate, sums, masks, back_masks, state, scores,
        normed, gated, tokens, gains, d_gain2, up_pad, low_pad, rank,
    ]
    *dw, d_small, d_tokens, s_gate, s_up, s_down = run_backward(
        operands, weights,
        [d_gate.reshape(n, D // n, ff), d_up_proj.reshape(n, D // n, ff), d_down.reshape(n, ff // n, D)],
        n_square, n_line, 3,
    )
    s_q, s_k, s_v, s_swish, s_out, s_small = reduce_scatter(
        [a.reshape(n, D // n, -1) for a in (*dw, d_small)], MIXER_PLAN + [(5, 0, 128, "a")], n_square, n_line, 4
    )
    o_low, o_up, o_bias, o_hgain, o_gain1, o_gain2 = unpack_small(s_small[None])
    return (
        output, d_tokens, o_gain1,
        s_q, s_k, s_v,
        o_low, o_up, o_bias, o_hgain,
        s_swish, s_out, o_gain2,
        s_gate, s_up, s_down,
    )


def solution(mesh):
    rows, row = P(("dp", "shard"), None), P(("dp", "shard"))
    placed = (rows, rows, P("dp"), row, rows, rows, rows, rows, rows, row, row, rows, rows, row, rows, rows, rows)
    out = (rows, rows, row, rows, rows, rows, rows, rows, row, row, rows, rows, row, rows, rows, rows)
    return jax.shard_map(
        functools.partial(per_device, mesh.shape["dp"] // 2, mesh.shape["shard"]),
        mesh=mesh,
        in_specs=placed,
        out_specs=out,
        check_vma=False,
    )
```

```python
import functools

import jax
import jax.numpy as jnp
import numpy as np
from jax import lax
from jax.experimental import pallas as pl
from jax.experimental.pallas import tpu as pltpu
from jax.sharding import PartitionSpec as P

D = 1024
HEADS = 4
HEAD = 256
SLOTS = 64
norm_eps = 1e-06
gate_norm = 8.0
MESH = pl.DeviceIdType.MESH


class Place:
    def __init__(self, n_square, n_line):
        self.n_square, self.n_line = n_square, n_line
        dp = lax.axis_index("dp")
        self.z = lax.axis_index("shard")
        self.c = lax.rem(dp, 2)
        self.a = lax.div(dp, 2)

    def slot(self, k):
        out = 0
        for z in range(self.n_line):
            near = sorted(range(self.n_line), key=lambda other: (abs(other - z), other))
            out = out + jnp.where(self.z == z, near[k], 0)
        return out

    def device(self, a, c, z):
        return {"dp": a * 2 + c, "shard": z}

    def slab(self, a, c, z):
        return (a * 2 + c) * self.n_line + z


def flip(value, bits):
    for b in range(8):
        if bits >> b & 1:
            digit = lax.rem(lax.div(value, 1 << b), 2)
            value = value + (1 - 2 * digit) * (1 << b)
    return value


LINE = "line"
LATE_LINE = 3.5


class Tree:
    def __init__(self, order, n_line):
        self.slabs = [(0, 0)]
        self.up, self.down, self.time = {}, {(0, 0): []}, {(0, 0): 0}
        late = order[0] != LINE
        for stage, dim in enumerate(order):
            for m, k in list(self.slabs):
                steps = range(1, n_line) if dim == LINE else [dim]
                for step in steps:
                    child = (m, step) if dim == LINE else (m ^ step, k)
                    self.slabs.append(child)
                    self.up[child] = (dim, step, (m, k))
                    self.down[child] = []
                    self.down[(m, k)].append(child)
                    if dim == LINE:
                        self.time[child] = step + (n_line + 1 if late else 0)
                    else:
                        self.time[child] = self.time[(m, k)] + 1


def orders(n_square):
    bits = [1 << b for b in range((n_square - 1).bit_length())]
    return {"a": (LINE, *bits), "b": (LINE, *bits[::-1]), "c": (*bits[::-1], LINE)}


def split_pieces(plan, n_square):
    by_name = orders(n_square)
    return [(i, start, width, by_name[name]) for i, start, width, name in plan]


MIXER_PLAN = [
    (0, 0, 1024, "a"), (1, 0, 1024, "b"), (2, 0, 1024, "a"), (3, 0, 1024, "b"), (4, 512, 512, "a"), (4, 0, 512, "c"),
]
FFN_PLAN = [(0, 0, 2816, "a"), (1, 0, 2816, "b"), (2, 0, 384, "a"), (2, 384, 384, "b"), (2, 768, 256, "c")]
MIXER_REDUCE_PLAN = [
    (0, 0, 1024, "a"), (1, 0, 1024, "b"), (2, 0, 1024, "a"), (3, 0, 1024, "b"),
    (4, 256, 384, "a"), (4, 640, 384, "b"), (4, 0, 256, "c"),
]
FFN_REDUCE_PLAN = [
    (0, 0, 2816, "a"), (1, 0, 2816, "b"), (2, 0, 384, "a"), (2, 384, 512, "b"), (2, 896, 128, "c"),
]


def barrier(place):
    sem = pltpu.get_barrier_semaphore()
    peers = [place.device(place.a, 1 - place.c, place.z)]
    bit = 1
    while bit < place.n_square:
        peers.append(place.device(flip(place.a, bit), place.c, place.z))
        bit *= 2
    for k in range(1, place.n_line):
        peers.append(place.device(place.a, place.c, flip(place.z, k)))
    for peer in peers:
        pl.semaphore_signal(sem, inc=1, device_id=peer, device_id_type=MESH)
    pl.semaphore_wait(sem, len(peers))


class Gather:
    def __init__(self, pieces, ins, outs, sems, n_square, n_line):
        self.pieces, self.ins, self.outs = pieces, ins, outs
        self.local_sem, self.net_send, self.net_recv, self.core_send, self.core_recv, self.line_send = sems
        self.n_square, self.n_line = n_square, n_line
        self.p = Place(n_square, n_line)
        self.own = [
            pltpu.make_async_copy(
                ins[i], outs[i].at[self.p.slab(self.p.a, self.p.c, self.p.z)], self.local_sem.at[i]
            )
            for i in range(len(ins))
        ]
        self.trees = [Tree(order, n_line) for i, start, width, order in pieces]
        events = [(tree.time[slab], q, slab, False) for q, tree in enumerate(self.trees) for slab in tree.slabs]
        for q, tree in enumerate(self.trees):
            if pieces[q][3][0] != LINE:
                events += [(LATE_LINE + 0.1 * j, q, slab, True) for j, slab in enumerate(tree.slabs) if slab[1] == 0]
        self.todo = sorted(events, key=lambda e: e[0])
        self.started = []
        self.places = [self.p.slot(k) for k in range(n_line)]

    def at(self, q, m, k, c=None):
        i, start, width, order = self.pieces[q]
        p = self.p
        z = self.places[k] if order[0] == LINE else flip(p.z, k)
        s = p.slab(flip(p.a, m), p.c if c is None else c, z)
        return self.outs[i].at[s, :, pl.ds(start, width)]

    def source(self, q, m, k):
        if m == 0 and k == 0:
            i, start, width, _ = self.pieces[q]
            return self.ins[i].at[:, pl.ds(start, width)]
        return self.at(q, m, k)

    def go(self, q, m, k, sems, index, peer):
        copy = pltpu.make_async_remote_copy(
            src_ref=self.source(q, m, k),
            dst_ref=self.at(q, m, k),
            send_sem=sems[0].at[index],
            recv_sem=sems[1].at[index],
            device_id=peer,
            device_id_type=MESH,
        )
        copy.start()
        self.started.append((None, copy))

    def along(self, q, k):
        p = self.p
        z = self.places[k]
        for way, (step, more) in enumerate(((1, (z <= p.z) & (p.z < self.n_line - 1)), (-1, (z >= p.z) & (p.z > 0)))):
            copy = pltpu.make_async_remote_copy(
                src_ref=self.source(q, 0, k),
                dst_ref=self.at(q, 0, k),
                send_sem=self.line_send.at[q, way, k],
                recv_sem=self.net_recv.at[q, 0, z],
                device_id=p.device(p.a, p.c, p.z + step),
                device_id_type=MESH,
            )
            pl.when(more)(copy.start)
            self.started.append((more, copy))

    def arrived(self, q, m, k, sems, c, place=None):
        p = self.p
        pltpu.make_async_remote_copy(
            src_ref=self.at(q, m, k, c),
            dst_ref=self.at(q, m, k, c),
            send_sem=sems[0].at[q, m, k],
            recv_sem=sems[1].at[q, m, k if place is None else place],
            device_id=p.device(p.a, 1 - p.c, p.z),
            device_id_type=MESH,
        ).wait_recv()

    def load_own(self):
        for copy in self.own:
            copy.start()

    def start(self):
        for q, tree in enumerate(self.trees):
            if self.pieces[q][3][0] == LINE:
                self.along(q, 0)

    def pass_on(self, q, slab, child):
        p = self.p
        dim, step, _ = self.trees[q].up[child]
        peer = p.device(p.a, p.c, flip(p.z, step)) if dim == LINE else p.device(flip(p.a, step), p.c, p.z)
        self.go(q, *slab, (self.net_send, self.net_recv), (q, *child), peer)

    def until(self, time):
        self.run(sum(e[0] <= time for e in self.todo))

    def run(self, n):
        p = self.p
        net, core = (self.net_send, self.net_recv), (self.core_send, self.core_recv)
        for time, q, slab, line in self.todo[:n]:
            tree = self.trees[q]
            first = self.pieces[q][3][0] == LINE
            if line:
                for child in tree.down[slab]:
                    if tree.up[child][0] == LINE:
                        self.pass_on(q, slab, child)
                continue
            if slab != (0, 0):
                lined = first and slab[0] == 0
                self.arrived(q, *slab, net, p.c, self.places[slab[1]] if lined else None)
                if lined:
                    self.along(q, slab[1])
            for child in tree.down[slab]:
                if tree.up[child][0] != LINE:
                    self.pass_on(q, slab, child)
            self.go(q, *slab, core, (q, *slab), p.device(p.a, 1 - p.c, p.z))
        self.todo = self.todo[n:]

    def arrivals(self):
        self.run(len(self.todo))
        for copy in self.own:
            copy.wait()
        for k in range(self.n_line):
            for q in range(len(self.pieces)):
                for m in range(self.n_square):
                    self.arrived(q, m, k, (self.core_send, self.core_recv), 1 - self.p.c)

    def close(self):
        for more, copy in self.started:
            if more is None:
                copy.wait_send()
            else:
                pl.when(more)(copy.wait_send)


def gather_sems(n_pieces, n_arrays, n_square, n_line):
    sem = pltpu.SemaphoreType.DMA((n_pieces, n_square, n_line))
    line = pltpu.SemaphoreType.DMA((n_pieces, 2, n_line))
    return [pltpu.SemaphoreType.DMA((n_arrays,)), sem, sem, sem, sem, line]


def add_into(ref, other):
    ref[...] = ref[...] + other[...]


class Reduce:
    def __init__(self, pieces, mine, theirs, peer_part, landed, sems, n_square, n_line):
        self.pieces, self.mine, self.theirs = pieces, mine, theirs
        self.peer_part, self.landed = peer_part, landed
        self.net_send, self.net_recv, self.core_send, self.core_recv = sems
        self.n_square, self.n_line = n_square, n_line
        self.p = Place(n_square, n_line)
        self.ks = list(range(n_line))[::-1]
        self.trees = [Tree(order, n_line) for i, start, width, order in pieces]
        events = [
            (-tree.time[slab], q, slab)
            for q, tree in enumerate(self.trees)
            for slab in tree.slabs[::-1]
        ]
        self.todo = sorted((e for e in events if e[2] != (0, 0)), key=lambda e: e[0])
        self.sent, self.have = [], set()

    def core(self, q, k):
        p = self.p
        return pltpu.make_async_remote_copy(
            src_ref=self.theirs(q, k),
            dst_ref=self.peer_part[q].at[:, flip(p.z, k)],
            send_sem=self.core_send.at[q, k],
            recv_sem=self.core_recv.at[q, k],
            device_id=p.device(p.a, 1 - p.c, p.z),
            device_id_type=MESH,
        )

    def net(self, q, slab):
        p = self.p
        m, k = slab
        dim, step, _ = self.trees[q].up[slab]
        peer = p.device(p.a, p.c, flip(p.z, step)) if dim == LINE else p.device(flip(p.a, step), p.c, p.z)
        return pltpu.make_async_remote_copy(
            src_ref=self.mine(q, flip(p.a, m), flip(p.z, k)),
            dst_ref=self.landed[q].at[m, k],
            send_sem=self.net_send.at[q, m, k],
            recv_sem=self.net_recv.at[q, m, k],
            device_id=peer,
            device_id_type=MESH,
        )

    def start(self, pieces=None):
        for q in range(len(self.pieces)) if pieces is None else pieces:
            for k in self.ks[:1] if self.pieces[q][3][0] == LINE else self.ks:
                self.core(q, k).start()

    def from_core(self, q, k):
        if (q, k) not in self.have:
            self.have.add((q, k))
            self.core(q, k).wait_recv()
            if k and self.pieces[q][3][0] == LINE:
                self.core(q, k - 1).start()

    def until(self, time):
        self.run(sum(e[0] <= time for e in self.todo))

    def run(self, n, pieces=None):
        p = self.p
        now = [e for e in self.todo if pieces is None or e[1] in pieces][:n]
        self.todo = [e for e in self.todo if e not in now]
        for time, q, slab in now:
            m, k = slab
            self.from_core(q, k)
            a, z = flip(p.a, m), flip(p.z, k)
            add_into(self.mine(q, a, z), self.peer_part[q].at[a, z])
            for child in self.trees[q].down[slab]:
                self.net(q, child).wait_recv()
                add_into(self.mine(q, a, z), self.landed[q].at[child])
            copy = self.net(q, slab)
            copy.start()
            self.sent.append(copy)

    def finish(self, outs):
        self.run(len(self.todo))
        p = self.p
        for q in range(len(self.pieces)):
            i, start, width, _ = self.pieces[q]
            self.from_core(q, 0)
            total = self.mine(q, p.a, p.z)[...].astype(jnp.float32)
            total = total + self.peer_part[q][p.a, p.z].astype(jnp.float32)
            for child in self.trees[q].down[(0, 0)]:
                self.net(q, child).wait_recv()
                total = total + self.landed[q][child].astype(jnp.float32)
            outs[i][:, pl.ds(start, width)] = total
        for copy in self.sent:
            copy.wait_send()
        for k in self.ks:
            for q in range(len(self.pieces)):
                self.core(q, k).wait_send()


def reduce_boxes(pieces, shapes, dtypes, n_square, n_line):
    return [
        pltpu.VMEM((n_square, n_line, shapes[i][0], width), dtypes[i]) for i, start, width, _ in pieces
    ]


def reduce_sems(n_pieces, n_square, n_line):
    sem = pltpu.SemaphoreType.DMA((n_pieces, n_square, n_line))
    core_sem = pltpu.SemaphoreType.DMA((n_pieces, n_line))
    return [sem, sem, core_sem, core_sem]


class ReduceFromHbm(Reduce):
    def __init__(self, pieces, ins, mine, peer_part, landed, local_sem, sems, n_square, n_line):
        p = Place(n_square, n_line)

        def columns(q):
            i, start, width, _ = pieces[q]
            return ins[i], pl.ds(start, width)

        def theirs(q, k):
            ref, cols = columns(q)
            return ref.at[:, 1 - p.c, flip(p.z, k), :, cols]

        super().__init__(pieces, lambda q, a, z: mine[q].at[a, z], theirs, peer_part, landed, sems, n_square, n_line)
        self.loads = []
        for q in range(len(pieces)):
            ref, cols = columns(q)
            self.loads.append(pltpu.make_async_copy(ref.at[:, p.c, :, :, cols], mine[q], local_sem.at[q]))

    def load(self):
        for copy in self.loads:
            copy.start()

    def loaded(self):
        for copy in self.loads:
            copy.wait()


def reduce_body(pieces, n_arrays, n_square, n_line, *refs):
    n = len(pieces)
    ins, outs, rest = refs[:n_arrays], refs[n_arrays : 2 * n_arrays], refs[2 * n_arrays :]
    job = ReduceFromHbm(
        pieces, ins, rest[:n], rest[n : 2 * n], rest[2 * n : 3 * n], rest[3 * n], rest[3 * n + 1 :], n_square, n_line
    )
    job.load()
    barrier(job.p)
    job.start()
    job.loaded()
    job.finish(outs)


def reduce_scatter(arrays, plan, n_square, n_line, collective_id):
    shapes = [a.shape[1:] for a in arrays]
    pieces = split_pieces(plan, n_square)
    views = [a.reshape((n_square, 2, n_line) + s) for a, s in zip(arrays, shapes)]
    any_space = pl.BlockSpec(memory_space=pl.ANY)
    boxes = reduce_boxes(pieces, shapes, [x.dtype for x in arrays], n_square, n_line)
    return pl.pallas_call(
        functools.partial(reduce_body, pieces, len(arrays), n_square, n_line),
        out_shape=[jax.ShapeDtypeStruct(s, jnp.float32) for s in shapes],
        in_specs=[any_space] * len(arrays),
        out_specs=[pl.BlockSpec(memory_space=pltpu.VMEM)] * len(arrays),
        scratch_shapes=boxes * 3
        + [pltpu.SemaphoreType.DMA((len(pieces),))]
        + reduce_sems(len(pieces), n_square, n_line),
        compiler_params=pltpu.CompilerParams(
            collective_id=collective_id, has_side_effects=True, vmem_limit_bytes=60 << 20
        ),
        name="reduce_grads",
    )(*views)


f32, bf16 = jnp.float32, jnp.bfloat16
ROWS = 256
LEVELS = 8


def level_constants(rows):
    t, i = np.arange(rows)[:, None], np.arange(rows)[None, :]
    sums, masks = [], []
    for level in range((rows - 1).bit_length()):
        same = (t >> (level + 1)) == (i >> (level + 1))
        upper_t, upper_i = (t >> level) & 1, (i >> level) & 1
        sums.append(
            (same & (upper_t == 1) & (upper_i == 1) & (i <= t))
            | (same & (upper_t == 0) & (upper_i == 0) & (i > t))
        )
        masks.append((t > i) & (((t ^ i) >> level) == 1))
    sums += [i <= t, i > t]
    masks.append(t == i)
    return np.stack(sums).astype(bf16), np.stack(masks).astype(bf16)


def nn(a, b):
    return lax.dot_general(a, b, (((1,), (0,)), ((), ())), preferred_element_type=f32)


def nt(a, b):
    return lax.dot_general(a, b, (((1,), (1,)), ((), ())), preferred_element_type=f32)


def tn(a, b):
    return lax.dot_general(a, b, (((0,), (0,)), ((), ())), preferred_element_type=f32)


def split_low(x):
    high = x.astype(bf16)
    return high, (x - high.astype(f32)).astype(bf16)


def head_of_lane(shape):
    return lax.broadcasted_iota(jnp.int32, shape, 1) // SLOTS


def tall(x):
    head = head_of_lane(x.shape)
    zero = jnp.zeros_like(x)
    return jnp.concatenate([jnp.where(head == h, x, zero) for h in range(HEADS)], axis=0)


def wide(state):
    head = lax.broadcasted_iota(jnp.int32, state.shape, 0) // SLOTS
    zero = jnp.zeros_like(state)
    return jnp.concatenate([jnp.where(head == h, state, zero) for h in range(HEADS)], axis=1)


def of(x, h):
    return x[:, HEAD * h : HEAD * (h + 1)]


def slots(h):
    return slice(SLOTS * h, SLOTS * (h + 1))


def products(a, b):
    return jnp.concatenate([nt(of(a, h), of(b, h)) for h in range(HEADS)], axis=1).astype(bf16)


def masked(a, mask):
    return a * jnp.concatenate([mask] * HEADS, axis=1)


def share_of(log_gate):
    small = -log_gate * (1.0 + log_gate * (0.5 + log_gate * (1.0 / 6.0)))
    return jnp.where(log_gate > -0.01, small, 1.0 - jnp.exp(log_gate))


def head_sums(x):
    ones = (head_of_lane((256, 256)) == lax.broadcasted_iota(jnp.int32, (256, 256), 0) // SLOTS)
    ones = jnp.where(ones, 1.0, 0.0).astype(bf16)
    high, low = split_low(x)
    return nn(high, ones) + nn(low, ones)


SCALE = 1.5 * HEAD ** (-0.25)


def softmax_slots(scores):
    head = head_of_lane(scores.shape)
    peak = jnp.zeros_like(scores)
    for h in range(HEADS):
        top = jnp.max(jnp.where(head == h, scores, -jnp.inf), axis=1, keepdims=True)
        peak = jnp.where(head == h, top, peak)
    power = jnp.exp(scores - peak)
    return power / head_sums(power)


def decays(log_gate, sums_ref, decay_ref, tick):
    high, low = split_low(log_gate)
    for level in range(LEVELS + 2):
        m = sums_ref[level]
        decay_ref[level] = jnp.exp(nn(m, high) + nn(m, low))
        if level % 2:
            tick(1)
    ones = jnp.ones((ROWS, 256), bf16)
    return jnp.exp(tn(high, ones) + tn(low, ones))


def summaries(share_end, rows):
    return jnp.concatenate([tn(share_end, of(rows, h))[slots(h)] for h in range(HEADS)], axis=0)


def lower_scores(a_ref, share, decay_ref, masks_ref, total_ref, tick, parts_ref=None):
    total_ref[...] = nn(masked(a_ref[...], masks_ref[LEVELS]), tall(share.astype(bf16)))
    for level in range(LEVELS):
        decay = decay_ref[level]
        part = decay * nn(
            masked(a_ref[...], masks_ref[level]), tall((decay * share).astype(bf16))
        )
        if parts_ref is not None:
            parts_ref[level] = part.astype(bf16)
        total_ref[...] += part
        tick(1)


def mixing(coefficient, share, decay_ref, masks_ref, out_ref, tick):
    def pairs(x, f, mask):
        return masked(nt(x.astype(bf16), tall(f.astype(bf16))).astype(bf16), mask)

    out_ref[...] = pairs(coefficient, share, masks_ref[LEVELS])
    for level in range(LEVELS):
        decay = decay_ref[level]
        out_ref[...] += pairs(coefficient * decay, decay * share, masks_ref[level])
        tick(1)


class Chain:
    def __init__(self, n_line, backward, in_ref, out_ref, send_sem, recv_sem):
        self.z = lax.axis_index("shard")
        self.turn = n_line - 1 - self.z if backward else self.z
        self.next = self.z - 1 if backward else self.z + 1
        self.n_line, self.in_ref, self.out_ref = n_line, in_ref, out_ref
        self.send_sem, self.recv_sem = send_sem, recv_sem

    def copy(self, part):
        half = (part // 2, pl.ds(128 * (part % 2), 128))
        return pltpu.make_async_remote_copy(
            src_ref=self.out_ref.at[half],
            dst_ref=self.in_ref.at[half],
            send_sem=self.send_sem.at[part],
            recv_sem=self.recv_sem.at[part],
            device_id={"dp": lax.axis_index("dp"), "shard": self.next},
            device_id_type=MESH,
        )

    def step(self, i, through, sums_ref):
        if i >= self.n_line:
            return

        @pl.when(self.turn == i)
        def _():
            for part in range(4):
                which, rows = part // 2, slice(128 * (part % 2), 128 * (part % 2) + 128)
                if i == 0:
                    self.in_ref[which, rows] = jnp.zeros((128, HEAD), bf16)
                    new = sums_ref[which, rows]
                else:
                    self.copy(part).wait_recv()
                    new = through[rows] * self.in_ref[which, rows].astype(f32) + sums_ref[which, rows]
                if i < self.n_line - 1:
                    self.out_ref[which, rows] = new.astype(bf16)
                    self.copy(part).start()

    def finish(self):
        @pl.when(self.turn < self.n_line - 1)
        def _():
            for part in range(4):
                self.copy(part).wait_send()


def chain_scratch():
    box = pltpu.VMEM((2, 256, HEAD), bf16)
    sem = pltpu.SemaphoreType.DMA((4,))
    return [box, box, sem, sem, pltpu.VMEM((2, 256, HEAD), f32)]


def sigmoid(x):
    return 1.0 / (1.0 + jnp.exp(-x))


def spots(r):
    gate = lax.broadcasted_iota(jnp.int32, (256, D), 0)
    row = lax.broadcasted_iota(jnp.int32, (256, D), 1)
    per = r // 4
    return jnp.where((gate // per) * r + gate % per == row, 1.0, 0.0).astype(bf16)


def ones_where(shape, condition):
    i = lax.broadcasted_iota(jnp.int32, shape, 0)
    j = lax.broadcasted_iota(jnp.int32, shape, 1)
    return jnp.where(condition(i, j), 1.0, 0.0).astype(bf16)


def forward_kernel(mixer_pieces, pieces, n_mixer, n_ffn, n_square, n_line, *refs):
    tokens_ref, sums_ref, masks_ref = refs[:3]
    mixer_shards, shards, refs = refs[3 : 3 + n_mixer], refs[3 + n_mixer : 3 + n_mixer + n_ffn], refs[3 + n_mixer + n_ffn :]
    (
        q_ref, k_ref, v_ref, swish_ref, mixed_ref, state_ref, scores_ref, gated_ref, hidden_ref, normed2_ref,
        normed_ref, gate_ref, rank_ref, gains_ref, hgain_ref, up_pad_ref, low_pad_ref,
    ) = refs[:17]
    refs = refs[17:]
    w_refs, gathered, refs = refs[:n_mixer], refs[n_mixer : n_mixer + n_ffn], refs[n_mixer + n_ffn :]
    w_in, small, decay_ref, a_ref, b_ref, in_ref, out_ref, chain_send, chain_recv, part_ref, w_sem = refs[:11]
    refs = refs[11:]
    first = Gather(mixer_pieces, mixer_shards, w_refs, refs[:6], n_square, n_line)
    job = Gather(pieces, shards, gathered, refs[6:], n_square, n_line)
    chain = Chain(n_line, False, in_ref, out_ref, chain_send, chain_recv)
    first.load_own()
    job.load_own()
    barrier(job.p)
    first.start()
    first.until(3)
    job.start()
    first.until(3.9)
    job.until(0)
    first.arrivals()
    n = n_square * 2 * n_line
    loads = {}
    loads[5] = pltpu.make_async_copy(w_refs[5], small, w_sem.at[5])
    loads[5].start()
    for i in (1, 2, 0, 3, 4):
        loads[i] = pltpu.make_async_copy(w_refs[i], w_in.at[i], w_sem.at[i])
        loads[i].start()
    tick = job.run
    few = job.run
    tick(10)
    x = tokens_ref[...].astype(f32)
    scale1 = lax.rsqrt(jnp.mean(x * x, axis=-1, keepdims=True) + norm_eps)
    loads[5].wait()
    packed = small[...].reshape(D, 128)
    rows = nt(ones_where((128, 128), lambda i, j: i == j), packed)
    gains_ref[...] = jnp.concatenate([rows[34:36], jnp.zeros((6, D), f32)], axis=0)
    by_gate = nn(spots(D // n), packed).astype(bf16)
    pair = nt(ones_where((8, 128), lambda i, j: j == i + 32), by_gate)
    bias = pair[:1]
    hgain = pair[1:2]
    hgain_ref[...] = jnp.broadcast_to(hgain, (8, HEAD))
    lane = lax.broadcasted_iota(jnp.int32, (D, 128), 1)
    low_pad = jnp.where(lane < 16, packed.astype(f32), 0.0).astype(bf16)
    low_pad_ref[...] = low_pad
    up_pad = nn(by_gate, ones_where((128, 128), lambda i, j: (i == j + 16) & (j < 16))).astype(bf16)
    up_pad_ref[...] = up_pad
    normed = (x * scale1 * rows[34:35]).astype(bf16)
    normed_ref[...] = normed
    low_rank = nn(normed, low_pad).astype(bf16)
    logits = nt(low_rank, up_pad) + bias
    log_gate = (jnp.minimum(logits, 0.0) - jnp.log1p(jnp.exp(-jnp.abs(logits)))) * (1.0 / gate_norm)
    gate_ref[...] = log_gate
    moved = nn(low_rank, ones_where((128, 128), lambda i, j: (j == i + 16) & (i < 16)))
    lane = lax.broadcasted_iota(jnp.int32, (ROWS, 128), 1)
    rank_ref[...] = jnp.where(lane == 32, 1.0, moved).astype(bf16)
    tick(2)

    def project(i):
        loads[i].wait()
        return nn(normed, w_in[i].reshape(D, D))

    share = share_of(log_gate)
    through = decays(log_gate, sums_ref, decay_ref, tick)
    share_end = (decay_ref[LEVELS + 1] * share).astype(bf16)
    k_ref[...] = project(1).astype(bf16)
    tick(2)
    v_ref[...] = project(2).astype(bf16)
    tick(2)
    part_ref[0] = summaries(share_end, k_ref[...])
    part_ref[1] = summaries(share_end, v_ref[...])
    chain.step(0, through, part_ref)
    tick(2)
    q_ref[...] = project(0).astype(bf16)
    tick(2)
    a_ref[...] = products(q_ref[...], k_ref[...])
    chain.step(1, through, part_ref)
    tick(2)
    swish_ref[...] = project(3)
    tick(2)
    lower_scores(a_ref, share, decay_ref, masks_ref, scores_ref, few)
    for i in range(2, n_line):
        chain.step(i, through, part_ref)
        tick(4)
    before = decay_ref[LEVELS]
    scores = scores_ref[...] + before * nt(q_ref[...], wide(in_ref[0]))
    scores_ref[...] = scores
    chance = softmax_slots(SCALE * scores)
    mixing(chance, share, decay_ref, masks_ref, b_ref, few)
    carried = nn((chance * before).astype(bf16), wide(in_ref[1]))
    state_ref[...] = in_ref[...]
    b, v = b_ref[...], v_ref[...]
    for h in range(HEADS):
        at = slice(HEAD * h, HEAD * (h + 1))
        mixed = nn(of(b, h), of(v, h)) + of(carried, h)
        mixed_ref[:, at] = mixed
        head_scale = lax.rsqrt(jnp.mean(mixed * mixed, axis=-1, keepdims=True) + norm_eps)
        swish = swish_ref[:, at]
        gated_ref[:, at] = (mixed * head_scale * hgain * (swish * sigmoid(swish))).astype(bf16)
        tick(2)
    loads[4].wait()
    hidden = tokens_ref[...].astype(f32) + nn(gated_ref[...], w_in[4].reshape(D, D))
    hidden_ref[...] = hidden
    scale2 = lax.rsqrt(jnp.mean(hidden * hidden, axis=-1, keepdims=True) + norm_eps)
    normed2_ref[...] = (hidden * scale2 * gains_ref[1:2]).astype(bf16)
    job.arrivals()
    first.close()
    job.close()
    chain.finish()


VMEM_BLOCK = pl.BlockSpec(memory_space=pltpu.VMEM)
ANY_BLOCK = pl.BlockSpec(memory_space=pl.ANY)


def run_forward(tokens, sums, masks, mixer_shards, shards, n_square, n_line, collective_id):
    rows = tokens.shape[0]
    n = n_square * 2 * n_line
    every = [*mixer_shards, *shards]
    mixer_pieces = split_pieces(MIXER_PLAN + [(5, 0, 128, "a")], n_square)
    pieces = split_pieces(FFN_PLAN, n_square)
    shape = lambda dtype, *dims: jax.ShapeDtypeStruct(dims, dtype)
    full = lambda dtype: shape(dtype, rows, D)
    pair = pltpu.VMEM((ROWS, HEADS * ROWS), bf16)
    return pl.pallas_call(
        functools.partial(forward_kernel, mixer_pieces, pieces, len(mixer_shards), len(shards), n_square, n_line),
        out_shape=[full(bf16)] * 3
        + [full(f32)] * 2
        + [shape(bf16, 2, 256, HEAD), shape(f32, rows, 256)]
        + [full(bf16), full(f32), full(bf16), full(bf16)]
        + [shape(f32, rows, 256), shape(bf16, rows, 128), shape(f32, 8, D), shape(f32, 8, HEAD)]
        + [shape(bf16, 256, 128), shape(bf16, D, 128)]
        + [shape(bf16, n, *s.shape) for s in every],
        in_specs=[VMEM_BLOCK] * 3 + [ANY_BLOCK] * len(every),
        out_specs=[VMEM_BLOCK] * 17 + [ANY_BLOCK] * len(every),
        scratch_shapes=[
            pltpu.VMEM((5, n, D // n, D), bf16),
            pltpu.VMEM((n, D // n, 128), bf16),
            pltpu.VMEM((LEVELS + 2, ROWS, 256), f32),
            pair,
            pair,
        ]
        + chain_scratch()
        + [pltpu.SemaphoreType.DMA((6,))]
        + gather_sems(len(mixer_pieces), len(mixer_shards), n_square, n_line)
        + gather_sems(len(pieces), len(shards), n_square, n_line),
        compiler_params=pltpu.CompilerParams(
            collective_id=collective_id, has_side_effects=True, vmem_limit_bytes=60 << 20
        ),
        name="mixer_forward",
    )(tokens, sums, masks, *every)


def backward_kernel(pieces, n_ffn, n_square, n_line, *refs):
    (
        gh_ref, swish_ref, mixed_ref, hgain_ref, q_ref, k_ref, v_ref, gate_ref, sums_ref, masks_ref, back_masks_ref,
        state_ref, scores_ref, normed_ref, gated_ref, tokens_ref, gain1_ref, dgain2_ref, up_pad_ref, low_pad_ref, rank_ref,
    ) = refs[:21]
    w_refs, refs = refs[21:26], refs[26:]
    partial, refs = refs[:n_ffn], refs[n_ffn:]
    dw_refs, small_ref, dtok_ref, refs = refs[:5], refs[5], refs[6], refs[7:]
    reduced, refs = refs[:n_ffn], refs[n_ffn:]
    (
        gqkvs_ref, dgate_ref, w_buf, stage, decay_ref, a_ref, av_ref, at_ref, avt_ref, s_parts, d_parts,
        s_sum, d_sum, shares_ref, g_ref, in_ref, out_ref, chain_send, chain_recv, part_ref, w_sem, stage_sem,
    ) = refs[:22]
    refs = refs[22:]
    b_ref, bk_ref = a_ref, av_ref
    m = len(pieces)
    job = ReduceFromHbm(
        pieces, partial, refs[:m], refs[m : 2 * m], refs[2 * m : 3 * m], refs[3 * m], refs[3 * m + 1 :], n_square, n_line
    )
    chain = Chain(n_line, True, in_ref, out_ref, chain_send, chain_recv)

    def w_load(i):
        slot = {4: 0, 3: 1, 0: 0, 1: 1, 2: 0}[i]
        return pltpu.make_async_copy(w_refs[i], w_buf.at[slot], w_sem.at[slot]), w_buf.at[slot]

    def w_store(i):
        slot = {4: 0, 3: 1, 0: 0, 1: 1, 2: 0}[i]
        return pltpu.make_async_copy(stage.at[slot], dw_refs[i], stage_sem.at[slot])

    def weight(i, left, right, wait=None):
        slot = {4: 0, 3: 1, 0: 0, 1: 1, 2: 0}[i]
        if wait is not None:
            w_store(wait).wait()
        stage[slot] = tn(left, right).astype(bf16)
        w_store(i).start()

    w_load(4)[0].start()
    w_load(3)[0].start()
    job.load()
    barrier(job.p)
    job.start()
    job.loaded()
    tick = job.run
    few = job.run
    none = lambda n: None

    log_gate = gate_ref[...]
    share = share_of(log_gate)
    through = decays(log_gate, sums_ref, decay_ref, none)
    branch = gh_ref[...].astype(bf16)
    load, w = w_load(4)
    load.wait()
    tick(8)
    grad_gated = nt(branch, w[...]).astype(bf16)
    w_load(0)[0].start()
    gain = hgain_ref[:1]
    dhgain = jnp.zeros((1, HEAD), f32)
    for h in range(HEADS):
        at = slice(HEAD * h, HEAD * (h + 1))
        mixed, swish = mixed_ref[:, at], swish_ref[:, at]
        gg = of(grad_gated, h).astype(f32)
        sig = sigmoid(swish)
        head_scale = lax.rsqrt(jnp.mean(mixed * mixed, axis=-1, keepdims=True) + norm_eps)
        scaled = mixed * head_scale
        g_head = gg * (swish * sig)
        dhgain += jnp.sum(g_head * scaled, axis=0, keepdims=True)
        gqkvs_ref[1, :, at] = (
            gg * (scaled * gain) * (sig * (1.0 + swish * (1.0 - sig)))
        ).astype(bf16)
        u = g_head * gain
        g_ref[:, at] = (
            head_scale * (u - scaled * (head_scale * jnp.mean(u * mixed, axis=-1, keepdims=True)))
        ).astype(bf16)
        tick(3)
    q, k, v, g = q_ref[...], k_ref[...], v_ref[...], g_ref[...]
    before, after = decay_ref[LEVELS], decay_ref[LEVELS + 1]
    key_in, value_in = state_ref[0], state_ref[1]
    chance = softmax_slots(SCALE * scores_ref[...])
    av_ref[...] = products(g, v)
    lower_scores(av_ref, share, decay_ref, masks_ref, d_sum, none, d_parts)
    d_state = before * nt(g, wide(value_in))
    slope = d_sum[...] + d_state
    spread = SCALE * chance * (slope - head_sums(chance * slope))
    chance_before = (chance * before).astype(bf16)
    spread_before = (spread * before).astype(bf16)
    part_ref[0] = summaries(spread_before, q)
    part_ref[1] = summaries(chance_before, g)
    chain.step(0, through, part_ref)
    tick(4)
    weight(4, gated_ref[...], branch)
    load, w = w_load(3)
    load.wait()
    grad_swish = gqkvs_ref[1]
    dtok_ref[...] = nt(grad_swish, w[...])
    w_load(1)[0].start()
    tick(1)
    weight(3, normed_ref[...], grad_swish)
    tick(1)
    chain.step(1, through, part_ref)
    a_ref[...] = products(q, k)
    tick(1)
    at_ref[...] = products(k, q)
    tick(1)
    avt_ref[...] = products(v, g)
    tick(8)
    lower_scores(a_ref, share, decay_ref, masks_ref, s_sum, none, s_parts)
    s_state = before * nt(q, wide(key_in))
    mixing(chance, share, decay_ref, masks_ref, b_ref, none)
    tick(8)
    mixing(spread, share, decay_ref, masks_ref, bk_ref, none)
    dgate_ref[...] = tn(sums_ref[LEVELS], (spread * s_state + chance * d_state).astype(bf16))
    diagonal = back_masks_ref[LEVELS]
    shares_ref[...] = nn(masked(at_ref[...], diagonal), tall(spread.astype(bf16))) + nn(
        masked(avt_ref[...], diagonal), tall(chance.astype(bf16))
    )

    for level in range(LEVELS):
        decay = decay_ref[level]
        mask = back_masks_ref[level]
        taken = decay * (
            nn(masked(at_ref[...], mask), tall((spread * decay).astype(bf16)))
            + nn(masked(avt_ref[...], mask), tall((chance * decay).astype(bf16)))
        )
        shares_ref[...] += taken
        given = spread * s_parts[level].astype(f32) + chance * d_parts[level].astype(f32)
        place = lax.broadcasted_iota(jnp.int32, (ROWS, 256), 0)
        upper = lax.bitwise_and(lax.shift_right_logical(place, level), 1) == 1
        both = jnp.where(upper, given, taken * share).astype(bf16)
        dgate_ref[...] += tn(sums_ref[level], both)
        if level >= 3:
            tick(2)
    q_state = nn(spread_before, wide(key_in))
    b, bk = b_ref[...], bk_ref[...]
    normed = normed_ref[...]

    def finish_rows(i, new_of):
        for h in range(HEADS):
            gqkvs_ref[0, :, HEAD * h : HEAD * (h + 1)] = new_of(h).astype(bf16)
        tick(1)
        grad = gqkvs_ref[0]
        weight(i, normed, grad, (4, 3, 0)[i])
        tick(1)
        load, w = w_load(i)
        load.wait()
        dtok_ref[...] += nt(grad, w[...])
        if i == 0:
            w_load(2)[0].start()
        tick(1)

    finish_rows(0, lambda h: nn(of(bk, h), of(k, h)) + of(q_state, h))
    job.until(-3)
    chain.step(2, through, part_ref)
    job.until(-2)
    for i in range(3, n_line):
        chain.step(i, through, part_ref)
    out_key, out_value = in_ref[0], in_ref[1]
    wide_key, wide_value = wide(out_key), wide(out_value)
    taken = after * (nt(k, wide_key) + nt(v, wide_value))
    shares = shares_ref[...] + taken
    kept = key_in.astype(f32) * out_key.astype(f32) + value_in.astype(f32) * out_value.astype(f32)
    high, low = split_low(kept * through)
    ones = jnp.ones((8, 256), bf16)
    kept_row = (nt(ones, high) + nt(ones, low))[:1]
    dgate = dgate_ref[...] + tn(sums_ref[LEVELS + 1], (taken * share).astype(bf16)) + kept_row
    dgate = dgate - jnp.exp(log_gate) * shares
    grad_logits = dgate * (1.0 / gate_norm) * share_of(gate_norm * log_gate)
    tick(2)
    end = (after * share).astype(bf16)
    k_state = nn(end, wide_key)
    v_state = nn(end, wide_value)
    finish_rows(1, lambda h: tn(of(bk, h), of(q, h)) + of(k_state, h))
    finish_rows(2, lambda h: tn(of(b, h), of(g, h)) + of(v_state, h))
    high, low = split_low(grad_logits)
    up_pad, rank = up_pad_ref[...], rank_ref[...]
    grad_low = (nn(high, up_pad) + nn(low, up_pad)).astype(bf16)
    g_normed = dtok_ref[...] + nt(grad_low, low_pad_ref[...])
    x = tokens_ref[...].astype(f32)
    scale1 = lax.rsqrt(jnp.mean(x * x, axis=-1, keepdims=True) + norm_eps)
    u = g_normed * gain1_ref[:1]
    dtok_ref[...] = (
        gh_ref[...] + scale1 * u - x * (scale1 * scale1 * scale1 * jnp.mean(u * x, axis=-1, keepdims=True))
    )
    tick(1)

    def at_lane(rows, which):
        lane = lax.broadcasted_iota(jnp.int32, (rows, 128), 1)
        return jnp.where(lane == which, 1.0, 0.0).astype(bf16)

    def column(row, which):
        row_high, row_low = split_low(row)
        place = lax.broadcasted_iota(jnp.int32, (8, row.shape[1]), 0)
        pair = jnp.where(place == 0, row_high.astype(f32), jnp.where(place == 1, row_low.astype(f32), 0.0)).astype(bf16)
        return tn(pair, at_lane(8, which))

    few = tn(high, rank) + tn(low, rank) + column(dhgain, 33)
    r = D // (n_square * 2 * n_line)
    gates = lax.broadcasted_iota(jnp.int32, (256, D), 0)
    rows = lax.broadcasted_iota(jnp.int32, (256, D), 1)
    per = r // 4
    spot = jnp.where((gates // per) * r + gates % per == rows, 1.0, 0.0).astype(bf16)
    few_high, few_low = split_low(few)
    total = tn(spot, few_high) + tn(spot, few_low)
    total = total + tn(normed, grad_low)
    scaled_high, scaled_low = split_low(g_normed * x * scale1)
    gain1_lane = at_lane(ROWS, 34)
    total = total + tn(scaled_high, gain1_lane) + tn(scaled_low, gain1_lane)
    small_ref[...] = total + column(dgain2_ref[:1], 35)
    tick(2)
    job.finish(reduced)
    chain.finish()
    w_store(1).wait()
    w_store(2).wait()


def run_backward(operands, weights, partial, n_square, n_line, collective_id):
    rows = operands[0].shape[0]
    shapes = [a.shape[1:] for a in partial]
    pieces = split_pieces(FFN_REDUCE_PLAN, n_square)
    views = [a.reshape((n_square, 2, n_line) + s) for a, s in zip(partial, shapes)]
    boxes = reduce_boxes(pieces, shapes, [a.dtype for a in partial], n_square, n_line)
    pair = pltpu.VMEM((ROWS, HEADS * ROWS), bf16)
    parts = pltpu.VMEM((LEVELS, ROWS, 256), bf16)
    flat = pltpu.VMEM((ROWS, 256), f32)
    two = pltpu.VMEM((2, D, D), bf16)
    return pl.pallas_call(
        functools.partial(backward_kernel, pieces, len(partial), n_square, n_line),
        out_shape=[jax.ShapeDtypeStruct((D, D), bf16)] * 5
        + [jax.ShapeDtypeStruct((D, 128), f32), jax.ShapeDtypeStruct((rows, D), f32)]
        + [jax.ShapeDtypeStruct(s, f32) for s in shapes],
        in_specs=[VMEM_BLOCK] * 21 + [ANY_BLOCK] * (5 + len(partial)),
        out_specs=[ANY_BLOCK] * 5 + [VMEM_BLOCK] * (2 + len(partial)),
        scratch_shapes=[pltpu.VMEM((2, rows, D), bf16), flat, two, two, pltpu.VMEM((LEVELS + 2, ROWS, 256), f32)]
        + [pair] * 4
        + [parts, parts, flat, flat, flat, pltpu.VMEM((ROWS, D), bf16)]
        + chain_scratch()
        + [pltpu.SemaphoreType.DMA((2,)), pltpu.SemaphoreType.DMA((2,))]
        + boxes * 3
        + [pltpu.SemaphoreType.DMA((len(pieces),))]
        + reduce_sems(len(pieces), n_square, n_line),
        compiler_params=pltpu.CompilerParams(
            collective_id=collective_id, has_side_effects=True, vmem_limit_bytes=63 << 20
        ),
        name="mixer_backward",
    )(*operands, *weights, *views)


FF_TILE = 256


def ffn_kernel(
    normed2_ref, hidden_ref, cot_ref, valid_ref, gain2_ref, wg_ref, wu_ref, wd_ref,
    output_ref, gh_ref, dgain2_ref, dg_ref, du_ref, dd_ref,
    low_ref, out_acc, back_acc,
):
    step = pl.program_id(0)

    @pl.when(step == 0)
    def _():
        low_ref[...] = (cot_ref[...].astype(f32) * valid_ref[...]).astype(bf16)
        out_acc[...] = jnp.zeros_like(out_acc)
        back_acc[...] = jnp.zeros_like(back_acc)

    x, low = normed2_ref[...], low_ref[...]
    wg, wu, wd = wg_ref[...], wu_ref[...], wd_ref[...]
    gate, up = nn(x, wg), nn(x, wu)
    inside = nt(low, wd).astype(bf16).astype(f32)
    sig = sigmoid(gate)
    act = gate * sig
    inner = (act * up).astype(bf16)
    g_gate = (inside * up * (sig * (1.0 + gate * (1.0 - sig)))).astype(bf16)
    g_up = (inside * act).astype(bf16)
    out_acc[...] += nn(inner, wd)
    dd_ref[...] = tn(inner, low).astype(bf16)
    dg_ref[...] = tn(x, g_gate).astype(bf16)
    du_ref[...] = tn(x, g_up).astype(bf16)
    back_acc[...] += nt(g_gate, wg) + nt(g_up, wu)

    @pl.when(step == pl.num_programs(0) - 1)
    def _():
        hidden, valid = hidden_ref[...], valid_ref[...]
        output_ref[...] = (valid * (hidden + out_acc[...])).astype(bf16)
        scale2 = lax.rsqrt(jnp.mean(hidden * hidden, axis=-1, keepdims=True) + norm_eps)
        back = back_acc[...]
        scaled = hidden * scale2
        dgain2_ref[...] = jnp.broadcast_to(jnp.sum(back * scaled, axis=0, keepdims=True), dgain2_ref.shape)
        u = back * gain2_ref[1:2]
        gh_ref[...] = cot_ref[...].astype(f32) * valid + scale2 * (
            u - scaled * (scale2 * jnp.mean(u * hidden, axis=-1, keepdims=True))
        )


def run_ffn(normed2, hidden, cotangent, valid, gain2, w_gate, w_up, w_down):
    rows = normed2.shape[0]
    ff = w_down.shape[0]
    tile = FF_TILE
    fixed = lambda *shape: pl.BlockSpec(shape, lambda j: (0, 0))
    cols = pl.BlockSpec((D, tile), lambda j: (0, j))
    down = pl.BlockSpec((tile, D), lambda j: (j, 0))
    return pl.pallas_call(
        ffn_kernel,
        grid=(ff // tile,),
        out_shape=[
            jax.ShapeDtypeStruct((rows, D), bf16),
            jax.ShapeDtypeStruct((rows, D), f32),
            jax.ShapeDtypeStruct((8, D), f32),
            jax.ShapeDtypeStruct((D, ff), bf16),
            jax.ShapeDtypeStruct((D, ff), bf16),
            jax.ShapeDtypeStruct((ff, D), bf16),
        ],
        in_specs=[fixed(rows, D)] * 3 + [fixed(rows, 1), fixed(8, D), cols, cols, down],
        out_specs=[fixed(rows, D), fixed(rows, D), fixed(8, D), cols, cols, down],
        scratch_shapes=[pltpu.VMEM((rows, D), bf16), pltpu.VMEM((rows, D), f32), pltpu.VMEM((rows, D), f32)],
        compiler_params=pltpu.CompilerParams(vmem_limit_bytes=40 << 20),
        name="ffn",
    )(normed2, hidden, cotangent, valid, gain2, w_gate, w_up, w_down)


def pack_small(low, up, bias, hgain, gain1, gain2, dtype):
    n, rows = low.shape[0], low.shape[1]
    fill = lambda a: jnp.pad(a.astype(dtype), ((0, 0), (0, rows - a.shape[1]), (0, 0)))
    parts = [fill(low), fill(up)] + [fill(a[:, :, None]) for a in (bias, hgain, gain1, gain2)]
    out = jnp.concatenate(parts, axis=2)
    return jnp.pad(out, ((0, 0), (0, 0), (0, 128 - out.shape[2])))


def unpack_small(packed):
    n, rows = packed.shape[0], packed.shape[1]
    few = rows // 4
    low = packed[:, :, :16].reshape(n * rows, 16)
    up = packed[:, :few, 16:32].reshape(n * few, 16)
    bias, hgain = (packed[:, :few, lane].reshape(n * few) for lane in (32, 33))
    gain1, gain2 = (packed[:, :, lane].reshape(n * rows) for lane in (34, 35))
    return low, up, bias, hgain, gain1, gain2


def per_device(
    n_square, n_line,
    tokens, cotangent, lengths, norm1_gain, w_query, w_key, w_value, w_gate_low, w_gate_up,
    gate_bias, head_gain, w_swish, w_out, norm2_gain, w_ffn_gate, w_ffn_up, w_ffn_down,
):
    count = tokens.shape[0]
    n = n_square * 2 * n_line
    small = pack_small(
        *(a[None] for a in (w_gate_low, w_gate_up, gate_bias, head_gain, norm1_gain, norm2_gain)), bf16
    )[0]
    sums, masks = level_constants(count)
    back_masks = np.ascontiguousarray(np.swapaxes(masks, 1, 2))
    position = lax.axis_index("shard") * count + jnp.arange(count, dtype=jnp.int32)
    valid = (position < lengths[0]).astype(f32)[:, None]
    (
        q, k, v, swish_pre, mixed, state, scores, gated, hidden, normed2, normed, log_gate, rank, gains, hgain, up_pad,
        low_pad, *got,
    ) = run_forward(
        tokens, sums, masks, [w_query, w_key, w_value, w_swish, w_out, small], [w_ffn_gate, w_ffn_up, w_ffn_down],
        n_square, n_line, 2,
    )
    weights = [g.reshape(D, D) for g in got[:5]]
    ffn_all = got[6:]
    w_g, w_u = (g.reshape(D, -1) for g in ffn_all[:2])
    w_d = ffn_all[2].reshape(-1, D)
    ff = w_d.shape[0]
    output, grad_hidden, d_gain2, d_gate, d_up_proj, d_down = run_ffn(
        normed2, hidden, cotangent, valid, gains, w_g, w_u, w_d
    )
    operands = [
        grad_hidden, swish_pre, mixed, hgain, q, k, v, log_gate, sums, masks, back_masks, state, scores,
        normed, gated, tokens, gains, d_gain2, up_pad, low_pad, rank,
    ]
    *dw, d_small, d_tokens, s_gate, s_up, s_down = run_backward(
        operands, weights,
        [d_gate.reshape(n, D // n, ff), d_up_proj.reshape(n, D // n, ff), d_down.reshape(n, ff // n, D)],
        n_square, n_line, 3,
    )
    s_q, s_k, s_v, s_swish, s_out, s_small = reduce_scatter(
        [a.reshape(n, D // n, -1) for a in (*dw, d_small)], MIXER_REDUCE_PLAN + [(5, 0, 128, "a")], n_square, n_line, 4
    )
    o_low, o_up, o_bias, o_hgain, o_gain1, o_gain2 = unpack_small(s_small[None])
    return (
        output, d_tokens, o_gain1,
        s_q, s_k, s_v,
        o_low, o_up, o_bias, o_hgain,
        s_swish, s_out, o_gain2,
        s_gate, s_up, s_down,
    )


def solution(mesh):
    rows, row = P(("dp", "shard"), None), P(("dp", "shard"))
    placed = (rows, rows, P("dp"), row, rows, rows, rows, rows, rows, row, row, rows, rows, row, rows, rows, rows)
    out = (rows, rows, row, rows, rows, rows, rows, rows, row, row, rows, rows, row, rows, rows, rows)
    return jax.shard_map(
        functools.partial(per_device, mesh.shape["dp"] // 2, mesh.shape["shard"]),
        mesh=mesh,
        in_specs=placed,
        out_specs=out,
        check_vma=False,
    )
```
